32 devices in a mesh: dp: 16 (over z, y, core), mp: 2 (over x).
Axes of the slice: x: 2, y: 2, z: 4, core: 2. Of those that a mesh axis runs over, the one named last changes fastest.
Arguments:
- tokens: bfloat16 [24576, 768], P('dp'), may hold values from -6 to 6
- out_grad: bfloat16 [24576, 768], P('dp'), may hold values from -6 to 6
- doc_lengths: int32 [16, 4], P('dp'), may hold values from 1 to 1024, 1536 in all within a row
- w_query: float32 [768, 768], P('dp', 'mp'), may hold values from -0.21875 to 0.21875
- w_key: float32 [768, 768], P('dp', 'mp'), may hold values from -0.21875 to 0.21875
- w_value: float32 [768, 768], P('dp', 'mp'), may hold values from -0.21875 to 0.21875
- w_out: float32 [768, 768], P('mp', 'dp'), may hold values from -0.875 to 0.875
- gain_one: float32 [768], P('dp'), may hold values from 0.5 to 1.5
- w_gate: float32 [768, 2560], P('dp', 'mp'), may hold values from -0.21875 to 0.21875
- w_up: float32 [768, 2560], P('dp', 'mp'), may hold values from -0.21875 to 0.21875
- w_down: float32 [2560, 768], P('mp', 'dp'), may hold values from -0.125 to 0.125
- gain_two: float32 [768], P('dp'), may hold values from 0.5 to 1.5
Outputs:
- output: bfloat16 [24576, 768], P('dp')
- grad_tokens: float32 [24576, 768], P('dp')
- grad_w_query: float32 [768, 768], P('dp', 'mp')
- grad_w_key: float32 [768, 768], P('dp', 'mp')
- grad_w_value: float32 [768, 768], P('dp', 'mp')
- grad_w_out: float32 [768, 768], P('mp', 'dp')
- grad_gain_one: float32 [768], P('dp')
- grad_w_gate: float32 [768, 2560], P('dp', 'mp')
- grad_w_up: float32 [768, 2560], P('dp', 'mp')
- grad_w_down: float32 [2560, 768], P('mp', 'dp')
- grad_gain_two: float32 [768], P('dp')
The draws below stay inside these ranges and needn't reach their ends.
Inputs may be any that keep to these rules, and one draw needn't show every extreme that they name: `doc_lengths`: each row lists the lengths of the 4 documents packed into one pack of 1536 tokens, in order; they sum to 1536 and the largest is exactly 1024.
All inputs are finite; a program needn't handle non-finite values.
Results may differ from the reference program's by a relative error of at most 0.019.
The reference program's roundings to bfloat16 on the way count: a program that leaves them out, or rounds other values in their place, can miss the bound.
Values may be sent and summed in bfloat16 or wider, within the bound.
A program may use at most 256 MiB of HBM per device.

```python
import math
import jax
import jax.numpy as jnp
import numpy as np
from jax import lax

D = 768
HEADS = 16
HD = 48
FF = 2560
TOK_DEV = 1536
MAXLEN = 1024
BLOCK = 512
DOCS = 4
PACKS = 16
TOKENS = 24576
N_MP = 2


def spiked(values, key, source, target, blocks, factor):
    owner, partner = [(jnp.arange(values.shape[dim]) // (values.shape[dim] // blocks)).reshape([-1 if axis == dim else 1 for axis in range(values.ndim)]) for dim in (source, target)]
    chosen = jax.random.permutation(key, blocks)[partner]
    strong = (owner == chosen) | (owner == (partner + blocks // 2) % blocks)
    return jnp.where(strong, factor * values, values)


def block_levels(stream_key, dims, cuts, smallest, top_value):
    def one(dim, blocks):
        heights = jax.random.uniform(jax.random.fold_in(jax.random.fold_in(stream_key, 6), dim), (blocks,), jnp.float32, smallest / len(cuts), top_value / len(cuts))
        return jnp.repeat(jnp.exp(heights), dims[dim] // blocks).reshape((-1,) + (1,) * (len(dims) - dim - 1))

    level = one(*cuts[0])
    for cut in cuts[1:]:
        level = level * one(*cut)
    return level


def split_up(amount, total, limit, skew):
    weights = [(1 << 20) // math.isqrt(standing ** skew) + 1 for standing in range(2, amount + 1)]
    rest, given = total - limit - (amount - 1), [1] * (amount - 1)
    while rest > 0:
        candidates = [i for i in range(amount - 1) if given[i] < limit]
        pool, left = sum([weights[i] for i in candidates]), rest
        for i in candidates:
            more = min(limit - given[i], max(1, left * weights[i] // pool), rest)
            given[i] = given[i] + more
            rest = rest - more
    return np.array([limit] + given)


def ragged_sizes(key, number_of, total, reach, slope):
    if number_of == 2:
        one = jax.random.randint(key, (), max(1, total - reach), min(reach, total - 1) + 1)
        return jnp.stack([one, total - one])
    sizes = jnp.asarray(split_up(number_of, total, reach, slope), jnp.int32)
    couples = (number_of - 1) // 2
    donor, receiver = sizes[1:1 + 2 * couples:2], sizes[2:2 + 2 * couples:2]
    room = jnp.minimum(donor - 1, reach - receiver)
    moved = jax.random.randint(jax.random.fold_in(key, 1), (couples,), 0, 1 << 20) % (room + 1)
    sizes = sizes.at[1:1 + 2 * couples:2].set(donor - moved).at[2:2 + 2 * couples:2].set(receiver + moved)
    return sizes[jax.random.permutation(jax.random.fold_in(key, 2), number_of)]


def centred(own_key, shape, spread, limit, split=(), kind=jnp.bfloat16):
    entries = spread * jax.random.normal(own_key, shape, jnp.float32)
    if split:
        entries = entries * block_levels(own_key, shape, split, -0.22, 0.18)
    return jnp.clip(entries, -limit, limit).astype(kind)


def gaussian_with(key, extent, spread, reach, cuts, heavy, held_as=jnp.bfloat16):
    array = spread * jax.random.normal(key, extent, jnp.float32)
    if cuts:
        array = array * block_levels(key, extent, cuts, -0.22, 0.18)
    return jnp.clip(spiked(array, jax.random.fold_in(key, 3), *heavy), -reach, reach).astype(held_as)


def setup_inputs(seed: int = 0) -> dict:
    key_list = jax.random.split(jax.random.key(seed), 13)
    tokens = gaussian_with(key_list[0], (TOKENS, D), 1.0, 6.0, ((0, 16),), (0, 1, 16, 2.0))
    out_grad = gaussian_with(key_list[1], (TOKENS, D), 1.0, 6.0, ((0, 16),), (0, 1, 16, 2.0))
    doc_lengths = jax.vmap(lambda own: ragged_sizes(own, DOCS, TOK_DEV, MAXLEN, 2))(jax.random.split(key_list[2], PACKS)).reshape((PACKS, DOCS)).astype(jnp.int32)
    w_query = centred(key_list[3], (D, HEADS * HD), D ** -0.5, 0.21875, ((0, 16), (1, 2)), jnp.float32)
    w_key = centred(key_list[4], (D, HEADS * HD), D ** -0.5, 0.21875, ((0, 16), (1, 2)), jnp.float32)
    w_value = centred(key_list[5], (D, HEADS * HD), D ** -0.5, 0.21875, ((0, 16), (1, 2)), jnp.float32)
    w_out = centred(key_list[6], (HEADS * HD, D), (HEADS * HD // 16) ** -0.5, 0.875, ((0, 2), (1, 16)), jnp.float32)
    gain_one = jnp.clip(1.0 + 0.1 * jax.random.normal(key_list[7], (D,), jnp.float32), 0.5, 1.5)
    w_gate = centred(key_list[8], (D, FF), D ** -0.5, 0.21875, ((0, 16), (1, 2)), jnp.float32)
    w_up = centred(key_list[9], (D, FF), D ** -0.5, 0.21875, ((0, 16), (1, 2)), jnp.float32)
    w_down = centred(key_list[10], (FF, D), FF ** -0.5, 0.125, ((0, 2), (1, 16)), jnp.float32)
    gain_two = jnp.clip(1.0 + 0.1 * jax.random.normal(key_list[11], (D,), jnp.float32), 0.5, 1.5)
    return {"tokens": tokens, "out_grad": out_grad, "doc_lengths": doc_lengths, "w_query": w_query, "w_key": w_key, "w_value": w_value, "w_out": w_out, "gain_one": gain_one, "w_gate": w_gate, "w_up": w_up, "w_down": w_down, "gain_two": gain_two}


NORM_EPS = 1e-05
NEG_FILL = -1000000000.0
HIGH = lax.Precision.HIGHEST

@jax.custom_vjp
def low(v):
    return lax.optimization_barrier(v.astype(jnp.bfloat16)).astype(jnp.float32)

@jax.custom_vjp
def low_back(v):
    return v

def low_keep(v):
    return (low(v), None)

def low_pass(kept, grad):
    return (grad,)

def back_keep(v):
    return (v, None)

def back_low(kept, grad):
    return (low(grad),)
low.defvjp(low_keep, low_pass)
low_back.defvjp(back_keep, back_low)

def matmul_high(left, right):
    return jnp.dot(left, right, precision=HIGH, preferred_element_type=jnp.float32)

def rope_tables(positions):
    half_dim = HD // 2
    frequency = jnp.exp(jnp.arange(half_dim, dtype=jnp.float32) * (-2.0 * math.log(10000.0) / HD))
    angles = positions.astype(jnp.float32)[:, None] * frequency[None, :]
    cos_table = jnp.cos(angles)
    sine_table = jnp.sin(angles)
    return (jnp.concatenate([cos_table, cos_table], 1), jnp.concatenate([sine_table, sine_table], 1))

def rotate_half(head_vals):
    half_dim = head_vals.shape[-1] // 2
    return jnp.concatenate([-head_vals[..., half_dim:], head_vals[..., :half_dim]], -1)

def apply_rope(head_vals, cos_table, sine_table):
    return head_vals * cos_table[:, None, :] + rotate_half(head_vals) * sine_table[:, None, :]

def doc_layout(lengths):
    doc_ends = jnp.cumsum(lengths, dtype=jnp.int32)
    starts = doc_ends - lengths
    token_index = jnp.arange(TOK_DEV, dtype=jnp.int32)
    doc_ids = lax.optimization_barrier(jnp.sum((token_index[:, None] >= doc_ends[None, :]).astype(jnp.int32), 1, dtype=jnp.int32))
    doc_picks = doc_ids[:, None] == jnp.arange(DOCS, dtype=jnp.int32)[None, :]
    start_of = lax.optimization_barrier(jnp.sum(jnp.where(doc_picks, starts[None, :], 0), 1, dtype=jnp.int32))
    return (doc_ids, token_index - start_of)

def attend(queries, key_rot, value_heads, doc_ids):
    blocks = TOK_DEV // BLOCK
    token_index = jnp.arange(TOK_DEV, dtype=jnp.int32)
    score_scale = HD ** (-0.5)

    @jax.checkpoint
    def block_fn(pieces):
        query_block, doc_block, index_block = pieces
        raw_scores = jnp.einsum('qhd,khd->hqk', query_block, key_rot, precision=HIGH) * score_scale
        raw_scores = low_back(raw_scores)
        allowed = (doc_block[:, None] == doc_ids[None, :]) & (index_block[:, None] >= token_index[None, :])
        masked = jnp.where(allowed[None], raw_scores, NEG_FILL)
        row_top = lax.optimization_barrier(jnp.max(masked, -1, keepdims=True))
        weights = jnp.exp(masked - row_top)
        soft_probs = weights / lax.optimization_barrier(jnp.sum(weights, -1, keepdims=True))
        return jnp.einsum('hqk,khd->qhd', low(soft_probs), value_heads, precision=HIGH)
    mixed_heads = lax.map(block_fn, (queries.reshape(blocks, BLOCK, HEADS, HD), doc_ids.reshape(blocks, BLOCK), token_index.reshape(blocks, BLOCK)))
    return mixed_heads.reshape(TOK_DEV, HEADS, HD)

def pack_layer(tokens_f, masters, doc_ids, cos_table, sine_table):
    w_query, w_key, w_value, w_out, gain_one, w_gate, w_up, w_down, gain_two = [low(weight) for weight in masters]
    heads_part = HEADS * HD // N_MP
    hidden_part = FF // N_MP
    head_shape = (TOK_DEV, heads_part // HD, HD)
    query_parts = []
    key_parts = []
    value_parts = []
    for mp_group in range(N_MP):
        head_cols = slice(mp_group * heads_part, (mp_group + 1) * heads_part)
        token_in = low_back(tokens_f)
        query_raw = low_back(matmul_high(token_in, w_query[:, head_cols])).reshape(head_shape)
        key_raw = low_back(matmul_high(token_in, w_key[:, head_cols])).reshape(head_shape)
        value_raw = low(low_back(matmul_high(token_in, w_value[:, head_cols]))).reshape(head_shape)
        query_parts.append(low(apply_rope(query_raw, cos_table, sine_table)))
        key_parts.append(low(apply_rope(key_raw, cos_table, sine_table)))
        value_parts.append(value_raw)
    mixed_heads = attend(jnp.concatenate(query_parts, 1), jnp.concatenate(key_parts, 1), jnp.concatenate(value_parts, 1), doc_ids)
    mixed_flat = low(low_back(mixed_heads.reshape(TOK_DEV, HEADS * HD)))
    attn_total = jnp.zeros((TOK_DEV, D), jnp.float32)
    for mp_group in range(N_MP):
        head_cols = slice(mp_group * heads_part, (mp_group + 1) * heads_part)
        attn_total = attn_total + low(matmul_high(mixed_flat[:, head_cols], w_out[head_cols, :]))
    attn_total = low_back(attn_total)
    resid_one = tokens_f + attn_total
    normed_one = resid_one * lax.rsqrt(lax.optimization_barrier(jnp.mean(resid_one * resid_one, -1, keepdims=True)) + NORM_EPS)
    hidden = normed_one * gain_one
    ffn_total = jnp.zeros((TOK_DEV, D), jnp.float32)
    for mp_group in range(N_MP):
        unit_cols = slice(mp_group * hidden_part, (mp_group + 1) * hidden_part)
        hidden_in = low(low_back(hidden))
        gate_proj = low_back(matmul_high(hidden_in, w_gate[:, unit_cols]))
        up_proj = low_back(matmul_high(hidden_in, w_up[:, unit_cols]))
        activated = low(jax.nn.silu(gate_proj) * up_proj)
        ffn_total = ffn_total + low(matmul_high(activated, w_down[unit_cols, :]))
    ffn_total = low_back(ffn_total)
    resid_two = hidden + ffn_total
    normed_two = resid_two * lax.rsqrt(lax.optimization_barrier(jnp.mean(resid_two * resid_two, -1, keepdims=True)) + NORM_EPS)
    return normed_two * gain_two

def reference(tokens, out_grad, doc_lengths, w_query, w_key, w_value, w_out, gain_one, w_gate, w_up, w_down, gain_two):
    masters = tuple((weight.astype(jnp.float32) for weight in (w_query, w_key, w_value, w_out, gain_one, w_gate, w_up, w_down, gain_two)))
    token_packs = tokens.reshape(PACKS, TOK_DEV, D)
    grad_packs = out_grad.reshape(PACKS, TOK_DEV, D)

    def pack_step(running, pieces):
        token_pack, grad_pack, lengths = pieces
        doc_ids, positions = doc_layout(lengths)
        cos_table, sine_table = rope_tables(positions)

        def layer_fn(tokens_f, weights):
            return pack_layer(tokens_f, weights, doc_ids, cos_table, sine_table)
        output, pullback = jax.vjp(layer_fn, token_pack.astype(jnp.float32), masters)
        token_grad, weight_grads = pullback(grad_pack.astype(jnp.float32))
        running = tuple((acc + gradient for acc, gradient in zip(running, weight_grads)))
        return (running, (output.astype(jnp.bfloat16), token_grad))
    initial = tuple((jnp.zeros_like(weight) for weight in masters))
    totals, (outputs, token_grads) = lax.scan(pack_step, initial, (token_packs, grad_packs, doc_lengths))
    return (outputs.reshape(TOKENS, D), token_grads.reshape(TOKENS, D), totals[0], totals[1], totals[2], totals[3], totals[4], totals[5], totals[6], totals[7], totals[8])
```

```python
import functools, math
import jax, jax.numpy as jnp
from jax import lax
from jax.experimental import pallas as pl
from jax.experimental.pallas import tpu as pltpu
HD=48
C2=HD**-0.5*math.log2(math.e)
NEG=-1e30
bf=jnp.bfloat16; f32=jnp.float32
QB=256; LOOK=4
NT=(((1,),(1,)),((),()))
def dot(a,b): return jnp.dot(a,b,preferred_element_type=f32)
def dot_nt(a,b): return lax.dot_general(a,b,NT,preferred_element_type=f32)

def spread(rows, cols, rot):
    r=lax.broadcasted_iota(jnp.int32,(rows,cols),0); c=lax.broadcasted_iota(jnp.int32,(rows,cols),1)
    h=r//64; d=r-h*64
    if not rot:
        return jnp.where((d<HD)&(c==h*HD+d),1.0,0.0).astype(bf)
    lo=(d<24)&(c==h*HD+d+24); hi=(d>=24)&(d<HD)&(c==h*HD+d-24)
    return jnp.where(lo,-1.0,jnp.where(hi,1.0,0.0)).astype(bf)

def proj(tok,w,cos,sin,wq_s,q_s,k_s,v_s,n,cols):
    hp=cols//HD*64
    pairs=hp//128
    for m,(col,rot) in enumerate(((0,False),(0,True),(1,False),(1,True),(2,False))):
        wq_s[m]=dot_nt(spread(hp,cols,rot),w[:,col*cols:(col+1)*cols]).astype(bf)
    def body(b,_):
        rows=pl.ds(pl.multiple_of(b*QB,QB),QB)
        x=tok[rows,:]
        cs=cos[rows,:]; sn=sin[rows,:]
        for dst,a in ((q_s,0),(k_s,2)):
            raw=dot_nt(x,wq_s[a]); rt=dot_nt(x,wq_s[a+1])
            for p in range(pairs):
                l=slice(p*128,p*128+128)
                dst[p,rows,:]=(raw[:,l]*cs+rt[:,l]*sn).astype(bf)
        raw=dot_nt(x,wq_s[4])
        for p in range(pairs):
            v_s[p,rows,:]=raw[:,p*128:p*128+128].astype(bf)
        return 0
    lax.fori_loop(0,n//QB,body,0)

def masks(kk0,nk,i,start):
    kidx=lax.broadcasted_iota(jnp.int32,(nk,QB),0)+kk0
    ok=kidx>=start
    qidx=lax.broadcasted_iota(jnp.int32,(nk,QB),1)+i*QB
    return ok&(kidx<=qidx)

def fwd_head(h,i,q_t,k_s,v_t,start,m_t,lse):
    p=h//2; half=h-2*p
    lo=max(0,i-LOOK)*QB; nk=(i+1)*QB-lo
    kk=slice(lo,lo+nk); qq=slice(i*QB,(i+1)*QB)
    row=lax.broadcasted_iota(jnp.int32,(128,QB),0)
    mine=(row>=half*64)&(row<half*64+64)
    qt=jnp.where(mine,q_t[p,:,qq],jnp.zeros((),bf))
    s=dot(k_s[p,kk,:],qt)
    st=start[:,qq]
    s=jnp.where(masks(lo,nk,i,st),s,NEG)
    m=jnp.max(s,0,keepdims=True)
    e=jnp.exp2((s-m)*C2)
    l=jnp.sum(e,0,keepdims=True)
    pr=(e*(1.0/l)).astype(bf)
    rows=pl.ds(pl.multiple_of(half*64,64),64)
    m_t[p,rows,qq]=dot(v_t[p,rows,kk],pr)
    lse[pl.ds(h,1),qq]=m*C2+jnp.log2(l)

def fwd_kernel(n,cols,tok,w,cos,sin,start,q_o,k_o,v_o,m_t,mixed,lse,wq_s,q_t,v_t):
    proj(tok,w,cos,sin,wq_s,q_o,k_o,v_o,n,cols)
    heads=cols//HD
    for p in range(heads//2):
        q_t[p]=q_o[p].T
        v_t[p]=v_o[p].T
    def body(h,_):
        for i in range(n//QB):
            fwd_head(h,i,q_t,k_o,v_t,start,m_t,lse)
        return 0
    lax.fori_loop(0,heads,body,0)
    for p in range(heads//2):
        mixed[:,p*128:p*128+128]=m_t[p].T.astype(bf)

def attn_fwd(tok,w,cos,sin,start):
    n=tok.shape[0]; cols=w.shape[1]//3; heads=cols//HD; P=heads//2
    V=pl.BlockSpec(memory_space=pltpu.VMEM)
    S=jax.ShapeDtypeStruct
    return pl.pallas_call(functools.partial(fwd_kernel,n,cols),
      out_shape=(S((P,n,128),bf),S((P,n,128),bf),S((P,n,128),bf),S((P,128,n),f32),S((n,P*128),bf),S((heads,n),f32)),
      in_specs=[V]*5,out_specs=[V]*6,
      scratch_shapes=[pltpu.VMEM((5,P*128,w.shape[0]),bf),pltpu.VMEM((P,128,n),bf),pltpu.VMEM((P,128,n),bf)],
      compiler_params=pltpu.CompilerParams(vmem_limit_bytes=60<<20),name="attn_fwd")(tok,w,cos,sin,start)

def bwd_head(h,i,q_t,q_s,k_s,k_t,v_s,dm_t,dm_s,lse,dd,start,dq_t,dk_s,dv_s):
    p=h//2; half=h-2*p
    lo=max(0,i-LOOK)*QB; nk=(i+1)*QB-lo
    kk=slice(lo,lo+nk); qq=slice(i*QB,(i+1)*QB)
    row=lax.broadcasted_iota(jnp.int32,(128,QB),0)
    mine=(row>=half*64)&(row<half*64+64)
    lane=lax.broadcasted_iota(jnp.int32,(QB,128),1)
    mlane=(lane>=half*64)&(lane<half*64+64)
    zero=jnp.zeros((),bf)
    qt=jnp.where(mine,q_t[p,:,qq],zero)
    dmt=jnp.where(mine,dm_t[p,:,qq],zero)
    qn=jnp.where(mlane,q_s[p,qq,:],zero)
    dmn=jnp.where(mlane,dm_s[p,qq,:],zero)
    s=dot(k_s[p,kk,:],qt)
    st=start[:,qq]
    pr=jnp.exp2(jnp.where(masks(lo,nk,i,st),s*C2,NEG)-lse[pl.ds(h,1),qq])
    dp=dot(v_s[p,kk,:],dmt)
    ds=(pr*(dp-dd[pl.ds(h,1),qq])).astype(bf)
    pb=pr.astype(bf)
    dv_s[p,kk,:]+=dot(pb,dmn)
    dk_s[p,kk,:]+=dot(ds,qn)
    rows=pl.ds(pl.multiple_of(half*64,64),64)
    dq_t[p,rows,qq]=dot(k_t[p,rows,kk],ds)

def rope_back(u,cs,sn):
    w=u*sn
    lane=lax.broadcasted_iota(jnp.int32,u.shape,1)&63
    up=pltpu.roll(w,128-24,axis=1); dn=pltpu.roll(w,24,axis=1)
    return u*cs+jnp.where(lane<24,up,jnp.where(lane<48,-dn,0.0))

def bwd_kernel(n,heads,q_s,k_s,v_s,m_t,dm,lse,start,cos,sin,dqkv,q_t,k_t,dm_t,dm_s,dq_t,dk_s,dv_s,dd):
    P=heads//2
    for p in range(P):
        q_t[p]=q_s[p].T
        k_t[p]=k_s[p].T
        dm_s[p]=dm[:,p*128:p*128+128]
        dm_t[p]=dm_s[p].T
        for half in range(2):
            r=slice(half*64,half*64+64)
            dd[2*p+half:2*p+half+1,:]=jnp.sum(dm_t[p,r,:].astype(f32)*m_t[p,r,:],0,keepdims=True)
    dk_s[...]=jnp.zeros_like(dk_s); dv_s[...]=jnp.zeros_like(dv_s)
    def body(h,_):
        for i in range(n//QB):
            bwd_head(h,i,q_t,q_s,k_s,k_t,v_s,dm_t,dm_s,lse,dd,start,dq_t,dk_s,dv_s)
        return 0
    lax.fori_loop(0,heads,body,0)
    sc=HD**-0.5
    for p in range(P):
        dqkv[0,:,p*128:p*128+128]=rope_back(dq_t[p].T*sc,cos[...],sin[...]).astype(bf)
        dqkv[1,:,p*128:p*128+128]=rope_back(dk_s[p]*sc,cos[...],sin[...]).astype(bf)
        dqkv[2,:,p*128:p*128+128]=dv_s[p].astype(bf)

def attn_bwd(q_s,k_s,v_s,m_t,dm,lse,start,cos,sin):
    P,n,_=q_s.shape; heads=2*P
    V=pl.BlockSpec(memory_space=pltpu.VMEM)
    S=jax.ShapeDtypeStruct
    return pl.pallas_call(functools.partial(bwd_kernel,n,heads),
      out_shape=S((3,n,P*128),bf),
      in_specs=[V]*9,out_specs=V,
      scratch_shapes=[pltpu.VMEM((P,128,n),bf),pltpu.VMEM((P,128,n),bf),pltpu.VMEM((P,128,n),bf),pltpu.VMEM((P,n,128),bf),pltpu.VMEM((P,128,n),f32),pltpu.VMEM((P,n,128),f32),pltpu.VMEM((P,n,128),f32),pltpu.VMEM((heads,n),f32)],
      compiler_params=pltpu.CompilerParams(vmem_limit_bytes=60<<20),name="attn_bwd")(q_s,k_s,v_s,m_t,dm,lse,start,cos,sin)


from jax.sharding import Mesh, PartitionSpec as P

NORM_EPS=1e-05
DIAG=[(0,0),(3,3),(1,2),(2,1)]
CORE=[(0,1),(1,0)]

def rms_forward(resid):
    inverse=lax.rsqrt(jnp.mean(resid*resid,-1,keepdims=True)+NORM_EPS)
    return (resid*inverse,inverse)

def rms_backward(grad_normed,normed,inverse):
    return inverse*(grad_normed-normed*jnp.mean(grad_normed*normed,-1,keepdims=True))

def doc_starts(lengths,n):
    at=jnp.arange(n,dtype=jnp.int32); start=jnp.zeros((n,),jnp.int32); end=jnp.int32(0)
    for i in range(lengths.shape[0]-1):
        end=end+lengths[i]
        start=jnp.where(at>=end,end,start)
    return start

def rope_tables(positions):
    half=HD//2
    fr=jnp.exp(jnp.arange(half,dtype=f32)*(-2.0*math.log(10000.0)/HD))
    a=positions.astype(f32)[:,None]*fr[None,:]
    c,s=jnp.cos(a),jnp.sin(a); z=jnp.zeros((positions.shape[0],64-HD),f32)
    return jnp.concatenate([c,c,z,c,c,z],1),jnp.concatenate([s,s,z,s,s,z],1)

def core_sum(part):
    return part.astype(f32)+lax.ppermute(part,"c",CORE).astype(f32)

def on_device(tokens,out_grad,doc_lengths,w_query,w_key,w_value,w_out,gain_one,w_gate,w_up,w_down,gain_two):
    own=lax.axis_index("c")==lax.axis_index("m")
    pick=lambda a: jnp.where(own,a,lax.ppermute(a,"c",CORE))
    tokens,out_grad,doc_lengths=pick(tokens),pick(out_grad),pick(doc_lengths)
    cast=lambda a: a.astype(bf)
    gains=jnp.pad(jnp.stack([cast(gain_one),cast(gain_two)],1),((0,0),(0,126)))
    apack=jnp.concatenate([cast(w_query),cast(w_key),cast(w_value),cast(w_out).T,gains],1)
    fpack=jnp.concatenate([cast(w_gate),cast(w_up),cast(w_down).T],1)
    def gather(a):
        return lax.all_gather(lax.ppermute(a,("c","m"),DIAG),("q","m"),axis=0,tiled=True)
    afull,ffull=gather(apack),gather(fpack)
    cols=w_query.shape[1]; ff=w_gate.shape[1]; n,width=tokens.shape
    hp=cols//HD*64
    put=spread(hp,cols,False)
    out_t=dot_nt(afull[:,3*cols:4*cols],put).astype(bf)
    gain_a=afull[:,4*cols].astype(f32); gain_b=afull[:,4*cols+1].astype(f32)
    gate_w,up_w,down_t=ffull[:,:ff],ffull[:,ff:2*ff],ffull[:,2*ff:]
    start=doc_starts(doc_lengths[0],n)
    cos,sin=rope_tables(jnp.arange(n,dtype=jnp.int32)-start)
    start=start[None]
    q,k,v,m_t,mixed,lse=attn_fwd(tokens,afull[:,:3*cols],cos,sin,start)
    attn=core_sum(dot_nt(mixed,out_t).astype(bf))
    normed_one,inv_one=rms_forward(tokens.astype(f32)+attn)
    hidden=normed_one*gain_a
    hb=hidden.astype(bf)
    gate=dot(hb,gate_w); up=dot(hb,up_w)
    sg=jax.nn.sigmoid(gate)
    act=(gate*sg*up).astype(bf)
    ffn=core_sum(dot_nt(act,down_t).astype(bf))
    normed_two,inv_two=rms_forward(hidden+ffn)
    output=(normed_two*gain_b).astype(bf)
    g=out_grad.astype(f32)
    g_gain_two=jnp.sum(g*normed_two,0)
    d_two=rms_backward(g*gain_b,normed_two,inv_two)
    d_ffn=d_two.astype(bf)
    tn=lambda a,b: lax.dot_general(a,b,(((0,),(0,)),((),())),preferred_element_type=f32)
    d_act=dot(d_ffn,down_t)
    d_up=(d_act*gate*sg).astype(bf)
    d_gate=(d_act*up*sg*(1.0+gate*(1.0-sg))).astype(bf)
    hterm=(dot_nt(d_gate,gate_w)+dot_nt(d_up,up_w)).astype(bf)
    gff=jnp.concatenate([tn(hb,d_gate).astype(bf),tn(hb,d_up).astype(bf),tn(d_ffn,act).astype(bf)],1)
    d_hidden=d_two+core_sum(hterm)
    g_gain_one=jnp.sum(d_hidden*normed_one,0)
    d_one=rms_backward(d_hidden*gain_a,normed_one,inv_one)
    d_attn=d_one.astype(bf)
    g_out=dot(tn(d_attn,mixed).astype(bf),put).astype(bf)
    dm=dot(d_attn,out_t).astype(bf)
    dqkv=attn_bwd(q,k,v,m_t,dm,lse,start,cos,sin)
    term=0.0; gqkv=[]
    for j in range(3):
        wp=dot_nt(afull[:,j*cols:(j+1)*cols],put).astype(bf)
        term=term+dot_nt(dqkv[j],wp)
        gqkv.append(dot(tn(tokens,dqkv[j]).astype(bf),put).astype(bf))
    gtok=(d_one+core_sum(term.astype(bf))).astype(bf)
    ggain=jnp.pad(jnp.stack([g_gain_one,g_gain_two],1),((0,0),(0,126))).astype(bf)
    gatt=jnp.concatenate(gqkv+[g_out,ggain],1)
    def scatter(a):
        return lax.ppermute(lax.psum_scatter(a,("q","m"),scatter_dimension=0,tiled=True),("c","m"),DIAG).astype(f32)
    sff,sat=scatter(gff),scatter(gatt)
    output=lax.ppermute(output,("c","m"),DIAG)
    gtok=lax.ppermute(gtok,("c","m"),DIAG).astype(f32)
    return (output,gtok,sat[:,:cols],sat[:,cols:2*cols],sat[:,2*cols:3*cols],sat[:,3*cols:4*cols].T,sat[:,4*cols],
            sff[:,:ff],sff[:,ff:2*ff],sff[:,2*ff:].T,sat[:,4*cols+1])

def solution(mesh):
    dp,mp=mesh.shape["dp"],mesh.shape["mp"]
    fine=Mesh(mesh.devices.reshape(dp//2,2,mp),("q","c","m"))
    d=("q","c")
    rows,cols_=P(d,"m"),P("m",d)
    return jax.shard_map(on_device,mesh=fine,
        in_specs=(P(d,None),P(d,None),P(d,None),rows,rows,rows,cols_,P(d),rows,rows,cols_,P(d)),
        out_specs=(P(d,None),P(d,None),rows,rows,rows,cols_,P(d),rows,rows,cols_,P(d)),check_vma=False)
```

```python
import functools
import math
import jax, jax.numpy as jnp
from jax import lax
from jax.experimental import pallas as pl
from jax.experimental.pallas import tpu as pltpu
from jax.sharding import Mesh, PartitionSpec as P
MESH=pl.DeviceIdType.MESH
HD=48
C2=HD**-0.5*math.log2(math.e)
NEG=-1e30
bf=jnp.bfloat16; f32=jnp.float32
QB=256; LOOK=4
NT=(((1,),(1,)),((),()))
def dot(a,b): return jnp.dot(a,b,preferred_element_type=f32)
def dot_nt(a,b): return lax.dot_general(a,b,NT,preferred_element_type=f32)

def spread(rows, cols, rot):
    r=lax.broadcasted_iota(jnp.int32,(rows,cols),0); c=lax.broadcasted_iota(jnp.int32,(rows,cols),1)
    h=r//64; d=r-h*64
    if not rot:
        return jnp.where((d<HD)&(c==h*HD+d),1.0,0.0).astype(bf)
    lo=(d<24)&(c==h*HD+d+24); hi=(d>=24)&(d<HD)&(c==h*HD+d-24)
    return jnp.where(lo,-1.0,jnp.where(hi,1.0,0.0)).astype(bf)

def proj(tok,w,cos,sin,wq_s,q_s,k_s,v_s,n,cols):
    hp=cols//HD*64
    pairs=hp//128
    for m,(col,rot) in enumerate(((0,False),(0,True),(1,False),(1,True),(2,False))):
        if len(w.shape)==2:
            part=w[:,col*cols:(col+1)*cols]
        else:
            part=w[:,:,:,:,col*cols:(col+1)*cols].reshape(-1,cols)
        wq_s[m]=dot_nt(spread(hp,cols,rot),part).astype(bf)
    def body(b,_):
        rows=pl.ds(pl.multiple_of(b*QB,QB),QB)
        x=tok[rows,:]
        cs=cos[rows,:]; sn=sin[rows,:]
        for dst,a in ((q_s,0),(k_s,2)):
            raw=dot_nt(x,wq_s[a]); rt=dot_nt(x,wq_s[a+1])
            for p in range(pairs):
                l=slice(p*128,p*128+128)
                dst[p,rows,:]=(raw[:,l]*cs+rt[:,l]*sn).astype(bf)
        raw=dot_nt(x,wq_s[4])
        for p in range(pairs):
            v_s[p,rows,:]=raw[:,p*128:p*128+128].astype(bf)
        return 0
    lax.fori_loop(0,n//QB,body,0)

def masks(kk0,nk,i,start):
    kidx=lax.broadcasted_iota(jnp.int32,(nk,QB),0)+kk0
    ok=kidx>=start
    qidx=lax.broadcasted_iota(jnp.int32,(nk,QB),1)+i*QB
    return ok&(kidx<=qidx)

def fwd_head(h,i,q_t,k_s,v_t,start,m_t,lse):
    p=h//2; half=h-2*p
    lo=max(0,i-LOOK)*QB; nk=(i+1)*QB-lo
    kk=slice(lo,lo+nk); qq=slice(i*QB,(i+1)*QB)
    row=lax.broadcasted_iota(jnp.int32,(128,QB),0)
    mine=(row>=half*64)&(row<half*64+64)
    qt=jnp.where(mine,q_t[p,:,qq],jnp.zeros((),bf))
    s=dot(k_s[p,kk,:],qt)
    st=start[:,qq]
    s=jnp.where(masks(lo,nk,i,st),s,NEG)
    m=jnp.max(s,0,keepdims=True)
    e=jnp.exp2((s-m)*C2)
    l=jnp.sum(e,0,keepdims=True)
    pr=(e*(1.0/l)).astype(bf)
    rows=pl.ds(pl.multiple_of(half*64,64),64)
    m_t[p,rows,qq]=dot(v_t[p,rows,kk],pr)
    lse[pl.ds(h,1),qq]=m*C2+jnp.log2(l)

def fwd_kernel(n,cols,tok,w,cos,sin,start,q_o,k_o,v_o,m_t,mixed,lse,wq_s,q_t,v_t):
    proj(tok,w,cos,sin,wq_s,q_o,k_o,v_o,n,cols)
    heads=cols//HD
    for p in range(heads//2):
        q_t[p]=q_o[p].T
        v_t[p]=v_o[p].T
    def body(h,_):
        for i in range(n//QB):
            fwd_head(h,i,q_t,k_o,v_t,start,m_t,lse)
        return 0
    lax.fori_loop(0,heads,body,0)
    for p in range(heads//2):
        mixed[:,p*128:p*128+128]=m_t[p].T.astype(bf)

def attn_fwd(tok,w,cos,sin,start):
    n=tok.shape[0]; cols=w.shape[1]//3; heads=cols//HD; P=heads//2
    V=pl.BlockSpec(memory_space=pltpu.VMEM)
    S=jax.ShapeDtypeStruct
    return pl.pallas_call(functools.partial(fwd_kernel,n,cols),
      out_shape=(S((P,n,128),bf),S((P,n,128),bf),S((P,n,128),bf),S((P,128,n),f32),S((n,P*128),bf),S((heads,n),f32)),
      in_specs=[V]*5,out_specs=[V]*6,
      scratch_shapes=[pltpu.VMEM((5,P*128,w.shape[0]),bf),pltpu.VMEM((P,128,n),bf),pltpu.VMEM((P,128,n),bf)],
      compiler_params=pltpu.CompilerParams(vmem_limit_bytes=60<<20),name="attn_fwd")(tok,w,cos,sin,start)

def bwd_head(h,i,q_t,q_s,k_s,k_t,v_s,dm_t,dm_s,lse,dd,start,dq_t,dk_s,dv_s):
    p=h//2; half=h-2*p
    lo=max(0,i-LOOK)*QB; nk=(i+1)*QB-lo
    kk=slice(lo,lo+nk); qq=slice(i*QB,(i+1)*QB)
    row=lax.broadcasted_iota(jnp.int32,(128,QB),0)
    mine=(row>=half*64)&(row<half*64+64)
    lane=lax.broadcasted_iota(jnp.int32,(QB,128),1)
    mlane=(lane>=half*64)&(lane<half*64+64)
    zero=jnp.zeros((),bf)
    qt=jnp.where(mine,q_t[p,:,qq],zero)
    dmt=jnp.where(mine,dm_t[p,:,qq],zero)
    qn=jnp.where(mlane,q_s[p,qq,:],zero)
    dmn=jnp.where(mlane,dm_s[p,qq,:],zero)
    s=dot(k_s[p,kk,:],qt)
    st=start[:,qq]
    pr=jnp.exp2(jnp.where(masks(lo,nk,i,st),s*C2,NEG)-lse[pl.ds(h,1),qq])
    dp=dot(v_s[p,kk,:],dmt)
    ds=(pr*(dp-dd[pl.ds(h,1),qq])).astype(bf)
    pb=pr.astype(bf)
    dv_s[p,kk,:]+=dot(pb,dmn)
    dk_s[p,kk,:]+=dot(ds,qn)
    rows=pl.ds(pl.multiple_of(half*64,64),64)
    dq_t[p,rows,qq]=dot(k_t[p,rows,kk],ds)

def rope_back(u,cs,sn):
    w=u*sn
    lane=lax.broadcasted_iota(jnp.int32,u.shape,1)&63
    up=pltpu.roll(w,128-24,axis=1); dn=pltpu.roll(w,24,axis=1)
    return u*cs+jnp.where(lane<24,up,jnp.where(lane<48,-dn,0.0))

def bwd_kernel(n,heads,q_s,k_s,v_s,m_t,dm,lse,start,cos,sin,dqkv,q_t,k_t,dm_t,dm_s,dq_t,dk_s,dv_s,dd):
    P=heads//2
    for p in range(P):
        q_t[p]=q_s[p].T
        k_t[p]=k_s[p].T
        dm_s[p]=dm[:,p*128:p*128+128]
        dm_t[p]=dm_s[p].T
        for half in range(2):
            r=slice(half*64,half*64+64)
            dd[2*p+half:2*p+half+1,:]=jnp.sum(dm_t[p,r,:].astype(f32)*m_t[p,r,:],0,keepdims=True)
    dk_s[...]=jnp.zeros_like(dk_s); dv_s[...]=jnp.zeros_like(dv_s)
    def body(h,_):
        for i in range(n//QB):
            bwd_head(h,i,q_t,q_s,k_s,k_t,v_s,dm_t,dm_s,lse,dd,start,dq_t,dk_s,dv_s)
        return 0
    lax.fori_loop(0,heads,body,0)
    sc=HD**-0.5
    for p in range(P):
        dqkv[0,:,p*128:p*128+128]=rope_back(dq_t[p].T*sc,cos[...],sin[...]).astype(bf)
        dqkv[1,:,p*128:p*128+128]=rope_back(dk_s[p]*sc,cos[...],sin[...]).astype(bf)
        dqkv[2,:,p*128:p*128+128]=dv_s[p].astype(bf)

def attn_bwd(q_s,k_s,v_s,m_t,dm,lse,start,cos,sin):
    P,n,_=q_s.shape; heads=2*P
    V=pl.BlockSpec(memory_space=pltpu.VMEM)
    S=jax.ShapeDtypeStruct
    return pl.pallas_call(functools.partial(bwd_kernel,n,heads),
      out_shape=S((3,n,P*128),bf),
      in_specs=[V]*9,out_specs=V,
      scratch_shapes=[pltpu.VMEM((P,128,n),bf),pltpu.VMEM((P,128,n),bf),pltpu.VMEM((P,128,n),bf),pltpu.VMEM((P,n,128),bf),pltpu.VMEM((P,128,n),f32),pltpu.VMEM((P,n,128),f32),pltpu.VMEM((P,n,128),f32),pltpu.VMEM((heads,n),f32)],
      compiler_params=pltpu.CompilerParams(vmem_limit_bytes=60<<20),name="attn_bwd")(q_s,k_s,v_s,m_t,dm,lse,start,cos,sin)


def place():
    q,m=lax.axis_index("q"),lax.axis_index("m")
    return q//2,lax.rem(q,2),m

def peers(z,y,m):
    return [{"q":z*2+1-y},{"m":1-m}]+[{"q":lax.rem(z+s,4)*2+y} for s in (1,2,3)]

def greet(where):
    barrier=pltpu.get_barrier_semaphore()
    for w in where:
        pl.semaphore_signal(barrier,inc=1,device_id=w,device_id_type=MESH)
    pl.semaphore_wait(barrier,len(where))

class Reduce:
    def __init__(self,source,one,two,three,out,send,recv,first):
        self.source,self.one,self.two,self.three,self.out,self.first=source,one,two,three,out,first
        z,y,m=place()
        self.z,self.y,self.m=z,y,m
        to=peers(z,y,m)
        a,b=(0,1) if first=="y" else (1,0)
        copy=lambda s,d,k,w: pltpu.make_async_remote_copy(src_ref=s,dst_ref=d,send_sem=send.at[k],recv_sem=recv.at[k],device_id=w,device_id_type=MESH)
        away=source.at[:,1-y] if first=="y" else source.at[:,:,1-m]
        self.c1=copy(away,one,0,to[a])
        self.c2=copy(one.at[:,(1-m) if first=="y" else (1-y)],two,1,to[b])
        self.c3=[copy(two.at[lax.rem(z+s,4)],three.at[s-1],1+s,to[1+s]) for s in (1,2,3)]
    def start(self):
        self.c1.start()
    def second(self):
        self.c1.wait_recv()
        def add(i,_):
            zz=i//2; o=i-zz*2
            mine=self.source[zz,self.y,o] if self.first=="y" else self.source[zz,o,self.m]
            self.one[zz,o]=(self.one[zz,o].astype(f32)+mine.astype(f32)).astype(bf)
            return 0
        lax.fori_loop(0,8,add,0)
        self.c2.start()
    def third(self):
        self.c2.wait_recv()
        keep=self.m if self.first=="y" else self.y
        def add(zz,_):
            self.two[zz]=(self.two[zz].astype(f32)+self.one[zz,keep].astype(f32)).astype(bf)
            return 0
        lax.fori_loop(0,4,add,0)
        for c in self.c3: c.start()
    def finish(self):
        for c in self.c3: c.wait_recv()
        t=self.two[self.z].astype(f32)
        for s in range(3): t=t+self.three[s].astype(f32)
        self.out[...]=t.astype(bf)
    def drain(self):
        self.c1.wait_send(); self.c2.wait_send()
        for c in self.c3: c.wait_send()
def chunk_scratch(c):
    return [pltpu.VMEM((4,2,48,c),bf),pltpu.VMEM((4,48,c),bf),pltpu.VMEM((3,48,c),bf),pltpu.SemaphoreType.DMA((5,)),pltpu.SemaphoreType.DMA((5,))]


class Gather:
    def __init__(self,full,cols,send,recv,first):
        z,y,m=place()
        to=peers(z,y,m)
        a,b=(0,1) if first=="y" else (1,0)
        def copy(at,k,w):
            return pltpu.make_async_remote_copy(src_ref=at,dst_ref=at,send_sem=send.at[k],recv_sem=recv.at[k],device_id=w,device_id_type=MESH)
        self.along=[copy(full.at[z,y,m,:,cols],s-1,to[1+s]) for s in (1,2,3)]
        self.c2=copy(full.at[:,y,m,:,cols],3,to[a])
        self.c3=copy(full.at[:,:,m,:,cols] if first=="y" else full.at[:,y,:,:,cols],4,to[b])
    def start(self):
        for c in self.along: c.start()
    def second(self):
        for c in self.along: c.wait_recv()
        self.c2.start()
    def third(self):
        self.c2.wait_recv()
        self.c3.start()
    def finish(self):
        self.c3.wait_recv()
    def drain(self):
        for c in self.along: c.wait_send()
        self.c2.wait_send(); self.c3.wait_send()

def both(c,m):
    return [{"c":1-c},{"c":1-c,"m":1-m}]

def fused_fwd_kernel(n,cols,ff,tok_i,og_i,cos_i,sin_i,start_i,apack,g_i,u_i,d_i,
        tok,og,cos,sin,start,wa,wg,wu,wd,q_o,k_o,v_o,m_t,mixed,lse,
        wq_s,q_t,v_t,swap_s,swap_r,put_s,put_r,a_s,a_r,b_s,b_r,g_s,g_r,u_s,u_r,d_s,d_r,e_s,e_r):
    z,y,m=place(); c=lax.axis_index("c")
    own=c==m
    greet(peers(z,y,m)+both(c,m))
    def remote(s,d,ss,rs,w):
        return pltpu.make_async_remote_copy(src_ref=s,dst_ref=d,send_sem=ss,recv_sem=rs,device_id=w,device_id_type=MESH)
    diag={"c":1-c,"m":1-m}
    shards=[(apack,wa),(g_i,wg),(u_i,wu),(d_i,wd)]
    put_far=[remote(s,d.at[z,y,c],put_s.at[i],put_r.at[i],diag) for i,(s,d) in enumerate(shards)]
    put_near=[pltpu.make_async_copy(s,d.at[z,y,c],put_s.at[i]) for i,(s,d) in enumerate(shards)]
    packs=[(tok_i,tok),(cos_i,cos),(sin_i,sin),(start_i,start),(og_i,og)]
    swap_far=[remote(s,d,swap_s.at[i],swap_r.at[i],{"c":1-c}) for i,(s,d) in enumerate(packs)]
    swap_near=[pltpu.make_async_copy(s,d,swap_r.at[i]) for i,(s,d) in enumerate(packs)]
    @pl.when(own)
    def _():
        for x in put_near: x.start()
        for x in swap_far: x.start()
        for x in swap_near: x.start()
        for x in put_near: x.wait()
    @pl.when(jnp.logical_not(own))
    def _():
        for x in put_far: x.start()
        for x in put_far: x.wait_recv()
    ac=wa.shape[-1]; half=ac//256*128
    a1=Gather(wa,slice(0,half),a_s,a_r,"x"); a2=Gather(wa,slice(half,ac),b_s,b_r,"y")
    fg=[Gather(wg,slice(0,ff),g_s,g_r,"x"),Gather(wu,slice(0,ff),u_s,u_r,"y"),
        Gather(wd,slice(0,ff//2),d_s,d_r,"x"),Gather(wd,slice(ff//2,ff),e_s,e_r,"y")]
    a1.start(); a2.start()
    a1.second(); a2.second()
    for f in fg: f.start()
    a1.third(); a2.third()
    @pl.when(own)
    def _():
        for x in swap_near: x.wait()
    @pl.when(jnp.logical_not(own))
    def _():
        for x in swap_far: x.wait_recv()
    a1.finish(); a2.finish()
    proj(tok,wa,cos,sin,wq_s,q_o,k_o,v_o,n,cols)
    heads=cols//HD
    for p in range(heads//2):
        q_t[p]=q_o[p].T
        v_t[p]=v_o[p].T
    def body(h,_):
        for i in range(n//QB):
            fwd_head(h,i,q_t,k_o,v_t,start,m_t,lse)
        @pl.when(h==0)
        def _():
            fg[0].second(); fg[1].second()
        @pl.when(h==1)
        def _():
            fg[2].second(); fg[3].second()
        @pl.when(h==2)
        def _():
            fg[0].third(); fg[1].third()
        @pl.when(h==4)
        def _():
            fg[2].third(); fg[3].third()
        return 0
    lax.fori_loop(0,heads,body,0)
    for p in range(heads//2):
        mixed[:,p*128:p*128+128]=m_t[p].T.astype(bf)
    for f in fg: f.finish()
    for f in [a1,a2]+fg: f.drain()
    @pl.when(own)
    def _():
        for x in swap_far: x.wait_send()
    @pl.when(jnp.logical_not(own))
    def _():
        for x in put_far: x.wait_send()

def fused_fwd(tok,og,cos,sin,start,apack,g,u,d,cols):
    n,width=tok.shape; heads=cols//HD; pr=heads//2; ff=g.shape[1]
    V=pl.BlockSpec(memory_space=pltpu.VMEM); A=pl.BlockSpec(memory_space=pl.ANY)
    S=jax.ShapeDtypeStruct
    like=lambda a: S(a.shape,a.dtype)
    wide=lambda a: S((4,2,2)+a.shape,bf)
    dma=lambda k: pltpu.SemaphoreType.DMA((k,))
    return pl.pallas_call(functools.partial(fused_fwd_kernel,n,cols,ff),
      out_shape=[like(tok),like(og),like(cos),like(sin),like(start),wide(apack),wide(g),wide(u),wide(d),
        S((pr,n,128),bf),S((pr,n,128),bf),S((pr,n,128),bf),S((pr,128,n),f32),S((n,pr*128),bf),S((heads,n),f32)],
      in_specs=[A]*9,out_specs=[V,A,V,V,V,V,A,A,A]+[V]*6,
      scratch_shapes=[pltpu.VMEM((5,pr*128,width),bf),pltpu.VMEM((pr,128,n),bf),pltpu.VMEM((pr,128,n),bf),
        dma(5),dma(5),dma(4),dma(4)]+[dma(5)]*12,
      compiler_params=pltpu.CompilerParams(vmem_limit_bytes=60<<20,collective_id=0,has_side_effects=True),name="attn_fwd_gather")(tok,og,cos,sin,start,apack,g,u,d)

def fused_bwd_kernel(n,heads,q_s,k_s,v_s,m_t,dm,lse,start,cos,sin,gg,gu,gd,dqkv,og,ou,od,q_t,k_t,dm_t,dm_s,dq_t,dk_s,dv_s,dd,*scr):
    z,y,m=place()
    greet(peers(z,y,m))
    half=gg.shape[-1]//2
    ch=[]
    for k in range(6):
        sl=slice((k%2)*half,(k%2)*half+half)
        src,dst=((gd,od),(gg,og),(gu,ou))[k//2]
        one,two,three,s,r=scr[5*k:5*k+5]
        ch.append(Reduce(src.at[:,:,:,:,sl],one,two,three,dst.at[:,sl],s,r,"yx"[k%2]))
    for x in ch[:4]: x.start()
    P_=heads//2
    for p in range(P_):
        q_t[p]=q_s[p].T
        k_t[p]=k_s[p].T
        dm_s[p]=dm[:,p*128:p*128+128]
        dm_t[p]=dm_s[p].T
        for half_ in range(2):
            r=slice(half_*64,half_*64+64)
            dd[2*p+half_:2*p+half_+1,:]=jnp.sum(dm_t[p,r,:].astype(f32)*m_t[p,r,:],0,keepdims=True)
    dk_s[...]=jnp.zeros_like(dk_s); dv_s[...]=jnp.zeros_like(dv_s)
    plan={2:[(0,"second"),(1,"second"),(4,"start"),(5,"start")],3:[(0,"third"),(1,"third")],4:[(2,"second"),(3,"second")],
          5:[(2,"third"),(3,"third")],6:[(0,"finish"),(1,"finish")],7:[(4,"second"),(5,"second")]}
    def body(h,_):
        for i in range(n//QB):
            bwd_head(h,i,q_t,q_s,k_s,k_t,v_s,dm_t,dm_s,lse,dd,start,dq_t,dk_s,dv_s)
        for at,todo in plan.items():
            @pl.when(h==at)
            def _():
                for k,what in todo: getattr(ch[k],what)()
        return 0
    lax.fori_loop(0,heads,body,0)
    ch[4].third(); ch[5].third()
    sc=HD**-0.5
    for p in range(P_):
        dqkv[0,:,p*128:p*128+128]=rope_back(dq_t[p].T*sc,cos[...],sin[...]).astype(bf)
        dqkv[1,:,p*128:p*128+128]=rope_back(dk_s[p]*sc,cos[...],sin[...]).astype(bf)
        dqkv[2,:,p*128:p*128+128]=dv_s[p].astype(bf)
    for k in (2,3,4,5): ch[k].finish()
    for x in ch: x.drain()

def fused_bwd(q_s,k_s,v_s,m_t,dm,lse,start,cos,sin,gg,gu,gd):
    pr,n,_=q_s.shape; heads=2*pr
    V=pl.BlockSpec(memory_space=pltpu.VMEM)
    S=jax.ShapeDtypeStruct
    ff=gg.shape[1]
    cut=lambda a: a.reshape(4,2,2,48,ff)
    return pl.pallas_call(functools.partial(fused_bwd_kernel,n,heads),
      out_shape=[S((3,n,pr*128),bf)]+[S((48,ff),bf)]*3,
      in_specs=[V]*12,out_specs=[V]*4,
      scratch_shapes=[pltpu.VMEM((pr,128,n),bf),pltpu.VMEM((pr,128,n),bf),pltpu.VMEM((pr,128,n),bf),pltpu.VMEM((pr,n,128),bf),pltpu.VMEM((pr,128,n),f32),pltpu.VMEM((pr,n,128),f32),pltpu.VMEM((pr,n,128),f32),pltpu.VMEM((heads,n),f32)]
        +sum([chunk_scratch(ff//2) for _ in range(6)],[]),
      compiler_params=pltpu.CompilerParams(vmem_limit_bytes=62<<20,collective_id=1,has_side_effects=True),name="attn_bwd_reduce")(
        q_s,k_s,v_s,m_t,dm,lse,start,cos,sin,cut(gg),cut(gu),cut(gd))

def reduce_kernel(g,out,*scr):
    z,y,m=place()
    greet(peers(z,y,m))
    w=g.shape[-1]; half=w//256*128
    ch=[]
    for k,(sl,first) in enumerate(((slice(0,half),"x"),(slice(half,w),"y"))):
        one,two,three,s,r=scr[5*k:5*k+5]
        ch.append(Reduce(g.at[:,:,:,:,sl],one,two,three,out.at[:,sl],s,r,first))
    for what in ("start","second","third","finish","drain"):
        for x in ch: getattr(x,what)()

def reduce_call(g):
    V=pl.BlockSpec(memory_space=pltpu.VMEM)
    w=g.shape[1]; half=w//256*128
    return pl.pallas_call(reduce_kernel,out_shape=jax.ShapeDtypeStruct((48,w),bf),in_specs=[V],out_specs=V,
      scratch_shapes=chunk_scratch(half)+chunk_scratch(w-half),
      compiler_params=pltpu.CompilerParams(vmem_limit_bytes=40<<20,collective_id=2,has_side_effects=True),name="reduce")(g.reshape(4,2,2,48,w))


NORM_EPS=1e-05
DIAG=[(0,0),(3,3),(1,2),(2,1)]
CORE=[(0,1),(1,0)]

def rms_forward(resid):
    inverse=lax.rsqrt(jnp.mean(resid*resid,-1,keepdims=True)+NORM_EPS)
    return (resid*inverse,inverse)

def rms_backward(grad_normed,normed,inverse):
    return inverse*(grad_normed-normed*jnp.mean(grad_normed*normed,-1,keepdims=True))

def doc_starts(lengths,n):
    at=jnp.arange(n,dtype=jnp.int32); start=jnp.zeros((n,),jnp.int32); end=jnp.int32(0)
    for i in range(lengths.shape[0]-1):
        end=end+lengths[i]
        start=jnp.where(at>=end,end,start)
    return start

def rope_tables(positions):
    half=HD//2
    fr=jnp.exp(jnp.arange(half,dtype=f32)*(-2.0*math.log(10000.0)/HD))
    a=positions.astype(f32)[:,None]*fr[None,:]
    c,s=jnp.cos(a),jnp.sin(a); z=jnp.zeros((positions.shape[0],64-HD),f32)
    return jnp.concatenate([c,c,z,c,c,z],1),jnp.concatenate([s,s,z,s,s,z],1)

def core_sum(part):
    return part.astype(f32)+lax.ppermute(part,"c",CORE).astype(f32)

def on_device(tokens,out_grad,doc_lengths,w_query,w_key,w_value,w_out,gain_one,w_gate,w_up,w_down,gain_two):
    cols=w_query.shape[1]; ff=w_gate.shape[1]; n,width=tokens.shape
    quad=lax.axis_size("q")==8 and w_query.shape[0]==48
    if not quad:
        own=lax.axis_index("c")==lax.axis_index("m")
        pick=lambda a: jnp.where(own,a,lax.ppermute(a,"c",CORE))
        tokens,out_grad,doc_lengths=pick(tokens),pick(out_grad),pick(doc_lengths)
    start=doc_starts(doc_lengths[0],n)
    cos,sin=rope_tables(jnp.arange(n,dtype=jnp.int32)-start)
    start=start[None]
    cast=lambda a: a.astype(bf)
    gains=jnp.pad(jnp.stack([cast(gain_one),cast(gain_two)],1),((0,0),(0,126)))
    apack=jnp.concatenate([cast(w_query),cast(w_key),cast(w_value),cast(w_out).T,gains],1)
    def gather(a):
        return lax.all_gather(lax.ppermute(a,("c","m"),DIAG),("q","m"),axis=0,tiled=True)
    if quad:
        tokens,out_grad,cos,sin,start,afull,gate_w,up_w,down_t,q,k,v,m_t,mixed,lse=fused_fwd(
            tokens,out_grad,cos,sin,start,apack,cast(w_gate),cast(w_up),cast(w_down).T,cols)
        afull,gate_w,up_w,down_t=[a.reshape(width,a.shape[-1]) for a in (afull,gate_w,up_w,down_t)]
    else:
        afull,gate_w,up_w,down_t=[gather(a) for a in (apack,cast(w_gate),cast(w_up),cast(w_down).T)]
        q,k,v,m_t,mixed,lse=attn_fwd(tokens,afull[:,:3*cols],cos,sin,start)
    hp=cols//HD*64
    put=spread(hp,cols,False)
    out_t=dot_nt(afull[:,3*cols:4*cols],put).astype(bf)
    gain_a=afull[:,4*cols].astype(f32); gain_b=afull[:,4*cols+1].astype(f32)
    attn=core_sum(dot_nt(mixed,out_t).astype(bf))
    normed_one,inv_one=rms_forward(tokens.astype(f32)+attn)
    hidden=normed_one*gain_a
    hb=hidden.astype(bf)
    gate=dot(hb,gate_w); up=dot(hb,up_w)
    sg=jax.nn.sigmoid(gate)
    act=(gate*sg*up).astype(bf)
    ffn=core_sum(dot_nt(act,down_t).astype(bf))
    normed_two,inv_two=rms_forward(hidden+ffn)
    output=(normed_two*gain_b).astype(bf)
    g=out_grad.astype(f32)
    g_gain_two=jnp.sum(g*normed_two,0)
    d_two=rms_backward(g*gain_b,normed_two,inv_two)
    d_ffn=d_two.astype(bf)
    tn=lambda a,b: lax.dot_general(a,b,(((0,),(0,)),((),())),preferred_element_type=f32)
    d_act=dot(d_ffn,down_t)
    d_up=(d_act*gate*sg).astype(bf)
    d_gate=(d_act*up*sg*(1.0+gate*(1.0-sg))).astype(bf)
    hterm=(dot_nt(d_gate,gate_w)+dot_nt(d_up,up_w)).astype(bf)
    gff=[tn(hb,d_gate).astype(bf),tn(hb,d_up).astype(bf),tn(d_ffn,act).astype(bf)]
    d_hidden=d_two+core_sum(hterm)
    g_gain_one=jnp.sum(d_hidden*normed_one,0)
    d_one=rms_backward(d_hidden*gain_a,normed_one,inv_one)
    d_attn=d_one.astype(bf)
    g_out=dot(tn(d_attn,mixed).astype(bf),put).astype(bf)
    dm=dot(d_attn,out_t).astype(bf)
    if quad:
        dqkv,*sff=fused_bwd(q,k,v,m_t,dm,lse,start,cos,sin,*gff)
    else:
        dqkv=attn_bwd(q,k,v,m_t,dm,lse,start,cos,sin)
    term=0.0; gqkv=[]
    for j in range(3):
        wp=dot_nt(afull[:,j*cols:(j+1)*cols],put).astype(bf)
        term=term+dot_nt(dqkv[j],wp)
        gqkv.append(dot(tn(tokens,dqkv[j]).astype(bf),put).astype(bf))
    gtok=(d_one+core_sum(term.astype(bf))).astype(bf)
    ggain=jnp.pad(jnp.stack([g_gain_one,g_gain_two],1),((0,0),(0,126))).astype(bf)
    gatt=jnp.concatenate(gqkv+[g_out,ggain],1)
    if quad:
        sat=reduce_call(gatt)
    else:
        add=lambda a: lax.psum_scatter(a,("q","m"),scatter_dimension=0,tiled=True)
        sff,sat=[add(a) for a in gff],add(gatt)
    sff,sat=lax.ppermute(jnp.concatenate(sff,1),("c","m"),DIAG).astype(f32),lax.ppermute(sat,("c","m"),DIAG).astype(f32)
    output=lax.ppermute(output,("c","m"),DIAG)
    gtok=lax.ppermute(gtok,("c","m"),DIAG).astype(f32)
    return (output,gtok,sat[:,:cols],sat[:,cols:2*cols],sat[:,2*cols:3*cols],sat[:,3*cols:4*cols].T,sat[:,4*cols],
            sff[:,:ff],sff[:,ff:2*ff],sff[:,2*ff:].T,sat[:,4*cols+1])

def solution(mesh):
    dp,mp=mesh.shape["dp"],mesh.shape["mp"]
    fine=Mesh(mesh.devices.reshape(dp//2,2,mp),("q","c","m"))
    d=("q","c")
    rows,cols_=P(d,"m"),P("m",d)
    return jax.shard_map(on_device,mesh=fine,
        in_specs=(P(d,None),P(d,None),P(d,None),rows,rows,rows,cols_,P(d),rows,rows,cols_,P(d)),
        out_specs=(P(d,None),P(d,None),rows,rows,rows,cols_,P(d),rows,rows,cols_,P(d)),check_vma=False)
```

```python
import functools
import math
import jax, jax.numpy as jnp
from jax import lax
from jax.experimental import pallas as pl
from jax.experimental.pallas import tpu as pltpu
from jax.sharding import Mesh, PartitionSpec as P
MESH=pl.DeviceIdType.MESH
HD=48
C2=HD**-0.5*math.log2(math.e)
NEG=-1e30
bf=jnp.bfloat16; f32=jnp.float32
QB=256; LOOK=4
NT=(((1,),(1,)),((),()))
def dot(a,b): return jnp.dot(a,b,preferred_element_type=f32)
def dot_nt(a,b): return lax.dot_general(a,b,NT,preferred_element_type=f32)

def spread(rows, cols, rot):
    r=lax.broadcasted_iota(jnp.int32,(rows,cols),0); c=lax.broadcasted_iota(jnp.int32,(rows,cols),1)
    h=r//64; d=r-h*64
    if not rot:
        return jnp.where((d<HD)&(c==h*HD+d),1.0,0.0).astype(bf)
    lo=(d<24)&(c==h*HD+d+24); hi=(d>=24)&(d<HD)&(c==h*HD+d-24)
    return jnp.where(lo,-1.0,jnp.where(hi,1.0,0.0)).astype(bf)

def proj(tok,w,cos,sin,wq_s,q_s,k_s,v_s,n,cols):
    hp=cols//HD*64
    pairs=hp//128
    for m,(col,rot) in enumerate(((0,False),(0,True),(1,False),(1,True),(2,False))):
        if len(w.shape)==2:
            part=w[:,col*cols:(col+1)*cols]
        else:
            part=w[:,:,:,:,col*cols:(col+1)*cols].reshape(-1,cols)
        wq_s[m]=dot_nt(spread(hp,cols,rot),part).astype(bf)
    def body(b,_):
        rows=pl.ds(pl.multiple_of(b*QB,QB),QB)
        x=tok[rows,:]
        cs=cos[rows,:]; sn=sin[rows,:]
        for dst,a in ((q_s,0),(k_s,2)):
            raw=dot_nt(x,wq_s[a]); rt=dot_nt(x,wq_s[a+1])
            for p in range(pairs):
                l=slice(p*128,p*128+128)
                dst[p,rows,:]=(raw[:,l]*cs+rt[:,l]*sn).astype(bf)
        raw=dot_nt(x,wq_s[4])
        for p in range(pairs):
            v_s[p,rows,:]=raw[:,p*128:p*128+128].astype(bf)
        return 0
    lax.fori_loop(0,n//QB,body,0)

def masks(kk0,nk,i,start):
    kidx=lax.broadcasted_iota(jnp.int32,(nk,QB),0)+kk0
    ok=kidx>=start
    qidx=lax.broadcasted_iota(jnp.int32,(nk,QB),1)+i*QB
    return ok&(kidx<=qidx)

def fwd_head(h,i,q_t,k_s,v_t,start,m_t,lse):
    p=h//2; half=h-2*p
    lo=max(0,i-LOOK)*QB; nk=(i+1)*QB-lo
    kk=slice(lo,lo+nk); qq=slice(i*QB,(i+1)*QB)
    row=lax.broadcasted_iota(jnp.int32,(128,QB),0)
    mine=(row>=half*64)&(row<half*64+64)
    qt=jnp.where(mine,q_t[p,:,qq],jnp.zeros((),bf))
    s=dot(k_s[p,kk,:],qt)
    st=start[:,qq]
    s=jnp.where(masks(lo,nk,i,st),s,NEG)
    m=jnp.max(s,0,keepdims=True)
    e=jnp.exp2((s-m)*C2)
    l=jnp.sum(e,0,keepdims=True)
    pr=(e*(1.0/l)).astype(bf)
    rows=pl.ds(pl.multiple_of(half*64,64),64)
    m_t[p,rows,qq]=dot(v_t[p,rows,kk],pr)
    lse[pl.ds(h,1),qq]=m*C2+jnp.log2(l)

def fwd_kernel(n,cols,tok,w,cos,sin,start,q_o,k_o,v_o,m_t,mixed,lse,wq_s,q_t,v_t):
    proj(tok,w,cos,sin,wq_s,q_o,k_o,v_o,n,cols)
    heads=cols//HD
    for p in range(heads//2):
        q_t[p]=q_o[p].T
        v_t[p]=v_o[p].T
    def body(h,_):
        for i in range(n//QB):
            fwd_head(h,i,q_t,k_o,v_t,start,m_t,lse)
        return 0
    lax.fori_loop(0,heads,body,0)
    for p in range(heads//2):
        mixed[:,p*128:p*128+128]=m_t[p].T.astype(bf)

def attn_fwd(tok,w,cos,sin,start):
    n=tok.shape[0]; cols=w.shape[1]//3; heads=cols//HD; P=heads//2
    V=pl.BlockSpec(memory_space=pltpu.VMEM)
    S=jax.ShapeDtypeStruct
    return pl.pallas_call(functools.partial(fwd_kernel,n,cols),
      out_shape=(S((P,n,128),bf),S((P,n,128),bf),S((P,n,128),bf),S((P,128,n),f32),S((n,P*128),bf),S((heads,n),f32)),
      in_specs=[V]*5,out_specs=[V]*6,
      scratch_shapes=[pltpu.VMEM((5,P*128,w.shape[0]),bf),pltpu.VMEM((P,128,n),bf),pltpu.VMEM((P,128,n),bf)],
      compiler_params=pltpu.CompilerParams(vmem_limit_bytes=60<<20),name="attn_fwd")(tok,w,cos,sin,start)

def bwd_head(h,i,q_t,q_s,k_s,k_t,v_s,dm_t,dm_s,lse,dd,start,dq_t,dk_s,dv_s):
    p=h//2; half=h-2*p
    lo=max(0,i-LOOK)*QB; nk=(i+1)*QB-lo
    kk=slice(lo,lo+nk); qq=slice(i*QB,(i+1)*QB)
    row=lax.broadcasted_iota(jnp.int32,(128,QB),0)
    mine=(row>=half*64)&(row<half*64+64)
    lane=lax.broadcasted_iota(jnp.int32,(QB,128),1)
    mlane=(lane>=half*64)&(lane<half*64+64)
    zero=jnp.zeros((),bf)
    qt=jnp.where(mine,q_t[p,:,qq],zero)
    dmt=jnp.where(mine,dm_t[p,:,qq],zero)
    qn=jnp.where(mlane,q_s[p,qq,:],zero)
    dmn=jnp.where(mlane,dm_s[p,qq,:],zero)
    s=dot(k_s[p,kk,:],qt)
    st=start[:,qq]
    pr=jnp.exp2(jnp.where(masks(lo,nk,i,st),s*C2,NEG)-lse[pl.ds(h,1),qq])
    dp=dot(v_s[p,kk,:],dmt)
    ds=(pr*(dp-dd[pl.ds(h,1),qq])).astype(bf)
    pb=pr.astype(bf)
    dv_s[p,kk,:]+=dot(pb,dmn)
    dk_s[p,kk,:]+=dot(ds,qn)
    rows=pl.ds(pl.multiple_of(half*64,64),64)
    dq_t[p,rows,qq]=dot(k_t[p,rows,kk],ds)

def rope_back(u,cs,sn):
    w=u*sn
    lane=lax.broadcasted_iota(jnp.int32,u.shape,1)&63
    up=pltpu.roll(w,128-24,axis=1); dn=pltpu.roll(w,24,axis=1)
    return u*cs+jnp.where(lane<24,up,jnp.where(lane<48,-dn,0.0))

def bwd_kernel(n,heads,q_s,k_s,v_s,m_t,dm,lse,start,cos,sin,dqkv,q_t,k_t,dm_t,dm_s,dq_t,dk_s,dv_s,dd):
    P=heads//2
    for p in range(P):
        q_t[p]=q_s[p].T
        k_t[p]=k_s[p].T
        dm_s[p]=dm[:,p*128:p*128+128]
        dm_t[p]=dm_s[p].T
        for half in range(2):
            r=slice(half*64,half*64+64)
            dd[2*p+half:2*p+half+1,:]=jnp.sum(dm_t[p,r,:].astype(f32)*m_t[p,r,:],0,keepdims=True)
    dk_s[...]=jnp.zeros_like(dk_s); dv_s[...]=jnp.zeros_like(dv_s)
    def body(h,_):
        for i in range(n//QB):
            bwd_head(h,i,q_t,q_s,k_s,k_t,v_s,dm_t,dm_s,lse,dd,start,dq_t,dk_s,dv_s)
        return 0
    lax.fori_loop(0,heads,body,0)
    sc=HD**-0.5
    for p in range(P):
        dqkv[0,:,p*128:p*128+128]=rope_back(dq_t[p].T*sc,cos[...],sin[...]).astype(bf)
        dqkv[1,:,p*128:p*128+128]=rope_back(dk_s[p]*sc,cos[...],sin[...]).astype(bf)
        dqkv[2,:,p*128:p*128+128]=dv_s[p].astype(bf)

def attn_bwd(q_s,k_s,v_s,m_t,dm,lse,start,cos,sin):
    P,n,_=q_s.shape; heads=2*P
    V=pl.BlockSpec(memory_space=pltpu.VMEM)
    S=jax.ShapeDtypeStruct
    return pl.pallas_call(functools.partial(bwd_kernel,n,heads),
      out_shape=S((3,n,P*128),bf),
      in_specs=[V]*9,out_specs=V,
      scratch_shapes=[pltpu.VMEM((P,128,n),bf),pltpu.VMEM((P,128,n),bf),pltpu.VMEM((P,128,n),bf),pltpu.VMEM((P,n,128),bf),pltpu.VMEM((P,128,n),f32),pltpu.VMEM((P,n,128),f32),pltpu.VMEM((P,n,128),f32),pltpu.VMEM((heads,n),f32)],
      compiler_params=pltpu.CompilerParams(vmem_limit_bytes=60<<20),name="attn_bwd")(q_s,k_s,v_s,m_t,dm,lse,start,cos,sin)


def place():
    q,m=lax.axis_index("q"),lax.axis_index("m")
    return q//2,lax.rem(q,2),m

def peers(z,y,m):
    return [{"q":z*2+1-y},{"m":1-m}]+[{"q":lax.rem(z+s,4)*2+y} for s in (1,2,3)]

def greet(where):
    barrier=pltpu.get_barrier_semaphore()
    for w in where:
        pl.semaphore_signal(barrier,inc=1,device_id=w,device_id_type=MESH)
    pl.semaphore_wait(barrier,len(where))

class Halve:
    def __init__(self,source,one,two,send,recv,first):
        self.source,self.one,self.two,self.first=source,one,two,first
        z,y,m=place()
        self.y,self.m=y,m
        to=peers(z,y,m)
        a,b=(0,1) if first=="y" else (1,0)
        copy=lambda s,d,k,w: pltpu.make_async_remote_copy(src_ref=s,dst_ref=d,send_sem=send.at[k],recv_sem=recv.at[k],device_id=w,device_id_type=MESH)
        self.c1=copy(source.at[:,1-y] if first=="y" else source.at[:,:,1-m],one,0,to[a])
        self.c2=copy(one.at[:,(1-m) if first=="y" else (1-y)],two,1,to[b])
    def start(self):
        self.c1.start()
    def second(self):
        self.c1.wait_recv()
        def add(i,_):
            zz=i//2; o=i-zz*2
            mine=self.source[zz,self.y,o] if self.first=="y" else self.source[zz,o,self.m]
            self.one[zz,o]=(self.one[zz,o].astype(f32)+mine.astype(f32)).astype(bf)
            return 0
        lax.fori_loop(0,8,add,0)
        self.c2.start()
    def third(self):
        self.c2.wait_recv()
        keep=self.m if self.first=="y" else self.y
        def add(zz,_):
            self.two[zz]=(self.two[zz].astype(f32)+self.one[zz,keep].astype(f32)).astype(bf)
            return 0
        lax.fori_loop(0,4,add,0)
    def drain(self):
        self.c1.wait_send(); self.c2.wait_send()

class Quarter:
    def __init__(self,two,three,out,send,recv):
        self.two,self.three,self.out=two,three,out
        z,y,m=place()
        self.z=z
        to=peers(z,y,m)
        self.c3=[pltpu.make_async_remote_copy(src_ref=two.at[lax.rem(z+s,4)],dst_ref=three.at[s-1],send_sem=send.at[s-1],recv_sem=recv.at[s-1],
            device_id=to[1+s],device_id_type=MESH) for s in (1,2,3)]
    def start(self):
        for c in self.c3: c.start()
    def finish(self):
        for c in self.c3: c.wait_recv()
        t=self.two[self.z].astype(f32)
        for s in range(3): t=t+self.three[s].astype(f32)
        self.out[...]=t.astype(bf)
    def drain(self):
        for c in self.c3: c.wait_send()

def halve_scratch(c):
    return [pltpu.VMEM((4,2,48,c),bf),pltpu.SemaphoreType.DMA((2,)),pltpu.SemaphoreType.DMA((2,))]
def quarter_scratch(c):
    return [pltpu.VMEM((3,48,c),bf),pltpu.SemaphoreType.DMA((3,)),pltpu.SemaphoreType.DMA((3,))]


class Gather:
    def __init__(self,full,cols,send,recv,first):
        z,y,m=place()
        to=peers(z,y,m)
        a,b=(0,1) if first=="y" else (1,0)
        def copy(at,k,w):
            return pltpu.make_async_remote_copy(src_ref=at,dst_ref=at,send_sem=send.at[k],recv_sem=recv.at[k],device_id=w,device_id_type=MESH)
        self.along=[copy(full.at[z,y,m,:,cols],s-1,to[1+s]) for s in (1,2,3)]
        self.c2=copy(full.at[:,y,m,:,cols],3,to[a])
        self.c3=copy(full.at[:,:,m,:,cols] if first=="y" else full.at[:,y,:,:,cols],4,to[b])
    def start(self):
        for c in self.along: c.start()
    def second(self):
        for c in self.along: c.wait_recv()
        self.c2.start()
    def third(self):
        self.c2.wait_recv()
        self.c3.start()
    def finish(self):
        self.c3.wait_recv()
    def drain(self):
        for c in self.along: c.wait_send()
        self.c2.wait_send(); self.c3.wait_send()

def both(c,m):
    return [{"c":1-c},{"c":1-c,"m":1-m}]

def fused_fwd_kernel(n,cols,ff,tok_i,og_i,cos_i,sin_i,start_i,a_i,o_i,g_i,u_i,d_i,
        tok,og,cos,sin,start,wa,wo,wg,wu,wd,q_o,k_o,v_o,m_t,mixed,lse,tok_t,wt,
        wq_s,q_t,v_t,swap_s,swap_r,put_s,put_r,*sems):
    z,y,m=place(); c=lax.axis_index("c")
    own=c==m
    greet(peers(z,y,m)+both(c,m))
    def remote(s,d,ss,rs,w):
        return pltpu.make_async_remote_copy(src_ref=s,dst_ref=d,send_sem=ss,recv_sem=rs,device_id=w,device_id_type=MESH)
    diag={"c":1-c,"m":1-m}
    shards=[(a_i,wa),(g_i,wg),(u_i,wu),(d_i,wd),(o_i,wo)]
    put_far=[remote(s,d.at[z,y,c],put_s.at[i],put_r.at[i],diag) for i,(s,d) in enumerate(shards)]
    put_near=[pltpu.make_async_copy(s,d.at[z,y,c],put_r.at[i]) for i,(s,d) in enumerate(shards)]
    packs=[(tok_i,tok),(cos_i,cos),(sin_i,sin),(start_i,start),(og_i,og)]
    swap_far=[remote(s,d,swap_s.at[i],swap_r.at[i],{"c":1-c}) for i,(s,d) in enumerate(packs)]
    swap_near=[pltpu.make_async_copy(s,d,swap_r.at[i]) for i,(s,d) in enumerate(packs)]
    @pl.when(own)
    def _():
        for x in put_near: x.start()
        for a,b in zip(swap_near,swap_far):
            a.start(); b.start()
        put_near[0].wait()
    @pl.when(jnp.logical_not(own))
    def _():
        for x in put_far: x.start()
        put_far[0].wait_recv()
    def ga(full,lo,hi,k,first): return Gather(full,slice(lo,hi),sems[2*k],sems[2*k+1],first)
    ac=wa.shape[-1]; cut=[0,ac//1280*256,ac//2,ac//2+ac//1280*384,ac]
    a=[ga(wa,cut[i],cut[i+1],i,"xy"[i%2]) for i in range(4)]
    h2=ff//2
    f=[ga(w,j*h2,j*h2+h2,4+2*i+j,"xy"[j]) for i,w in enumerate((wg,wu,wd)) for j in range(2)]
    f.append(ga(wo,0,wo.shape[-1],10,"x"))
    for x in a: x.start()
    @pl.when(own)
    def _():
        for x in put_near[1:]: x.wait()
    @pl.when(jnp.logical_not(own))
    def _():
        for x in put_far[1:]: x.wait_recv()
    a[0].second(); a[1].second()
    for x in f: x.start()
    @pl.when(own)
    def _():
        for x in swap_near: x.wait()
    @pl.when(jnp.logical_not(own))
    def _():
        for x in swap_far: x.wait_recv()
    a[0].third(); a[1].third()
    a[2].second(); a[3].second()
    tok_t[:tok_t.shape[0]//2,:]=tok[:,:tok_t.shape[0]//2].T
    a[2].third(); a[3].third()
    tok_t[tok_t.shape[0]//2:,:]=tok[:,tok_t.shape[0]//2:].T
    for x in a: x.finish()
    f[0].second(); f[1].second()
    proj(tok,wa,cos,sin,wq_s,q_o,k_o,v_o,n,cols)
    f[0].third(); f[1].third()
    f[2].second(); f[3].second()
    for j in range(3): wt[j]=wq_s[2*j]
    heads=cols//HD
    for p in range(heads//2):
        q_t[p]=q_o[p].T
        v_t[p]=v_o[p].T
    plan={1:[(4,"second"),(5,"second")],2:[(2,"third"),(3,"third")],3:[(6,"second")],4:[(4,"third"),(5,"third")],5:[(6,"third")]}
    def body(h,_):
        for i in range(n//QB):
            fwd_head(h,i,q_t,k_o,v_t,start,m_t,lse)
        for at,todo in plan.items():
            @pl.when(h==at)
            def _():
                for k,what in todo: getattr(f[k],what)()
        return 0
    lax.fori_loop(0,heads,body,0)
    for p in range(heads//2):
        mixed[:,p*128:p*128+128]=m_t[p].T.astype(bf)
    for x in f: x.finish()
    for x in a+f: x.drain()
    @pl.when(own)
    def _():
        for x in swap_far: x.wait_send()
    @pl.when(jnp.logical_not(own))
    def _():
        for x in put_far: x.wait_send()

def fused_fwd(tok,og,cos,sin,start,a,o,g,u,d,cols):
    n,width=tok.shape; heads=cols//HD; pr=heads//2; ff=g.shape[1]
    V=pl.BlockSpec(memory_space=pltpu.VMEM); A=pl.BlockSpec(memory_space=pl.ANY)
    S=jax.ShapeDtypeStruct
    like=lambda a: S(a.shape,a.dtype)
    wide=lambda a: S((4,2,2)+a.shape,bf)
    dma=lambda k: pltpu.SemaphoreType.DMA((k,))
    return pl.pallas_call(functools.partial(fused_fwd_kernel,n,cols,ff),
      out_shape=[like(tok),like(og),like(cos),like(sin),like(start),wide(a),wide(o),wide(g),wide(u),wide(d),
        S((pr,n,128),bf),S((pr,n,128),bf),S((pr,n,128),bf),S((pr,128,n),f32),S((n,pr*128),bf),S((heads,n),f32),S((width,n),bf),S((3,pr*128,width),bf)],
      in_specs=[A]*10,out_specs=[V]*18,
      scratch_shapes=[pltpu.VMEM((5,pr*128,width),bf),pltpu.VMEM((pr,128,n),bf),pltpu.VMEM((pr,128,n),bf),
        dma(5),dma(5),dma(5),dma(5)]+[dma(5)]*22,
      compiler_params=pltpu.CompilerParams(vmem_limit_bytes=60<<20,collective_id=0,has_side_effects=True),name="attn_fwd_gather")(tok,og,cos,sin,start,a,o,g,u,d)

def fused_bwd_kernel(n,heads,q_s,k_s,v_s,m_t,dm,lse,start,cos,sin,gg,gu,gd,dqkv,t0,t1,t2,t3,t4,t5,q_t,k_t,dm_t,dm_s,dq_t,dk_s,dv_s,dd,*scr):
    z,y,m=place()
    greet(peers(z,y,m))
    half=gg.shape[-1]//2
    two=[t0,t1,t2,t3,t4,t5]
    ch=[]
    for k in range(6):
        src=(gd,gg,gu)[k//2]
        one,s,r=scr[3*k:3*k+3]
        ch.append(Halve(src.at[:,:,:,:,(k%2)*half:(k%2)*half+half],one,two[k],s,r,"yx"[k%2]))
    for x in ch: x.start()
    P_=heads//2
    for p in range(P_):
        q_t[p]=q_s[p].T
        k_t[p]=k_s[p].T
        dm_s[p]=dm[:,p*128:p*128+128]
        dm_t[p]=dm_s[p].T
        for half_ in range(2):
            r=slice(half_*64,half_*64+64)
            dd[2*p+half_:2*p+half_+1,:]=jnp.sum(dm_t[p,r,:].astype(f32)*m_t[p,r,:],0,keepdims=True)
    dk_s[...]=jnp.zeros_like(dk_s); dv_s[...]=jnp.zeros_like(dv_s)
    plan={1:[(0,"second"),(1,"second")],3:[(0,"third"),(1,"third")],4:[(2,"second"),(3,"second")],6:[(2,"third"),(3,"third")],7:[(4,"second"),(5,"second")]}
    def body(h,_):
        for i in range(n//QB):
            bwd_head(h,i,q_t,q_s,k_s,k_t,v_s,dm_t,dm_s,lse,dd,start,dq_t,dk_s,dv_s)
        for at,todo in plan.items():
            @pl.when(h==at)
            def _():
                for k,what in todo: getattr(ch[k],what)()
        return 0
    lax.fori_loop(0,heads,body,0)
    sc=HD**-0.5
    for p in range(P_):
        dqkv[0,:,p*128:p*128+128]=rope_back(dq_t[p].T*sc,cos[...],sin[...]).astype(bf)
        dqkv[1,:,p*128:p*128+128]=rope_back(dk_s[p]*sc,cos[...],sin[...]).astype(bf)
        dqkv[2,:,p*128:p*128+128]=dv_s[p].astype(bf)
    ch[4].third(); ch[5].third()
    for x in ch: x.drain()

def fused_bwd(q_s,k_s,v_s,m_t,dm,lse,start,cos,sin,gg,gu,gd):
    pr,n,_=q_s.shape; heads=2*pr
    V=pl.BlockSpec(memory_space=pltpu.VMEM)
    S=jax.ShapeDtypeStruct
    ff=gg.shape[1]
    cut=lambda a: a.reshape(4,2,2,48,ff)
    return pl.pallas_call(functools.partial(fused_bwd_kernel,n,heads),
      out_shape=[S((3,n,pr*128),bf)]+[S((4,48,ff//2),bf)]*6,
      in_specs=[V]*12,out_specs=[V]*7,
      scratch_shapes=[pltpu.VMEM((pr,128,n),bf),pltpu.VMEM((pr,128,n),bf),pltpu.VMEM((pr,128,n),bf),pltpu.VMEM((pr,n,128),bf),pltpu.VMEM((pr,128,n),f32),pltpu.VMEM((pr,n,128),f32),pltpu.VMEM((pr,n,128),f32),pltpu.VMEM((heads,n),f32)]
        +sum([halve_scratch(ff//2) for _ in range(6)],[]),
      compiler_params=pltpu.CompilerParams(vmem_limit_bytes=60<<20,collective_id=1,has_side_effects=True),name="attn_bwd_reduce")(
        q_s,k_s,v_s,m_t,dm,lse,start,cos,sin,cut(gg),cut(gu),cut(gd))

def tail_kernel(n,cols,dqkv,tok_t,wt,dattn,mixed,d_one,gains,t0,t1,t2,t3,t4,t5,og,ou,od,oa,gtok,ga,term,other,summed,core_s,core_r,far_s,far_r,
        h0,h0s,h0r,h1,h1s,h1r,two0,two1,*scr):
    z,y,m=place(); c=lax.axis_index("c")
    own=c==m
    greet(peers(z,y,m)+both(c,m))
    half=t0.shape[-1]
    ff=[]
    for k,t in enumerate((t0,t1,t2,t3,t4,t5)):
        three,s,r=scr[3*k:3*k+3]
        ff.append(Quarter(t,three,(od,og,ou)[k//2].at[:,(k%2)*half:(k%2)*half+half],s,r))
    for x in ff: x.start()
    w=ga.shape[-1]; mid=2*cols+128
    c0,c1=ga.at[:,:,:,:,0:mid],ga.at[:,:,:,:,mid:w]
    halves=[Halve(c0,h0,two0,h0s,h0r,"y"),Halve(c1,h1,two1,h1s,h1r,"y")]
    quarters=[Quarter(two0,scr[18],oa.at[:,0:mid],scr[19],scr[20]),Quarter(two1,scr[21],oa.at[:,mid:w],scr[22],scr[23])]
    put=spread(cols//HD*64,cols,False)
    width=tok_t.shape[0]; part=width//2
    def pack(val): return val.reshape(2,2,2,48,val.shape[-1])
    for i in range(2):
        zz=slice(2*i,2*i+2); rows=slice(i*part,(i+1)*part)
        ga[zz,:,:,:,0:128]=pack(gains[rows,:])
        ga[zz,:,:,:,128:128+cols]=pack(dot_nt_t(dattn[:,rows].T,mixed[...],put))
        ga[zz,:,:,:,128+cols:128+2*cols]=pack(dot_nt_t(tok_t[rows,:],dqkv[0],put))
    halves[0].start()
    for i in range(2):
        zz=slice(2*i,2*i+2); rows=slice(i*part,(i+1)*part)
        for j in (1,2):
            ga[zz,:,:,:,128+(j+1)*cols:128+(j+2)*cols]=pack(dot_nt_t(tok_t[rows,:],dqkv[j],put))
    halves[1].start()
    nb=n//QB
    def cross(b): return pltpu.make_async_remote_copy(src_ref=term.at[b],dst_ref=other.at[b],send_sem=core_s.at[b],recv_sem=core_r.at[b],device_id={"c":1-c},device_id_type=MESH)
    def far(b): return pltpu.make_async_remote_copy(src_ref=summed.at[b],dst_ref=gtok.at[b],send_sem=far_s.at[b],recv_sem=far_r.at[b],device_id={"c":1-c,"m":1-m},device_id_type=MESH)
    def near(b): return pltpu.make_async_copy(summed.at[b],gtok.at[b],far_r.at[b])
    def make(b,_):
        rows=pl.ds(pl.multiple_of(b*QB,QB),QB)
        t=dot(dqkv[0,rows,:],wt[0])+dot(dqkv[1,rows,:],wt[1])+dot(dqkv[2,rows,:],wt[2])
        term[b]=t.astype(bf)
        cross(b).start()
        return 0
    lax.fori_loop(0,nb,make,0)
    def total(b,_):
        rows=pl.ds(pl.multiple_of(b*QB,QB),QB)
        cross(b).wait_recv()
        summed[b]=(d_one[rows,:]+(term[b].astype(f32)+other[b].astype(f32))).astype(bf)
        @pl.when(own)
        def _():
            near(b).start()
        @pl.when(jnp.logical_not(own))
        def _():
            far(b).start()
        return 0
    lax.fori_loop(0,nb,total,0)
    halves[0].second()
    for x in ff[:2]: x.finish()
    halves[1].second()
    for x in ff[2:]: x.finish()
    halves[0].third(); quarters[0].start()
    halves[1].third(); quarters[1].start()
    quarters[0].finish(); quarters[1].finish()
    for x in ff+halves+quarters: x.drain()
    def drain(b,_):
        cross(b).wait_send()
        @pl.when(own)
        def _():
            near(b).wait()
        @pl.when(jnp.logical_not(own))
        def _():
            far(b).wait_recv()
            far(b).wait_send()
        return 0
    lax.fori_loop(0,nb,drain,0)

def dot_nt_t(a,b,put):
    return dot(dot(a,b).astype(bf),put).astype(bf)

def tail(dqkv,tok_t,wt,dattn,mixed,d_one,gains,twos,cols):
    n,width=dattn.shape; ff=2*twos[0].shape[-1]; w=4*cols+128; mid=2*cols+128
    V=pl.BlockSpec(memory_space=pltpu.VMEM); A=pl.BlockSpec(memory_space=pl.ANY)
    S=jax.ShapeDtypeStruct
    blocks=(n//QB,QB,width)
    dma=lambda k: pltpu.SemaphoreType.DMA((k,))
    half=lambda k: [pltpu.VMEM((4,2,48,k),bf),dma(2),dma(2)]
    return pl.pallas_call(functools.partial(tail_kernel,n,cols),
      out_shape=[S((48,ff),bf)]*3+[S((48,w),bf),S(blocks,bf)],
      in_specs=[V]*13,out_specs=[V]*4+[A],
      scratch_shapes=[pltpu.VMEM((4,2,2,48,w),bf),pltpu.VMEM(blocks,bf),pltpu.VMEM(blocks,bf),pltpu.VMEM(blocks,bf)]+[dma(n//QB)]*4
        +halve_scratch(mid)+halve_scratch(w-mid)+[pltpu.VMEM((4,48,mid),bf),pltpu.VMEM((4,48,w-mid),bf)]
        +sum([quarter_scratch(ff//2) for _ in range(6)],[])+quarter_scratch(mid)+quarter_scratch(w-mid),
      compiler_params=pltpu.CompilerParams(vmem_limit_bytes=60<<20,collective_id=2,has_side_effects=True),name="token_grad_reduce")(
        dqkv,tok_t,wt,dattn,mixed,d_one,gains,*twos)

NORM_EPS=1e-05
DIAG=[(0,0),(3,3),(1,2),(2,1)]
CORE=[(0,1),(1,0)]

def rms_forward(resid):
    inverse=lax.rsqrt(jnp.mean(resid*resid,-1,keepdims=True)+NORM_EPS)
    return (resid*inverse,inverse)

def rms_backward(grad_normed,normed,inverse):
    return inverse*(grad_normed-normed*jnp.mean(grad_normed*normed,-1,keepdims=True))

def doc_starts(lengths,n):
    at=jnp.arange(n,dtype=jnp.int32); start=jnp.zeros((n,),jnp.int32); end=jnp.int32(0)
    for i in range(lengths.shape[0]-1):
        end=end+lengths[i]
        start=jnp.where(at>=end,end,start)
    return start

def rope_tables(positions):
    half=HD//2
    fr=jnp.exp(jnp.arange(half,dtype=f32)*(-2.0*math.log(10000.0)/HD))
    a=positions.astype(f32)[:,None]*fr[None,:]
    c,s=jnp.cos(a),jnp.sin(a); z=jnp.zeros((positions.shape[0],64-HD),f32)
    return jnp.concatenate([c,c,z,c,c,z],1),jnp.concatenate([s,s,z,s,s,z],1)

def core_sum(part):
    return part.astype(f32)+lax.ppermute(part,"c",CORE).astype(f32)

def on_device(tokens,out_grad,doc_lengths,w_query,w_key,w_value,w_out,gain_one,w_gate,w_up,w_down,gain_two):
    cols=w_query.shape[1]; ff=w_gate.shape[1]; n,width=tokens.shape
    quad=lax.axis_size("q")==8 and w_query.shape[0]==48
    if not quad:
        own=lax.axis_index("c")==lax.axis_index("m")
        pick=lambda a: jnp.where(own,a,lax.ppermute(a,"c",CORE))
        tokens,out_grad,doc_lengths=pick(tokens),pick(out_grad),pick(doc_lengths)
    start=doc_starts(doc_lengths[0],n)
    cos,sin=rope_tables(jnp.arange(n,dtype=jnp.int32)-start)
    start=start[None]
    cast=lambda a: a.astype(bf)
    gains=jnp.pad(jnp.stack([cast(gain_one),cast(gain_two)],1),((0,0),(0,126)))
    apack=jnp.concatenate([cast(w_query),cast(w_key),cast(w_value),gains],1)
    def gather(a):
        return lax.all_gather(lax.ppermute(a,("c","m"),DIAG),("q","m"),axis=0,tiled=True)
    if quad:
        tokens,out_grad,cos,sin,start,afull,ofull,gate_w,up_w,down_t,q,k,v,m_t,mixed,lse,tok_t,wt=fused_fwd(
            tokens,out_grad,cos,sin,start,apack,cast(w_out).T,cast(w_gate),cast(w_up),cast(w_down).T,cols)
        afull,ofull,gate_w,up_w,down_t=[a.reshape(width,a.shape[-1]) for a in (afull,ofull,gate_w,up_w,down_t)]
    else:
        afull,ofull,gate_w,up_w,down_t=[gather(a) for a in (apack,cast(w_out).T,cast(w_gate),cast(w_up),cast(w_down).T)]
        q,k,v,m_t,mixed,lse=attn_fwd(tokens,afull[:,:3*cols],cos,sin,start)
    hp=cols//HD*64
    put=spread(hp,cols,False)
    out_t=dot_nt(ofull,put).astype(bf)
    gain_a=afull[:,3*cols].astype(f32); gain_b=afull[:,3*cols+1].astype(f32)
    attn=core_sum(dot_nt(mixed,out_t).astype(bf))
    normed_one,inv_one=rms_forward(tokens.astype(f32)+attn)
    hidden=normed_one*gain_a
    hb=hidden.astype(bf)
    gate=dot(hb,gate_w); up=dot(hb,up_w)
    sg=jax.nn.sigmoid(gate)
    act=(gate*sg*up).astype(bf)
    ffn=core_sum(dot_nt(act,down_t).astype(bf))
    normed_two,inv_two=rms_forward(hidden+ffn)
    output=(normed_two*gain_b).astype(bf)
    g=out_grad.astype(f32)
    g_gain_two=jnp.sum(g*normed_two,0)
    d_two=rms_backward(g*gain_b,normed_two,inv_two)
    d_ffn=d_two.astype(bf)
    tn=lambda a,b: lax.dot_general(a,b,(((0,),(0,)),((),())),preferred_element_type=f32)
    d_act=dot(d_ffn,down_t)
    d_up=(d_act*gate*sg).astype(bf)
    d_gate=(d_act*up*sg*(1.0+gate*(1.0-sg))).astype(bf)
    hterm=(dot_nt(d_gate,gate_w)+dot_nt(d_up,up_w)).astype(bf)
    gff=[tn(hb,d_gate).astype(bf),tn(hb,d_up).astype(bf),tn(d_ffn,act).astype(bf)]
    d_hidden=d_two+core_sum(hterm)
    g_gain_one=jnp.sum(d_hidden*normed_one,0)
    d_one=rms_backward(d_hidden*gain_a,normed_one,inv_one)
    d_attn=d_one.astype(bf)
    dm=dot(d_attn,out_t).astype(bf)
    ggain=jnp.pad(jnp.stack([g_gain_one,g_gain_two],1),((0,0),(0,126))).astype(bf)
    own=lax.axis_index("c")==lax.axis_index("m")
    output=jnp.where(own,output,lax.ppermute(output,("c","m"),[(1,2),(2,1)]))
    if quad:
        dqkv,*twos=fused_bwd(q,k,v,m_t,dm,lse,start,cos,sin,*gff)
        *sff,sat,gtok=tail(dqkv,tok_t,wt,d_attn,mixed,d_one,ggain,twos,cols)
        gtok=gtok.reshape(n,width).astype(f32)
    else:
        dqkv=attn_bwd(q,k,v,m_t,dm,lse,start,cos,sin)
        term=0.0; gqkv=[]
        for j in range(3):
            wp=dot_nt(afull[:,j*cols:(j+1)*cols],put).astype(bf)
            term=term+dot_nt(dqkv[j],wp)
            gqkv.append(dot(tn(tokens,dqkv[j]).astype(bf),put).astype(bf))
        gtok=(d_one+core_sum(term.astype(bf))).astype(bf)
        gtok=lax.ppermute(gtok,("c","m"),DIAG).astype(f32)
        g_out=dot(tn(d_attn,mixed).astype(bf),put).astype(bf)
        gatt=jnp.concatenate([ggain,g_out]+gqkv,1)
        add=lambda a: lax.psum_scatter(a,("q","m"),scatter_dimension=0,tiled=True)
        sff,sat=[add(a) for a in gff],add(gatt)
    sff,sat=lax.ppermute(jnp.concatenate(sff,1),("c","m"),DIAG).astype(f32),lax.ppermute(sat,("c","m"),DIAG).astype(f32)
    piece=lambda j: sat[:,128+j*cols:128+(j+1)*cols]
    return (output,gtok,piece(1),piece(2),piece(3),piece(0).T,sat[:,0],sff[:,:ff],sff[:,ff:2*ff],sff[:,2*ff:].T,sat[:,1])

def solution(mesh):
    dp,mp=mesh.shape["dp"],mesh.shape["mp"]
    fine=Mesh(mesh.devices.reshape(dp//2,2,mp),("q","c","m"))
    d=("q","c")
    rows,cols_=P(d,"m"),P("m",d)
    return jax.shard_map(on_device,mesh=fine,
        in_specs=(P(d,None),P(d,None),P(d,None),rows,rows,rows,cols_,P(d),rows,rows,cols_,P(d)),
        out_specs=(P(d,None),P(d,None),rows,rows,rows,cols_,P(d),rows,rows,cols_,P(d)),check_vma=False)
```

```python
import functools
import math
import jax, jax.numpy as jnp
from jax import lax
from jax.experimental import pallas as pl
from jax.experimental.pallas import tpu as pltpu
from jax.sharding import Mesh, PartitionSpec as P
MESH=pl.DeviceIdType.MESH
HD=48
C2=HD**-0.5*math.log2(math.e)
NEG=-1e30
bf=jnp.bfloat16; f32=jnp.float32
QB=256; LOOK=4
NT=(((1,),(1,)),((),()))
def dot(a,b): return jnp.dot(a,b,preferred_element_type=f32)
def dot_nt(a,b): return lax.dot_general(a,b,NT,preferred_element_type=f32)

def spread(rows, cols, rot):
    r=lax.broadcasted_iota(jnp.int32,(rows,cols),0); c=lax.broadcasted_iota(jnp.int32,(rows,cols),1)
    h=r//64; d=r-h*64
    if not rot:
        return jnp.where((d<HD)&(c==h*HD+d),1.0,0.0).astype(bf)
    lo=(d<24)&(c==h*HD+d+24); hi=(d>=24)&(d<HD)&(c==h*HD+d-24)
    return jnp.where(lo,-1.0,jnp.where(hi,1.0,0.0)).astype(bf)

def proj(tok,w,cos,sin,wq_s,q_s,k_s,v_s,n,cols):
    hp=cols//HD*64
    pairs=hp//128
    for m,(col,rot) in enumerate(((0,False),(0,True),(1,False),(1,True),(2,False))):
        if len(w.shape)==2:
            part=w[:,col*cols:(col+1)*cols]
        else:
            part=w[:,:,:,:,col*cols:(col+1)*cols].reshape(-1,cols)
        wq_s[m]=dot_nt(spread(hp,cols,rot),part).astype(bf)
    def body(b,_):
        rows=pl.ds(pl.multiple_of(b*QB,QB),QB)
        x=tok[rows,:]
        cs=cos[rows,:]; sn=sin[rows,:]
        for dst,a in ((q_s,0),(k_s,2)):
            raw=dot_nt(x,wq_s[a]); rt=dot_nt(x,wq_s[a+1])
            for p in range(pairs):
                l=slice(p*128,p*128+128)
                dst[p,rows,:]=(raw[:,l]*cs+rt[:,l]*sn).astype(bf)
        raw=dot_nt(x,wq_s[4])
        for p in range(pairs):
            v_s[p,rows,:]=raw[:,p*128:p*128+128].astype(bf)
        return 0
    lax.fori_loop(0,n//QB,body,0)

def masks(kk0,nk,i,start):
    kidx=lax.broadcasted_iota(jnp.int32,(nk,QB),0)+kk0
    ok=kidx>=start
    qidx=lax.broadcasted_iota(jnp.int32,(nk,QB),1)+i*QB
    return ok&(kidx<=qidx)

def fwd_head(h,i,q_t,k_s,v_t,start,m_t,lse):
    p=h//2; half=h-2*p
    lo=max(0,i-LOOK)*QB; nk=(i+1)*QB-lo
    kk=slice(lo,lo+nk); qq=slice(i*QB,(i+1)*QB)
    row=lax.broadcasted_iota(jnp.int32,(128,QB),0)
    mine=(row>=half*64)&(row<half*64+64)
    qt=jnp.where(mine,q_t[p,:,qq],jnp.zeros((),bf))
    s=dot(k_s[p,kk,:],qt)
    st=start[:,qq]
    s=jnp.where(masks(lo,nk,i,st),s,NEG)
    m=jnp.max(s,0,keepdims=True)
    e=jnp.exp2((s-m)*C2)
    l=jnp.sum(e,0,keepdims=True)
    pr=(e*(1.0/l)).astype(bf)
    rows=pl.ds(pl.multiple_of(half*64,64),64)
    m_t[p,rows,qq]=dot(v_t[p,rows,kk],pr)
    lse[pl.ds(h,1),qq]=m*C2+jnp.log2(l)

def fwd_kernel(n,cols,tok,w,cos,sin,start,q_o,k_o,v_o,m_t,mixed,lse,wq_s,q_t,v_t):
    proj(tok,w,cos,sin,wq_s,q_o,k_o,v_o,n,cols)
    heads=cols//HD
    for p in range(heads//2):
        q_t[p]=q_o[p].T
        v_t[p]=v_o[p].T
    def body(h,_):
        for i in range(n//QB):
            fwd_head(h,i,q_t,k_o,v_t,start,m_t,lse)
        return 0
    lax.fori_loop(0,heads,body,0)
    for p in range(heads//2):
        mixed[:,p*128:p*128+128]=m_t[p].T.astype(bf)

def attn_fwd(tok,w,cos,sin,start):
    n=tok.shape[0]; cols=w.shape[1]//3; heads=cols//HD; P=heads//2
    V=pl.BlockSpec(memory_space=pltpu.VMEM)
    S=jax.ShapeDtypeStruct
    return pl.pallas_call(functools.partial(fwd_kernel,n,cols),
      out_shape=(S((P,n,128),bf),S((P,n,128),bf),S((P,n,128),bf),S((P,128,n),f32),S((n,P*128),bf),S((heads,n),f32)),
      in_specs=[V]*5,out_specs=[V]*6,
      scratch_shapes=[pltpu.VMEM((5,P*128,w.shape[0]),bf),pltpu.VMEM((P,128,n),bf),pltpu.VMEM((P,128,n),bf)],
      compiler_params=pltpu.CompilerParams(vmem_limit_bytes=60<<20),name="attn_fwd")(tok,w,cos,sin,start)

def bwd_head(h,i,q_t,q_s,k_s,k_t,v_s,dm_t,dm_s,lse,dd,start,dq_t,dk_s,dv_s):
    p=h//2; half=h-2*p
    lo=max(0,i-LOOK)*QB; nk=(i+1)*QB-lo
    kk=slice(lo,lo+nk); qq=slice(i*QB,(i+1)*QB)
    row=lax.broadcasted_iota(jnp.int32,(128,QB),0)
    mine=(row>=half*64)&(row<half*64+64)
    lane=lax.broadcasted_iota(jnp.int32,(QB,128),1)
    mlane=(lane>=half*64)&(lane<half*64+64)
    zero=jnp.zeros((),bf)
    qt=jnp.where(mine,q_t[p,:,qq],zero)
    dmt=jnp.where(mine,dm_t[p,:,qq],zero)
    qn=jnp.where(mlane,q_s[p,qq,:],zero)
    dmn=jnp.where(mlane,dm_s[p,qq,:],zero)
    s=dot(k_s[p,kk,:],qt)
    st=start[:,qq]
    pr=jnp.exp2(jnp.where(masks(lo,nk,i,st),s*C2,NEG)-lse[pl.ds(h,1),qq])
    dp=dot(v_s[p,kk,:],dmt)
    ds=(pr*(dp-dd[pl.ds(h,1),qq])).astype(bf)
    pb=pr.astype(bf)
    dv_s[p,kk,:]+=dot(pb,dmn)
    dk_s[p,kk,:]+=dot(ds,qn)
    rows=pl.ds(pl.multiple_of(half*64,64),64)
    dq_t[p,rows,qq]=dot(k_t[p,rows,kk],ds)

def rope_back(u,cs,sn):
    w=u*sn
    lane=lax.broadcasted_iota(jnp.int32,u.shape,1)&63
    up=pltpu.roll(w,128-24,axis=1); dn=pltpu.roll(w,24,axis=1)
    return u*cs+jnp.where(lane<24,up,jnp.where(lane<48,-dn,0.0))

def bwd_kernel(n,heads,q_s,k_s,v_s,m_t,dm,lse,start,cos,sin,dqkv,q_t,k_t,dm_t,dm_s,dq_t,dk_s,dv_s,dd):
    P=heads//2
    for p in range(P):
        q_t[p]=q_s[p].T
        k_t[p]=k_s[p].T
        dm_s[p]=dm[:,p*128:p*128+128]
        dm_t[p]=dm_s[p].T
        for half in range(2):
            r=slice(half*64,half*64+64)
            dd[2*p+half:2*p+half+1,:]=jnp.sum(dm_t[p,r,:].astype(f32)*m_t[p,r,:],0,keepdims=True)
    dk_s[...]=jnp.zeros_like(dk_s); dv_s[...]=jnp.zeros_like(dv_s)
    def body(h,_):
        for i in range(n//QB):
            bwd_head(h,i,q_t,q_s,k_s,k_t,v_s,dm_t,dm_s,lse,dd,start,dq_t,dk_s,dv_s)
        return 0
    lax.fori_loop(0,heads,body,0)
    sc=HD**-0.5
    for p in range(P):
        dqkv[0,:,p*128:p*128+128]=rope_back(dq_t[p].T*sc,cos[...],sin[...]).astype(bf)
        dqkv[1,:,p*128:p*128+128]=rope_back(dk_s[p]*sc,cos[...],sin[...]).astype(bf)
        dqkv[2,:,p*128:p*128+128]=dv_s[p].astype(bf)

def attn_bwd(q_s,k_s,v_s,m_t,dm,lse,start,cos,sin):
    P,n,_=q_s.shape; heads=2*P
    V=pl.BlockSpec(memory_space=pltpu.VMEM)
    S=jax.ShapeDtypeStruct
    return pl.pallas_call(functools.partial(bwd_kernel,n,heads),
      out_shape=S((3,n,P*128),bf),
      in_specs=[V]*9,out_specs=V,
      scratch_shapes=[pltpu.VMEM((P,128,n),bf),pltpu.VMEM((P,128,n),bf),pltpu.VMEM((P,128,n),bf),pltpu.VMEM((P,n,128),bf),pltpu.VMEM((P,128,n),f32),pltpu.VMEM((P,n,128),f32),pltpu.VMEM((P,n,128),f32),pltpu.VMEM((heads,n),f32)],
      compiler_params=pltpu.CompilerParams(vmem_limit_bytes=60<<20),name="attn_bwd")(q_s,k_s,v_s,m_t,dm,lse,start,cos,sin)


def place():
    q,m=lax.axis_index("q"),lax.axis_index("m")
    return q//2,lax.rem(q,2),m

def peers(z,y,m):
    return [{"q":z*2+1-y},{"m":1-m}]+[{"q":lax.rem(z+s,4)*2+y} for s in (1,2,3)]

def greet(where):
    barrier=pltpu.get_barrier_semaphore()
    for w in where:
        pl.semaphore_signal(barrier,inc=1,device_id=w,device_id_type=MESH)
    pl.semaphore_wait(barrier,len(where))

def remote(s,d,ss,rs,w):
    return pltpu.make_async_remote_copy(src_ref=s,dst_ref=d,send_sem=ss,recv_sem=rs,device_id=w,device_id_type=MESH)

class First:
    def __init__(self,source,one,sem,first="y"):
        self.source,self.one,self.first=source,one,first
        z,y,m=place()
        self.y,self.m=y,m
        ny,nx=peers(z,y,m)[:2]
        self.copy=remote(source.at[:,1-y],one,sem.at[0],sem.at[1],ny) if first=="y" else remote(source.at[:,:,1-m],one,sem.at[0],sem.at[1],nx)
    def start(self): self.copy.start()
    def finish(self):
        self.copy.wait_recv()
        def add(i,_):
            zz=i//2; o=i-zz*2
            mine=self.source[zz,self.y,o] if self.first=="y" else self.source[zz,o,self.m]
            self.one[zz,o]=(self.one[zz,o].astype(f32)+mine.astype(f32)).astype(bf)
            return 0
        lax.fori_loop(0,8,add,0)
    def drain(self): self.copy.wait_send()

class Second:
    def __init__(self,one,two,sem,first="y"):
        self.one,self.two=one,two
        z,y,m=place()
        ny,nx=peers(z,y,m)[:2]
        self.keep=m if first=="y" else y
        self.copy=remote(one.at[:,1-self.keep],two,sem.at[0],sem.at[1],nx if first=="y" else ny)
    def start(self): self.copy.start()
    def finish(self):
        self.copy.wait_recv()
        def add(zz,_):
            self.two[zz]=(self.two[zz].astype(f32)+self.one[zz,self.keep].astype(f32)).astype(bf)
            return 0
        lax.fori_loop(0,4,add,0)
    def drain(self): self.copy.wait_send()

class Third:
    def __init__(self,two,three,out,send,recv):
        self.two,self.three,self.out=two,three,out
        z,y,m=place()
        self.z=z
        to=peers(z,y,m)
        self.copies=[remote(two.at[lax.rem(z+s,4)],three.at[s-1],send.at[s-1],recv.at[s-1],to[1+s]) for s in (1,2,3)]
    def start(self):
        for c in self.copies: c.start()
    def finish(self):
        for c in self.copies: c.wait_recv()
        t=self.two[self.z].astype(f32)
        for s in range(3): t=t+self.three[s].astype(f32)
        self.out[...]=t.astype(bf)
    def drain(self):
        for c in self.copies: c.wait_send()

class Gather:
    def __init__(self,full,cols,send,recv,first):
        z,y,m=place()
        to=peers(z,y,m)
        a,b=(0,1) if first=="y" else (1,0)
        def copy(at,k,w):
            return pltpu.make_async_remote_copy(src_ref=at,dst_ref=at,send_sem=send.at[k],recv_sem=recv.at[k],device_id=w,device_id_type=MESH)
        self.along=[copy(full.at[z,y,m,:,cols],s-1,to[1+s]) for s in (1,2,3)]
        self.c2=copy(full.at[:,y,m,:,cols],3,to[a])
        self.c3=copy(full.at[:,:,m,:,cols] if first=="y" else full.at[:,y,:,:,cols],4,to[b])
    def start(self):
        for c in self.along: c.start()
    def second(self):
        for c in self.along: c.wait_recv()
        self.c2.start()
    def third(self):
        self.c2.wait_recv()
        self.c3.start()
    def finish(self):
        self.c3.wait_recv()
    def drain(self):
        for c in self.along: c.wait_send()
        self.c2.wait_send(); self.c3.wait_send()

def both(c,m):
    return [{"c":1-c},{"c":1-c,"m":1-m}]

def fused_fwd_kernel(n,cols,ff,tok_i,cos_i,sin_i,start_i,a_i,o_i,g_i,u_i,d_i,
        tok,cos,sin,start,wa,wo,wg,wu,wd,q_o,k_o,v_o,m_t,mixed,lse,tok_t,wt,
        wq_s,q_t,v_t,swap_s,swap_r,put_s,put_r,*sems):
    z,y,m=place(); c=lax.axis_index("c")
    own=c==m
    greet(peers(z,y,m)+both(c,m))
    def remote(s,d,ss,rs,w):
        return pltpu.make_async_remote_copy(src_ref=s,dst_ref=d,send_sem=ss,recv_sem=rs,device_id=w,device_id_type=MESH)
    diag={"c":1-c,"m":1-m}
    shards=[(a_i,wa),(g_i,wg),(u_i,wu),(d_i,wd),(o_i,wo)]
    put_far=[remote(s,d.at[z,y,c],put_s.at[i],put_r.at[i],diag) for i,(s,d) in enumerate(shards)]
    put_near=[pltpu.make_async_copy(s,d.at[z,y,c],put_r.at[i]) for i,(s,d) in enumerate(shards)]
    packs=[(tok_i,tok),(cos_i,cos),(sin_i,sin),(start_i,start)]
    swap_far=[remote(s,d,swap_s.at[i],swap_r.at[i],{"c":1-c}) for i,(s,d) in enumerate(packs)]
    swap_near=[pltpu.make_async_copy(s,d,swap_r.at[i]) for i,(s,d) in enumerate(packs)]
    @pl.when(own)
    def _():
        for x in put_near: x.start()
        for a,b in zip(swap_near,swap_far):
            a.start(); b.start()
        put_near[0].wait()
    @pl.when(jnp.logical_not(own))
    def _():
        for x in put_far: x.start()
        put_far[0].wait_recv()
    def ga(full,lo,hi,k,first): return Gather(full,slice(lo,hi),sems[2*k],sems[2*k+1],first)
    ac=wa.shape[-1]; cut=[0,ac//1280*256,ac//2,ac//2+ac//1280*384,ac]
    a=[ga(wa,cut[i],cut[i+1],i,"xy"[i%2]) for i in range(4)]
    h2=ff//2
    f=[ga(w,j*h2,j*h2+h2,4+2*i+j,"xy"[j]) for i,w in enumerate((wg,wu,wd)) for j in range(2)]
    f.append(ga(wo,0,wo.shape[-1],10,"x"))
    for x in a: x.start()
    @pl.when(own)
    def _():
        for x in put_near[1:]: x.wait()
    @pl.when(jnp.logical_not(own))
    def _():
        for x in put_far[1:]: x.wait_recv()
    a[0].second(); a[1].second()
    for x in f: x.start()
    @pl.when(own)
    def _():
        for x in swap_near: x.wait()
    @pl.when(jnp.logical_not(own))
    def _():
        for x in swap_far: x.wait_recv()
    a[0].third(); a[1].third()
    a[2].second(); a[3].second()
    tok_t[:tok_t.shape[0]//2,:]=tok[:,:tok_t.shape[0]//2].T
    a[2].third(); a[3].third()
    tok_t[tok_t.shape[0]//2:,:]=tok[:,tok_t.shape[0]//2:].T
    for x in a: x.finish()
    f[0].second(); f[1].second()
    proj(tok,wa,cos,sin,wq_s,q_o,k_o,v_o,n,cols)
    f[0].third(); f[1].third()
    f[2].second(); f[3].second()
    for j in range(3): wt[j]=wq_s[2*j]
    heads=cols//HD
    for p in range(heads//2):
        q_t[p]=q_o[p].T
        v_t[p]=v_o[p].T
    plan={1:[(4,"second"),(5,"second")],2:[(2,"third"),(3,"third")],3:[(6,"second")],4:[(4,"third"),(5,"third")],5:[(6,"third")]}
    def body(h,_):
        for i in range(n//QB):
            fwd_head(h,i,q_t,k_o,v_t,start,m_t,lse)
        for at,todo in plan.items():
            @pl.when(h==at)
            def _():
                for k,what in todo: getattr(f[k],what)()
        return 0
    lax.fori_loop(0,heads,body,0)
    for p in range(heads//2):
        mixed[:,p*128:p*128+128]=m_t[p].T.astype(bf)
    for x in f: x.finish()
    for x in a+f: x.drain()
    @pl.when(own)
    def _():
        for x in swap_far: x.wait_send()
    @pl.when(jnp.logical_not(own))
    def _():
        for x in put_far: x.wait_send()

def fused_fwd(tok,cos,sin,start,a,o,g,u,d,cols):
    n,width=tok.shape; heads=cols//HD; pr=heads//2; ff=g.shape[1]
    V=pl.BlockSpec(memory_space=pltpu.VMEM); A=pl.BlockSpec(memory_space=pl.ANY)
    S=jax.ShapeDtypeStruct
    like=lambda a: S(a.shape,a.dtype)
    wide=lambda a: S((4,2,2)+a.shape,bf)
    dma=lambda k: pltpu.SemaphoreType.DMA((k,))
    return pl.pallas_call(functools.partial(fused_fwd_kernel,n,cols,ff),
      out_shape=[like(tok),like(cos),like(sin),like(start),wide(a),wide(o),wide(g),wide(u),wide(d),
        S((pr,n,128),bf),S((pr,n,128),bf),S((pr,n,128),bf),S((pr,128,n),f32),S((n,pr*128),bf),S((heads,n),f32),S((width,n),bf),S((3,pr*128,width),bf)],
      in_specs=[A]*9,out_specs=[V]*17,
      scratch_shapes=[pltpu.VMEM((5,pr*128,width),bf),pltpu.VMEM((pr,128,n),bf),pltpu.VMEM((pr,128,n),bf),
        dma(4),dma(4),dma(5),dma(5)]+[dma(5)]*22,
      compiler_params=pltpu.CompilerParams(vmem_limit_bytes=60<<20,collective_id=0,has_side_effects=True),name="attn_fwd_gather")(tok,cos,sin,start,a,o,g,u,d)

def fused_bwd_kernel(n,cols,q_s,k_s,v_s,dm,lse,start,cos,sin,d0,d1,m_i,g_i,u_i,o_i,tok_i,wt_i,d_one,od,og,ou,oo,oh0,oh1,gtok,
        q_t,k_t,dm_t,dq_t,dk_s,dv_s,dd,dqkv,gg,gu,gow,tok_t,wt,d_buf,ga0,ga1,term,other,summed,load_s,d_sem,core_s,core_r,far_s,far_r,fin_s,fin_r,*scr):
    z,y,m=place(); c=lax.axis_index("c")
    own=c==m
    diag={"c":1-c,"m":1-m}
    loads=[pltpu.make_async_copy(a,b,load_s.at[i]) for i,(a,b) in enumerate(((m_i,dq_t),(g_i,gg),(u_i,gu),(o_i,gow),(tok_i,tok_t),(wt_i,wt)))]
    for x in loads: x.start()
    greet(peers(z,y,m)+both(c,m))
    scr=list(scr)
    def take(k):
        got=scr[:k]
        del scr[:k]
        return got
    half=gg.shape[-1]//2
    srcs=[(g_i,gg,0,"y"),(g_i,gg,half,"x"),(u_i,gu,0,"y"),(u_i,gu,half,"y")]
    firsts,seconds,thirds,lasts={},{},{},{}
    for name,k in (("g0",0),("g1",1),("u0",2),("u1",3)):
        _,own_ref,lo,first=srcs[k]
        one,sem=take(2)
        firsts[name]=First(own_ref.at[:,:,:,:,lo:lo+half],one,sem,first)
        two,sem=take(2)
        seconds[name]=Second(one,two,sem,first)
    for name,src in (("o",gow),("h0",ga0),("h1",ga1)):
        one,sem=take(2)
        firsts[name]=First(src,one,sem)
        two,sem=take(2)
        seconds[name]=Second(one,two,sem)
    for name,one in (("d0",d0),("d1",d1)):
        two,sem=take(2)
        seconds[name]=Second(one,two,sem)
    fd,fg,fu,fo,fh0,fh1=take(6)
    outs={"d0":fd.at[:,0:half],"d1":fd.at[:,half:2*half],"g0":fg.at[:,0:half],"g1":fg.at[:,half:2*half],"u0":fu.at[:,0:half],"u1":fu.at[:,half:2*half],
        "o":fo,"h0":fh0,"h1":fh1}
    for name,out in outs.items():
        three,ss,rs=take(3)
        thirds[name]=Third(seconds[name].two,three,out,ss,rs)
    pairs={"d":(fd,od),"g":(fg,og),"u":(fu,ou),"o":(fo,oo),"h0":(fh0,oh0),"h1":(fh1,oh1)}
    finals={k:remote(a,b,fin_s.at[i],fin_r.at[i],diag) for i,(k,(a,b)) in enumerate(pairs.items())}
    def give(*names):
        @pl.when(own)
        def _():
            for k in names: pairs[k][1][...]=pairs[k][0][...]
        @pl.when(jnp.logical_not(own))
        def _():
            for k in names: finals[k].start()
    def run(*steps):
        for group,what,names in steps:
            for k in names.split(): getattr(group[k],what)()
    run((seconds,"start","d0 d1"))
    loads[1].wait(); loads[2].wait()
    run((firsts,"start","g0 u0 g1 u1"))
    heads=cols//HD; P_=heads//2
    for p in range(P_):
        q_t[p]=q_s[p].T
        k_t[p]=k_s[p].T
        dm_t[p]=dm[p].T
    loads[0].wait()
    for p in range(P_):
        for half_ in range(2):
            r=slice(half_*64,half_*64+64)
            dd[2*p+half_:2*p+half_+1,:]=jnp.sum(dm_t[p,r,:].astype(f32)*dq_t[p,r,:],0,keepdims=True)
    dk_s[...]=jnp.zeros_like(dk_s); dv_s[...]=jnp.zeros_like(dv_s)
    loads[3].wait(); loads[4].wait(); loads[5].wait()
    sc=HD**-0.5
    width=tok_t.shape[0]; quarter=width//4; hp=P_*128; part=hp//2
    def raw_grads(half_):
        for p in range(half_*P_//2,(half_+1)*P_//2):
            dqkv[0,:,p*128:p*128+128]=rope_back(dq_t[p].T*sc,cos[...],sin[...]).astype(bf)
            dqkv[1,:,p*128:p*128+128]=rope_back(dk_s[p]*sc,cos[...],sin[...]).astype(bf)
            dqkv[2,:,p*128:p*128+128]=dv_s[p].astype(bf)
    def weight_grads(half_):
        ga=(ga0,ga1)[half_]
        w=ga.shape[-1]; hc=cols//2
        maps=[]
        for j in range(3):
            rr=lax.broadcasted_iota(jnp.int32,(part,w),0); cc=lax.broadcasted_iota(jnp.int32,(part,w),1)
            hh=rr//64; dd_=rr-hh*64
            maps.append(jnp.where((dd_<HD)&(cc==j*hc+hh*HD+dd_),1.0,0.0).astype(bf))
        def body(i,_):
            r=pl.ds(pl.multiple_of(i*quarter,quarter),quarter)
            t=0.0
            for j in range(3):
                t=t+dot(dot(tok_t[r,:],dqkv[j,:,half_*part:(half_+1)*part]).astype(bf),maps[j])
            ga[i]=t.astype(bf).reshape(2,2,quarter//4,w)
            return 0
        lax.fori_loop(0,4,body,0)
    def middle():
        raw_grads(0)
        weight_grads(0)
    events={1:[lambda: run((seconds,"finish","d0 d1"),(thirds,"start","d0 d1"),(firsts,"finish","g0"),(seconds,"start","g0"))],
        3:[lambda: run((firsts,"finish","u0 g1"),(seconds,"start","u0 g1"),(firsts,"start","o")),middle,lambda: run((firsts,"start","h0"))],
        4:[lambda: run((thirds,"finish","d0 d1")),lambda: give("d"),lambda: run((seconds,"finish","g0"),(thirds,"start","g0"))],
        5:[lambda: run((firsts,"finish","u1"),(seconds,"start","u1"),(seconds,"finish","u0"),(thirds,"start","u0"))],
        6:[lambda: run((seconds,"finish","g1"),(thirds,"start","g1"))]}
    def body(h,_):
        for i in range(n//QB):
            bwd_head(h,i,q_t,q_s,k_s,k_t,v_s,dm_t,dm,lse,dd,start,dq_t,dk_s,dv_s)
        for at,calls in events.items():
            @pl.when(h==at)
            def _():
                for call in calls: call()
        return 0
    lax.fori_loop(0,heads,body,0)
    raw_grads(1)
    nb=n//QB
    def cross(b): return remote(term.at[b],other.at[b],core_s.at[b],core_r.at[b],{"c":1-c})
    def far(b): return remote(summed.at[b],gtok.at[b],far_s.at[b],far_r.at[b],diag)
    def near(b): return pltpu.make_async_copy(summed.at[b],gtok.at[b],far_r.at[b])
    def fetch(b): return pltpu.make_async_copy(d_one.at[b],d_buf.at[lax.rem(b,2)],d_sem.at[lax.rem(b,2)])
    fetch(0).start(); fetch(1).start()
    def make(b,_):
        rows=pl.ds(pl.multiple_of(b*QB,QB),QB)
        t=dot(dqkv[0,rows,:],wt[0])+dot(dqkv[1,rows,:],wt[1])+dot(dqkv[2,rows,:],wt[2])
        term[b]=t.astype(bf)
        cross(b).start()
        return 0
    lax.fori_loop(0,nb,make,0)
    run((seconds,"finish","u1"),(thirds,"start","u1"),(firsts,"finish","o"),(seconds,"start","o"))
    def total(b,_):
        cross(b).wait_recv()
        fetch(b).wait()
        summed[b]=(d_buf[lax.rem(b,2)]+(term[b].astype(f32)+other[b].astype(f32))).astype(bf)
        @pl.when(b+2<nb)
        def _():
            fetch(b+2).start()
        @pl.when(own)
        def _():
            near(b).start()
        @pl.when(jnp.logical_not(own))
        def _():
            far(b).start()
        return 0
    lax.fori_loop(0,1,total,0)
    weight_grads(1)
    run((firsts,"start","h1"))
    lax.fori_loop(1,2,total,0)
    run((firsts,"finish","h0"),(seconds,"start","h0"),(seconds,"finish","o"),(thirds,"start","o"))
    lax.fori_loop(2,4,total,0)
    run((thirds,"finish","g0 g1 u0 u1"))
    run((firsts,"finish","h1"),(seconds,"start","h1"))
    lax.fori_loop(4,nb,total,0)
    run((seconds,"finish","h0"),(thirds,"start","h0"),(thirds,"finish","o"))
    give("g","u","o")
    run((seconds,"finish","h1"),(thirds,"start","h1"),(thirds,"finish","h0"))
    give("h0")
    run((thirds,"finish","h1"))
    give("h1")
    for group in (firsts,seconds,thirds):
        for x in group.values(): x.drain()
    def drain(b,_):
        cross(b).wait_send()
        @pl.when(own)
        def _():
            near(b).wait()
        @pl.when(jnp.logical_not(own))
        def _():
            far(b).wait_recv()
            far(b).wait_send()
        return 0
    lax.fori_loop(0,nb,drain,0)
    @pl.when(jnp.logical_not(own))
    def _():
        for x in finals.values():
            x.wait_recv()
            x.wait_send()

def fused_bwd(q_s,k_s,v_s,m_t,dm,lse,start,cos,sin,gg,gu,gow,d0,d1,tok_t,wt,d_one,cols):
    pr,n,_=q_s.shape; heads=2*pr; width=tok_t.shape[0]; nb=n//QB
    V=pl.BlockSpec(memory_space=pltpu.VMEM); A=pl.BlockSpec(memory_space=pl.ANY)
    S=jax.ShapeDtypeStruct
    ff=gg.shape[-1]; r=gg.shape[-2]; w=gow.shape[-1]; h=ff//2; hw=-(-3*cols//2//128)*128
    vm=pltpu.VMEM
    dma=lambda k: pltpu.SemaphoreType.DMA((k,))
    blocks=(nb,QB,width)
    like=lambda a: vm(a.shape,a.dtype)
    one=lambda k: [vm((4,2,r,k),bf),dma(2)]
    two=lambda k: [vm((4,r,k),bf),dma(2)]
    three=lambda k: [vm((3,r,k),bf),dma(3),dma(3)]
    return pl.pallas_call(functools.partial(fused_bwd_kernel,n,cols),
      out_shape=[S((r,ff),bf)]*3+[S((r,w),bf)]+[S((r,hw),bf)]*2+[S(blocks,bf)],
      in_specs=[V]*10+[A]*7,out_specs=[V]*6+[A],
      scratch_shapes=[vm((pr,128,n),bf)]*3+[vm((pr,128,n),f32),vm((pr,n,128),f32),vm((pr,n,128),f32),vm((heads,n),f32),vm((3,n,pr*128),bf),
        like(gg),like(gu),like(gow),like(tok_t),like(wt),vm((2,QB,width),f32),vm((4,2,2,r,hw),bf),vm((4,2,2,r,hw),bf)]+[vm(blocks,bf)]*3
        +[dma(6),dma(2)]+[dma(nb)]*4+[dma(6),dma(6)]
        +(one(h)+two(h))*4+one(w)+two(w)+(one(hw)+two(hw))*2+two(h)*2
        +[vm((r,ff),bf)]*3+[vm((r,w),bf)]+[vm((r,hw),bf)]*2+three(h)*6+three(w)+three(hw)*2,
      compiler_params=pltpu.CompilerParams(vmem_limit_bytes=64<<20,collective_id=1,has_side_effects=True),name="attn_bwd_reduce")(
        q_s,k_s,v_s,dm,lse,start,cos,sin,d0,d1,m_t,gg,gu,gow,tok_t,wt,d_one.reshape(blocks))

def dot_nt_t(a,b,put):
    return dot(dot(a,b).astype(bf),put).astype(bf)

NORM_EPS=1e-05
DIAG=[(0,0),(3,3),(1,2),(2,1)]
CORE=[(0,1),(1,0)]

def cross_copies(n,part,other,send,recv,c):
    def one(b): return pltpu.make_async_remote_copy(src_ref=part.at[b],dst_ref=other.at[b],send_sem=send.at[b],recv_sem=recv.at[b],device_id={"c":1-c},device_id_type=MESH)
    return one

def norm_of(r):
    inv=lax.rsqrt(jnp.mean(r*r,-1,keepdims=True)+NORM_EPS)
    return r*inv,inv

def norm_back(e,nrm,inv):
    return inv*(e-nrm*jnp.mean(e*nrm,-1,keepdims=True))

def ffn_kernel(n,cols,tok,og,mixed,ofull,wg,wu,wd,ga,gb,output,gg,gu,d_one,dm,gow,one0,one1,
        out_t,t1,t2,act,normed,inv1,hb_t,dff_t,part,oa,of,oh,summed,gsum,gd,og_s,og_r,a_s,a_r,f_s,f_r,h_s,h_r,x_s,x_r,s0,s1):
    z,y,m=place(); c=lax.axis_index("c")
    own=c==m
    greet(peers(z,y,m)+both(c,m))
    nb=n//QB
    grad_far=pltpu.make_async_remote_copy(src_ref=og,dst_ref=summed,send_sem=og_s,recv_sem=og_r,device_id={"c":1-c},device_id_type=MESH)
    grad_near=pltpu.make_async_copy(og,summed,og_r)
    def rows_of(b): return pl.ds(pl.multiple_of(b*QB,QB),QB)
    ca,cf,ch=[cross_copies(n,part,o,ss,rs,c) for o,ss,rs in ((oa,a_s,a_r),(of,f_s,f_r),(oh,h_s,h_r))]
    def far(b): return pltpu.make_async_remote_copy(src_ref=summed.at[b],dst_ref=output.at[b],send_sem=x_s.at[b],recv_sem=x_r.at[b],device_id={"c":1-c,"m":1-m},device_id_type=MESH)
    def near(b): return pltpu.make_async_copy(summed.at[b],output.at[b],x_r.at[b])
    out_t[...]=dot_nt(ofull[...],spread(cols//HD*64,cols,False)).astype(bf)
    def attn_part(b,_):
        part[b]=dot_nt(mixed[rows_of(b),:],out_t[...]).astype(bf)
        ca(b).start()
        return 0
    lax.fori_loop(0,nb,attn_part,0)
    @pl.when(own)
    def _():
        grad_far.start()
        grad_near.start()
    def forward(b,_):
        rows=rows_of(b)
        ca(b).wait_recv()
        r=tok[rows,:].astype(f32)+(part[b].astype(f32)+oa[b].astype(f32))
        nrm,inv=norm_of(r)
        normed[rows,:]=nrm
        inv1[rows,:]=inv
        hb=(nrm*ga[...]).astype(bf)
        hb_t[:,rows]=hb.T
        gate=dot(hb,wg[...]); up=dot(hb,wu[...])
        sg=jax.nn.sigmoid(gate)
        gs=gate*sg
        a=(gs*up).astype(bf)
        act[rows,:]=a
        t2[rows,:]=gs.astype(bf)
        t1[rows,:]=(up*sg*(1.0+gate*(1.0-sg))).astype(bf)
        ca(b).wait_send()
        part[b]=dot_nt(a,wd[...]).astype(bf)
        cf(b).start()
        return 0
    lax.fori_loop(0,nb,forward,0)
    @pl.when(own)
    def _():
        grad_near.wait()
        grad_far.wait_send()
    @pl.when(jnp.logical_not(own))
    def _():
        grad_far.wait_recv()
    gsum[...]=jnp.zeros_like(gsum)
    def fold(v): return jnp.sum(v.reshape(QB//8,8,v.shape[-1]),0)
    def norm_two(b,_):
        rows=rows_of(b)
        cf(b).wait_recv()
        nrm,inv=norm_of(normed[rows,:]*ga[...]+(part[b].astype(f32)+of[b].astype(f32)))
        g=summed[b].astype(f32)
        summed[b]=(nrm*gb[...]).astype(bf)
        @pl.when(own)
        def _():
            near(b).start()
        @pl.when(jnp.logical_not(own))
        def _():
            far(b).start()
        gsum[8:16,:]+=fold(g*nrm)
        d2=norm_back(g*gb[...],nrm,inv)
        d_one[rows,:]=d2
        df=d2.astype(bf)
        oa[b]=df
        dff_t[:,rows]=df.T
        return 0
    lax.fori_loop(0,nb,norm_two,0)
    width=hb_t.shape[0]; quarter=width//4; ff=act.shape[1]
    def rows4(i): return pl.ds(pl.multiple_of(i*quarter,quarter),quarter)
    def down_grad(i,_):
        gd[i]=dot(dff_t[rows4(i),:],act[...]).astype(bf).reshape(2,2,quarter//4,ff)
        return 0
    lax.fori_loop(0,4,down_grad,0)
    h2=ff//2
    ch2=[First(gd.at[:,:,:,:,0:h2],one0,s0),First(gd.at[:,:,:,:,h2:ff],one1,s1)]
    for x in ch2: x.start()
    def backward(b,_):
        rows=rows_of(b)
        da=dot(oa[b],wd[...])
        dg=(da*t1[rows,:].astype(f32)).astype(bf); du=(da*t2[rows,:].astype(f32)).astype(bf)
        t1[rows,:]=dg; t2[rows,:]=du
        cf(b).wait_send()
        part[b]=(dot_nt(dg,wg[...])+dot_nt(du,wu[...])).astype(bf)
        ch(b).start()
        return 0
    lax.fori_loop(0,nb,backward,0)
    def grads(i,_):
        gg[i]=dot(hb_t[rows4(i),:],t1[...]).astype(bf).reshape(2,2,quarter//4,ff)
        gu[i]=dot(hb_t[rows4(i),:],t2[...]).astype(bf).reshape(2,2,quarter//4,ff)
        return 0
    lax.fori_loop(0,4,grads,0)
    def last(b,_):
        rows=rows_of(b)
        ch(b).wait_recv()
        dh=d_one[rows,:]+(part[b].astype(f32)+oh[b].astype(f32))
        nrm=normed[rows,:]
        gsum[0:8,:]+=fold(dh*nrm)
        d1=norm_back(dh*ga[...],nrm,inv1[rows,:])
        d_one[rows,:]=d1
        da=d1.astype(bf)
        hb_t[:,rows]=da.T
        back=dot(da,out_t[...]).astype(bf)
        for p in range(dm.shape[0]): dm[p,rows,:]=back[:,p*128:p*128+128]
        return 0
    lax.fori_loop(0,nb,last,0)
    put=spread(cols//HD*64,cols,False)
    def out_grads(i,_):
        gow[i,:,:,:,128:128+cols]=dot_nt_t(hb_t[rows4(i),:],mixed[...],put).reshape(2,2,quarter//4,cols)
        return 0
    lax.fori_loop(0,4,out_grads,0)
    line=lax.broadcasted_iota(jnp.int32,(128,width),0)
    both_gains=jnp.where(line==0,jnp.sum(gsum[0:8,:],0,keepdims=True),jnp.where(line==1,jnp.sum(gsum[8:16,:],0,keepdims=True),0.0))
    gow[:,:,:,:,0:128]=both_gains.T.astype(bf).reshape(4,2,2,quarter//4,128)
    for x in ch2: x.finish()
    for x in ch2: x.drain()
    def drain(b,_):
        ch(b).wait_send()
        @pl.when(own)
        def _():
            near(b).wait()
        @pl.when(jnp.logical_not(own))
        def _():
            far(b).wait_recv()
            far(b).wait_send()
        return 0
    lax.fori_loop(0,nb,drain,0)

def ffn_call(tok,og,mixed,ofull,wg,wu,wd,ga,gb,cols):
    n,width=tok.shape; ff=wg.shape[1]; hp=mixed.shape[1]; nb=n//QB
    V=pl.BlockSpec(memory_space=pltpu.VMEM); A=pl.BlockSpec(memory_space=pl.ANY)
    S=jax.ShapeDtypeStruct
    blocks=(nb,QB,width); r=width//16
    dma=pltpu.SemaphoreType.DMA((nb,))
    vm=pltpu.VMEM
    return pl.pallas_call(functools.partial(ffn_kernel,n,cols),
      out_shape=[S(blocks,bf)]+[S((4,2,2,r,ff),bf)]*2+[S((n,width),f32),S((hp//128,n,128),bf),S((4,2,2,r,cols+128),bf)]+[S((4,2,r,ff//2),bf)]*2,
      in_specs=[V,A]+[V]*7,out_specs=[A]+[V]*7,
      scratch_shapes=[vm((width,hp),bf),vm((n,ff),bf),vm((n,ff),bf),vm((n,ff),bf),vm((n,width),f32),vm((n,1),f32),vm((width,n),bf),vm((width,n),bf),
        vm(blocks,bf),vm(blocks,bf),vm(blocks,bf),vm(blocks,bf),vm(blocks,bf),vm((16,width),f32),vm((4,2,2,r,ff),bf),
        pltpu.SemaphoreType.DMA,pltpu.SemaphoreType.DMA]+[dma]*8+[pltpu.SemaphoreType.DMA((2,))]*2,
      compiler_params=pltpu.CompilerParams(vmem_limit_bytes=64<<20,collective_id=3,has_side_effects=True),name="ffn")(
        tok,og.reshape(blocks),mixed,ofull,wg,wu,wd,ga[None],gb[None])

def rms_forward(resid):
    inverse=lax.rsqrt(jnp.mean(resid*resid,-1,keepdims=True)+NORM_EPS)
    return (resid*inverse,inverse)

def rms_backward(grad_normed,normed,inverse):
    return inverse*(grad_normed-normed*jnp.mean(grad_normed*normed,-1,keepdims=True))

def doc_starts(lengths,n):
    at=jnp.arange(n,dtype=jnp.int32); start=jnp.zeros((n,),jnp.int32); end=jnp.int32(0)
    for i in range(lengths.shape[0]-1):
        end=end+lengths[i]
        start=jnp.where(at>=end,end,start)
    return start

def rope_tables(positions):
    lane=jnp.arange(128,dtype=jnp.int32)%64
    fr=jnp.where(lane<HD,jnp.exp((lane%(HD//2)).astype(f32)*(-2.0*math.log(10000.0)/HD)),0.0)
    a=positions.astype(f32)[:,None]*fr[None,:]
    return jnp.cos(a),jnp.sin(a)

def core_sum(part):
    return part.astype(f32)+lax.ppermute(part,"c",CORE).astype(f32)

def on_device(tokens,out_grad,doc_lengths,w_query,w_key,w_value,w_out,gain_one,w_gate,w_up,w_down,gain_two):
    cols=w_query.shape[1]; ff=w_gate.shape[1]; n,width=tokens.shape
    quad=lax.axis_size("q")==8 and w_query.shape[0]==48
    if not quad:
        own=lax.axis_index("c")==lax.axis_index("m")
        pick=lambda a: jnp.where(own,a,lax.ppermute(a,"c",CORE))
        tokens,out_grad,doc_lengths=pick(tokens),pick(out_grad),pick(doc_lengths)
    start=doc_starts(doc_lengths[0],n)
    cos,sin=rope_tables(jnp.arange(n,dtype=jnp.int32)-start)
    start=start[None]
    cast=lambda a: a.astype(bf)
    gains=jnp.pad(jnp.stack([cast(gain_one),cast(gain_two)],1),((0,0),(0,126)))
    apack=jnp.concatenate([cast(w_query),cast(w_key),cast(w_value),gains],1)
    def gather(a):
        return lax.all_gather(lax.ppermute(a,("c","m"),DIAG),("q","m"),axis=0,tiled=True)
    if quad:
        tokens,cos,sin,start,afull,ofull,gate_w,up_w,down_t,q,k,v,m_t,mixed,lse,tok_t,wt=fused_fwd(
            tokens,cos,sin,start,apack,cast(w_out).T,cast(w_gate),cast(w_up),cast(w_down).T,cols)
        afull,ofull,gate_w,up_w,down_t=[a.reshape(width,a.shape[-1]) for a in (afull,ofull,gate_w,up_w,down_t)]
    else:
        afull,ofull,gate_w,up_w,down_t=[gather(a) for a in (apack,cast(w_out).T,cast(w_gate),cast(w_up),cast(w_down).T)]
        q,k,v,m_t,mixed,lse=attn_fwd(tokens,afull[:,:3*cols],cos,sin,start)
    hp=cols//HD*64
    put=spread(hp,cols,False)
    out_t=dot_nt(ofull,put).astype(bf)
    gain_a=afull[:,3*cols].astype(f32); gain_b=afull[:,3*cols+1].astype(f32)
    own=lax.axis_index("c")==lax.axis_index("m")
    if quad:
        output,gg,gu,d_one,dm,gow,*downs=ffn_call(tokens,out_grad,mixed,ofull,gate_w,up_w,down_t,gain_a,gain_b,cols)
        output=output.reshape(n,width)
        sdown,sgate,sup,sout,sh0,sh1,gtok=[a.astype(f32) for a in fused_bwd(q,k,v,m_t,dm,lse,start,cos,sin,gg,gu,gow,*downs,tok_t,wt,d_one,cols)]
        hc=cols//2
        sq,sk,sv=[jnp.concatenate([a[:,j*hc:(j+1)*hc] for a in (sh0,sh1)],1) for j in range(3)]
        return (output,gtok.reshape(n,width),sq,sk,sv,sout[:,128:].T,sout[:,0],sgate,sup,sdown.T,sout[:,1])
    else:
        attn=core_sum(dot_nt(mixed,out_t).astype(bf))
        normed_one,inv_one=rms_forward(tokens.astype(f32)+attn)
        hidden=normed_one*gain_a
        hb=hidden.astype(bf)
        gate=dot(hb,gate_w); up=dot(hb,up_w)
        sg=jax.nn.sigmoid(gate)
        act=(gate*sg*up).astype(bf)
        ffn=core_sum(dot_nt(act,down_t).astype(bf))
        normed_two,inv_two=rms_forward(hidden+ffn)
        output=(normed_two*gain_b).astype(bf)
        g=out_grad.astype(f32)
        g_gain_two=jnp.sum(g*normed_two,0)
        d_two=rms_backward(g*gain_b,normed_two,inv_two)
        d_ffn=d_two.astype(bf)
        tn=lambda a,b: lax.dot_general(a,b,(((0,),(0,)),((),())),preferred_element_type=f32)
        d_act=dot(d_ffn,down_t)
        d_up=(d_act*gate*sg).astype(bf)
        d_gate=(d_act*up*sg*(1.0+gate*(1.0-sg))).astype(bf)
        hterm=(dot_nt(d_gate,gate_w)+dot_nt(d_up,up_w)).astype(bf)
        gff=[tn(hb,d_gate).astype(bf),tn(hb,d_up).astype(bf),tn(d_ffn,act).astype(bf)]
        d_hidden=d_two+core_sum(hterm)
        g_gain_one=jnp.sum(d_hidden*normed_one,0)
        d_one=rms_backward(d_hidden*gain_a,normed_one,inv_one)
        d_attn=d_one.astype(bf)
        dm=dot(d_attn,out_t).astype(bf)
        output=jnp.where(own,output,lax.ppermute(output,("c","m"),[(1,2),(2,1)]))

        ggain=jnp.pad(jnp.stack([g_gain_one,g_gain_two],1),((0,0),(0,126))).astype(bf)
        dqkv=attn_bwd(q,k,v,m_t,dm,lse,start,cos,sin)
        term=0.0; gqkv=[]
        for j in range(3):
            wp=dot_nt(afull[:,j*cols:(j+1)*cols],put).astype(bf)
            term=term+dot_nt(dqkv[j],wp)
            gqkv.append(dot(tn(tokens,dqkv[j]).astype(bf),put).astype(bf))
        gtok=(d_one+core_sum(term.astype(bf))).astype(bf)
        gtok=lax.ppermute(gtok,("c","m"),DIAG).astype(f32)
        g_out=dot(tn(d_attn,mixed).astype(bf),put).astype(bf)
        gatt=jnp.concatenate([ggain,g_out]+gqkv,1)
        add=lambda a: lax.psum_scatter(a,("q","m"),scatter_dimension=0,tiled=True)
        sff,sat=[add(a) for a in gff],add(gatt)
        sff,sat=lax.ppermute(jnp.concatenate(sff,1),("c","m"),DIAG).astype(f32),lax.ppermute(sat,("c","m"),DIAG).astype(f32)
        piece=lambda j: sat[:,128+j*cols:128+(j+1)*cols]
        return (output,gtok,piece(1),piece(2),piece(3),piece(0).T,sat[:,0],sff[:,:ff],sff[:,ff:2*ff],sff[:,2*ff:].T,sat[:,1])

def solution(mesh):
    dp,mp=mesh.shape["dp"],mesh.shape["mp"]
    fine=Mesh(mesh.devices.reshape(dp//2,2,mp),("q","c","m"))
    d=("q","c")
    rows,cols_=P(d,"m"),P("m",d)
    return jax.shard_map(on_device,mesh=fine,
        in_specs=(P(d,None),P(d,None),P(d,None),rows,rows,rows,cols_,P(d),rows,rows,cols_,P(d)),
        out_specs=(P(d,None),P(d,None),rows,rows,rows,cols_,P(d),rows,rows,cols_,P(d)),check_vma=False)
```

```python
import functools
import math
import jax
import jax.numpy as jnp
import numpy as np
from jax import lax
from jax.experimental import pallas as pl
from jax.experimental.pallas import tpu as pltpu
from jax.sharding import Mesh, PartitionSpec as P
MESH=pl.DeviceIdType.MESH
HD=48
C2=HD**-0.5*math.log2(math.e)
NEG=-1e30
bf=jnp.bfloat16; f32=jnp.float32
QB=256; LOOK=4
NT=(((1,),(1,)),((),()))
def dot(a,b): return jnp.dot(a,b,preferred_element_type=f32)
def dot_nt(a,b): return lax.dot_general(a,b,NT,preferred_element_type=f32)

def spread(rows, cols, rot):
    r=lax.broadcasted_iota(jnp.int32,(rows,cols),0); c=lax.broadcasted_iota(jnp.int32,(rows,cols),1)
    h=r//64; d=r-h*64
    if not rot:
        return jnp.where((d<HD)&(c==h*HD+d),1.0,0.0).astype(bf)
    lo=(d<24)&(c==h*HD+d+24); hi=(d>=24)&(d<HD)&(c==h*HD+d-24)
    return jnp.where(lo,-1.0,jnp.where(hi,1.0,0.0)).astype(bf)

def proj_weights(w,wq_s,cols):
    hp=cols//HD*64
    for m,(col,rot) in enumerate(((0,False),(0,True),(1,False),(1,True),(2,False))):
        if len(w.shape)==2:
            part=w[:,col*cols:(col+1)*cols]
        else:
            part=w[:,:,:,:,col*cols:(col+1)*cols].reshape(-1,cols)
        wq_s[m]=dot_nt(spread(hp,cols,rot),part).astype(bf)

def proj(tok,cos,sin,wq_s,q_s,k_s,v_s,lo,hi):
    def body(b,_):
        rows=pl.ds(pl.multiple_of(b*QB,QB),QB)
        x=tok[rows,:]
        cs=cos[rows,:]; sn=sin[rows,:]
        for dst,a in ((q_s,0),(k_s,2)):
            raw=dot_nt(x,wq_s[a]); rt=dot_nt(x,wq_s[a+1])
            for p in range(dst.shape[0]):
                l=slice(p*128,p*128+128)
                dst[p,rows,:]=(raw[:,l]*cs+rt[:,l]*sn).astype(bf)
        raw=dot_nt(x,wq_s[4])
        for p in range(v_s.shape[0]):
            v_s[p,rows,:]=raw[:,p*128:p*128+128].astype(bf)
        return 0
    lax.fori_loop(lo,hi,body,0)

def masks(kk0,nk,i,start):
    kidx=lax.broadcasted_iota(jnp.int32,(nk,QB),0)+kk0
    ok=kidx>=start
    qidx=lax.broadcasted_iota(jnp.int32,(nk,QB),1)+i*QB
    return ok&(kidx<=qidx)

def fwd_head(h,i,q_t,k_s,v_t,start,m_t,lse):
    p=h//2; half=h-2*p
    lo=max(0,i-LOOK)*QB; nk=(i+1)*QB-lo
    kk=slice(lo,lo+nk); qq=slice(i*QB,(i+1)*QB)
    row=lax.broadcasted_iota(jnp.int32,(128,QB),0)
    mine=(row>=half*64)&(row<half*64+64)
    qt=jnp.where(mine,q_t[p,:,qq],jnp.zeros((),bf))
    s=dot(k_s[p,kk,:],qt)
    st=start[:,qq]
    s=jnp.where(masks(lo,nk,i,st),s,NEG)
    m=jnp.max(s,0,keepdims=True)
    e=jnp.exp2((s-m)*C2)
    l=jnp.sum(e,0,keepdims=True)
    pr=(e*(1.0/l)).astype(bf)
    rows=pl.ds(pl.multiple_of(half*64,64),64)
    m_t[p,rows,qq]=dot(v_t[p,rows,kk],pr)
    lse[pl.ds(h,1),qq]=m*C2+jnp.log2(l)

def fwd_kernel(n,cols,tok,w,cos,sin,start,q_o,k_o,v_o,m_t,mixed,lse,wq_s,q_t,v_t):
    proj_weights(w,wq_s,cols)
    proj(tok,cos,sin,wq_s,q_o,k_o,v_o,0,n//QB)
    heads=cols//HD
    for p in range(heads//2):
        q_t[p]=q_o[p].T
        v_t[p]=v_o[p].T
    def body(h,_):
        for i in range(n//QB):
            fwd_head(h,i,q_t,k_o,v_t,start,m_t,lse)
        return 0
    lax.fori_loop(0,heads,body,0)
    for p in range(heads//2):
        mixed[:,p*128:p*128+128]=m_t[p].T.astype(bf)

def attn_fwd(tok,w,cos,sin,start):
    n=tok.shape[0]; cols=w.shape[1]//3; heads=cols//HD; P=heads//2
    V=pl.BlockSpec(memory_space=pltpu.VMEM)
    S=jax.ShapeDtypeStruct
    return pl.pallas_call(functools.partial(fwd_kernel,n,cols),
      out_shape=(S((P,n,128),bf),S((P,n,128),bf),S((P,n,128),bf),S((P,128,n),f32),S((n,P*128),bf),S((heads,n),f32)),
      in_specs=[V]*5,out_specs=[V]*6,
      scratch_shapes=[pltpu.VMEM((5,P*128,w.shape[0]),bf),pltpu.VMEM((P,128,n),bf),pltpu.VMEM((P,128,n),bf)],
      compiler_params=pltpu.CompilerParams(vmem_limit_bytes=60<<20),name="attn_fwd")(tok,w,cos,sin,start)

def bwd_head(h,i,q_t,q_s,k_s,k_t,v_s,dm_t,dm_s,lse,dd,start,dq_t,dk_s,dv_s):
    p=h//2; half=h-2*p
    lo=max(0,i-LOOK)*QB; nk=(i+1)*QB-lo
    kk=slice(lo,lo+nk); qq=slice(i*QB,(i+1)*QB)
    row=lax.broadcasted_iota(jnp.int32,(128,QB),0)
    mine=(row>=half*64)&(row<half*64+64)
    lane=lax.broadcasted_iota(jnp.int32,(QB,128),1)
    mlane=(lane>=half*64)&(lane<half*64+64)
    zero=jnp.zeros((),bf)
    qt=jnp.where(mine,q_t[p,:,qq],zero)
    dmt=jnp.where(mine,dm_t[p,:,qq],zero)
    qn=jnp.where(mlane,q_s[p,qq,:],zero)
    dmn=jnp.where(mlane,dm_s[p,qq,:],zero)
    s=dot(k_s[p,kk,:],qt)
    st=start[:,qq]
    pr=jnp.exp2(jnp.where(masks(lo,nk,i,st),s*C2,NEG)-lse[pl.ds(h,1),qq])
    dp=dot(v_s[p,kk,:],dmt)
    ds=(pr*(dp-dd[pl.ds(h,1),qq])).astype(bf)
    pb=pr.astype(bf)
    dv_s[p,kk,:]+=dot(pb,dmn)
    dk_s[p,kk,:]+=dot(ds,qn)
    rows=pl.ds(pl.multiple_of(half*64,64),64)
    dq_t[p,rows,qq]=dot(k_t[p,rows,kk],ds)

def rope_back(u,cs,sn):
    w=u*sn
    lane=lax.broadcasted_iota(jnp.int32,u.shape,1)&63
    up=pltpu.roll(w,128-24,axis=1); dn=pltpu.roll(w,24,axis=1)
    return u*cs+jnp.where(lane<24,up,jnp.where(lane<48,-dn,0.0))

def bwd_kernel(n,heads,q_s,k_s,v_s,m_t,dm,lse,start,cos,sin,dqkv,q_t,k_t,dm_t,dm_s,dq_t,dk_s,dv_s,dd):
    P=heads//2
    for p in range(P):
        q_t[p]=q_s[p].T
        k_t[p]=k_s[p].T
        dm_s[p]=dm[:,p*128:p*128+128]
        dm_t[p]=dm_s[p].T
        for half in range(2):
            r=slice(half*64,half*64+64)
            dd[2*p+half:2*p+half+1,:]=jnp.sum(dm_t[p,r,:].astype(f32)*m_t[p,r,:],0,keepdims=True)
    dk_s[...]=jnp.zeros_like(dk_s); dv_s[...]=jnp.zeros_like(dv_s)
    def body(h,_):
        for i in range(n//QB):
            bwd_head(h,i,q_t,q_s,k_s,k_t,v_s,dm_t,dm_s,lse,dd,start,dq_t,dk_s,dv_s)
        return 0
    lax.fori_loop(0,heads,body,0)
    sc=HD**-0.5
    for p in range(P):
        dqkv[0,:,p*128:p*128+128]=rope_back(dq_t[p].T*sc,cos[...],sin[...]).astype(bf)
        dqkv[1,:,p*128:p*128+128]=rope_back(dk_s[p]*sc,cos[...],sin[...]).astype(bf)
        dqkv[2,:,p*128:p*128+128]=dv_s[p].astype(bf)

def attn_bwd(q_s,k_s,v_s,m_t,dm,lse,start,cos,sin):
    P,n,_=q_s.shape; heads=2*P
    V=pl.BlockSpec(memory_space=pltpu.VMEM)
    S=jax.ShapeDtypeStruct
    return pl.pallas_call(functools.partial(bwd_kernel,n,heads),
      out_shape=S((3,n,P*128),bf),
      in_specs=[V]*9,out_specs=V,
      scratch_shapes=[pltpu.VMEM((P,128,n),bf),pltpu.VMEM((P,128,n),bf),pltpu.VMEM((P,128,n),bf),pltpu.VMEM((P,n,128),bf),pltpu.VMEM((P,128,n),f32),pltpu.VMEM((P,n,128),f32),pltpu.VMEM((P,n,128),f32),pltpu.VMEM((heads,n),f32)],
      compiler_params=pltpu.CompilerParams(vmem_limit_bytes=60<<20),name="attn_bwd")(q_s,k_s,v_s,m_t,dm,lse,start,cos,sin)


def place():
    q,m=lax.axis_index("q"),lax.axis_index("m")
    return q//2,lax.rem(q,2),m

def peers(z,y,m):
    return [{"q":z*2+1-y},{"m":1-m}]+[{"q":lax.rem(z+s,4)*2+y} for s in (1,2,3)]

def greet(where):
    barrier=pltpu.get_barrier_semaphore()
    for w in where:
        pl.semaphore_signal(barrier,inc=1,device_id=w,device_id_type=MESH)
    pl.semaphore_wait(barrier,len(where))

def remote(s,d,ss,rs,w):
    return pltpu.make_async_remote_copy(src_ref=s,dst_ref=d,send_sem=ss,recv_sem=rs,device_id=w,device_id_type=MESH)

class First:
    def __init__(self,source,one,sem,first="y"):
        self.source,self.one,self.first=source,one,first
        z,y,m=place()
        self.y,self.m=y,m
        ny,nx=peers(z,y,m)[:2]
        self.copy=remote(source.at[:,1-y],one,sem.at[0],sem.at[1],ny) if first=="y" else remote(source.at[:,:,1-m],one,sem.at[0],sem.at[1],nx)
    def start(self): self.copy.start()
    def finish(self):
        self.copy.wait_recv()
        def add(i,_):
            zz=i//2; o=i-zz*2
            mine=self.source[zz,self.y,o] if self.first=="y" else self.source[zz,o,self.m]
            self.one[zz,o]=(self.one[zz,o].astype(f32)+mine.astype(f32)).astype(bf)
            return 0
        lax.fori_loop(0,8,add,0)
    def drain(self): self.copy.wait_send()

class Second:
    def __init__(self,one,two,sem,first="y"):
        self.one,self.two=one,two
        z,y,m=place()
        ny,nx=peers(z,y,m)[:2]
        self.keep=m if first=="y" else y
        self.copy=remote(one.at[:,1-self.keep],two,sem.at[0],sem.at[1],nx if first=="y" else ny)
    def start(self): self.copy.start()
    def finish(self):
        self.copy.wait_recv()
        def add(zz,_):
            self.two[zz]=(self.two[zz].astype(f32)+self.one[zz,self.keep].astype(f32)).astype(bf)
            return 0
        lax.fori_loop(0,4,add,0)
    def drain(self): self.copy.wait_send()

class SecondZ:
    def __init__(self,one,two,three,send,recv):
        self.one,self.two,self.three=one,two,three
        z,y,m=place()
        self.z=z
        to=peers(z,y,m)
        self.copies=[remote(one.at[lax.rem(z+s,4)],three.at[s-1],send.at[s-1],recv.at[s-1],to[1+s]) for s in (1,2,3)]
    def start(self):
        for c in self.copies: c.start()
    def finish(self):
        for c in self.copies: c.wait_recv()
        for o in range(2):
            t=self.one[self.z,o].astype(f32)
            for s in range(3): t=t+self.three[s,o].astype(f32)
            self.two[o]=t.astype(bf)
    def drain(self):
        for c in self.copies: c.wait_send()

class ThirdX:
    def __init__(self,two,other,out,sem):
        self.two,self.other,self.out=two,other,out
        z,y,m=place()
        self.m=m
        self.copy=remote(two.at[1-m],other,sem.at[0],sem.at[1],{"m":1-m})
    def start(self): self.copy.start()
    def finish(self):
        self.copy.wait_recv()
        self.out[...]=(self.two[self.m].astype(f32)+self.other[...].astype(f32)).astype(bf)
    def drain(self): self.copy.wait_send()

class Third:
    def __init__(self,two,three,out,send,recv):
        self.two,self.three,self.out=two,three,out
        z,y,m=place()
        self.z=z
        to=peers(z,y,m)
        self.copies=[remote(two.at[lax.rem(z+s,4)],three.at[s-1],send.at[s-1],recv.at[s-1],to[1+s]) for s in (1,2,3)]
    def start(self):
        for c in self.copies: c.start()
    def finish(self):
        for c in self.copies: c.wait_recv()
        t=self.two[self.z].astype(f32)
        for s in range(3): t=t+self.three[s].astype(f32)
        self.out[...]=t.astype(bf)
    def drain(self):
        for c in self.copies: c.wait_send()

class Gather:
    def __init__(self,shard,full,cols,stage,sem,sem_z,first):
        z,y,m=place(); c=lax.axis_index("c")
        to=peers(z,y,m)
        src=shard.at[:,cols]
        self.first=first
        self.own=c==m
        self.here=pltpu.make_async_copy(src,stage.at[z,y],sem.at[0])
        self.along=[remote(src,stage.at[z,y],sem_z.at[0,s-1],sem_z.at[1,s-1],to[1+s]) for s in (1,2,3)]
        a,b=(stage.at[:,y],full.at[:,y,c,:,cols]) if first=="x" else (stage,full.at[:,:,c,:,cols])
        self.near_self=pltpu.make_async_copy(a,b,sem.at[1])
        self.near=remote(a,b,sem.at[2],sem.at[3],{"c":1-c})
        self.far_same=remote(a,b,sem.at[4],sem.at[5],{"m":1-m})
        self.far_diag=remote(a,b,sem.at[4],sem.at[6],{"c":1-c,"m":1-m})
        d=full.at[:,y,:,:,cols] if first=="x" else stage.at[:,y]
        self.across=remote(d,d,sem.at[7],sem.at[8],to[0])
    def start(self):
        self.here.start()
        for c in self.along: c.start()
    def cross(self):
        @pl.when(self.own)
        def _():
            self.near_self.start()
            self.far_same.start()
        @pl.when(jnp.logical_not(self.own))
        def _():
            self.far_diag.start()
            self.near.start()
    def crossed(self):
        @pl.when(self.own)
        def _():
            self.near_self.wait()
            self.near.wait_recv()
        @pl.when(jnp.logical_not(self.own))
        def _():
            self.far_same.wait_recv()
            self.far_diag.wait_recv()
    def second(self):
        self.here.wait()
        for c in self.along: c.wait_recv()
        if self.first=="x": self.cross()
        else: self.across.start()
    def third(self):
        if self.first=="x":
            self.crossed()
            self.across.start()
        else:
            self.across.wait_recv()
            self.cross()
    def finish(self):
        if self.first=="x": self.across.wait_recv()
        else: self.crossed()
    def drain(self):
        for c in self.along: c.wait_send()
        self.across.wait_send()
        @pl.when(self.own)
        def _():
            self.far_same.wait_send()
        @pl.when(jnp.logical_not(self.own))
        def _():
            self.far_diag.wait_send()
            self.near.wait_send()

def both(c,m):
    return [{"c":1-c},{"c":1-c,"m":1-m}]

def fused_fwd_kernel(n,cols,lengths,freq,tok_i,wq_i,wk_i,wv_i,wo_i,wg_i,wu_i,wd_i,g1_i,g2_i,
        tok_o,cos_o,sin_o,q_o,k_o,v_o,tok_t_o,wt_o,start,ga,gb,wo,wg,wu,wd,m_t,mixed,lse,
        tok,cos,sin,q_s,k_s,v_s,tok_t,wa,wq_s,q_t,v_t,docs_i,docs,a_b,o_b,g_b,u_b,d_b,swap_s,swap_r,out_s,*scr):
    z,y,m=place(); c=lax.axis_index("c")
    own=c==m
    r=a_b.shape[0]; ff=g_b.shape[1]
    eye=(lax.broadcasted_iota(jnp.int32,(r,r),0)==lax.broadcasted_iota(jnp.int32,(r,r),1)).astype(bf)
    line=lax.broadcasted_iota(jnp.int32,(128,r),0)
    gains=jnp.where(line==0,g1_i[...],jnp.where(line==1,g2_i[...],0.0)).astype(bf)
    for j,w in enumerate((wq_i,wk_i,wv_i)): a_b[:,j*cols:(j+1)*cols]=w[...].astype(bf)
    a_b[:,3*cols:]=dot_nt(eye,gains).astype(bf)
    g_b[...]=wg_i[...].astype(bf)
    u_b[...]=wu_i[...].astype(bf)
    o_b[...]=wo_i[...].astype(bf)
    d_b[...]=wd_i[...].astype(bf)
    row=lax.broadcasted_iota(jnp.int32,(8,128),0)
    table=jnp.zeros((8,128),jnp.int32)
    for i in range(lengths.shape[1]): table=jnp.where(row==i,lengths[0,i],table)
    docs_i[...]=table
    greet(peers(z,y,m)+both(c,m))
    packs=[(docs_i,docs),(tok_i,tok)]
    swap_far=[remote(a,b,swap_s.at[i],swap_r.at[i],{"c":1-c}) for i,(a,b) in enumerate(packs)]
    swap_near=[pltpu.make_async_copy(a,b,swap_r.at[i]) for i,(a,b) in enumerate(packs)]
    scr=list(scr)
    def chunk(shard,full,lo,hi,first):
        stage,sem,sem_z=scr[:3]
        del scr[:3]
        return Gather(shard,full,slice(lo,hi),stage,sem,sem_z,first)
    cut=cuts(a_b.shape[1])
    a=[chunk(a_b,wa,cut[i],cut[i+1],"xy"[i%2]) for i in range(4)]
    h2=ff//2
    f=[chunk(b,w,j*h2,j*h2+h2,"xy"[j]) for b,w in ((g_b,wg),(u_b,wu),(d_b,wd)) for j in range(2)]
    f.append(chunk(o_b,wo,0,cols,"x"))
    for x in a: x.start()
    @pl.when(own)
    def _():
        for x,w in zip(swap_near,swap_far):
            x.start(); w.start()
        swap_near[0].wait()
    @pl.when(jnp.logical_not(own))
    def _():
        swap_far[0].wait_recv()
    for x in f: x.start()
    def begin(at):
        end=jnp.zeros((1,1),jnp.int32); first=jnp.zeros(at.shape,jnp.int32)
        for i in range(lengths.shape[1]-1):
            end=end+docs[i:i+1,0:1]
            first=jnp.where(at>=end,end,first)
        return first
    start[...]=begin(lax.broadcasted_iota(jnp.int32,(1,n),1))
    def tables(b,_):
        rows=pl.ds(pl.multiple_of(b*QB,QB),QB)
        at=lax.broadcasted_iota(jnp.int32,(QB,128),0)+b*QB
        angle=(at-begin(at)).astype(f32)*freq[...]
        cos[rows,:]=jnp.cos(angle)
        sin[rows,:]=jnp.sin(angle)
        return 0
    nb=n//QB
    lax.fori_loop(0,nb//2,tables,0)
    a[0].second(); a[1].second()
    lax.fori_loop(nb//2,nb,tables,0)
    a[0].third(); a[1].third()
    a[2].second(); a[3].second()
    keep=[pltpu.make_async_copy(v,h,out_s.at[i]) for i,(v,h) in enumerate(((cos,cos_o),(sin,sin_o),(tok,tok_o),(tok_t,tok_t_o),(wq_s.at[0],wt_o.at[0]),(wq_s.at[2],wt_o.at[1]),
        (wq_s.at[4],wt_o.at[2]),(q_s,q_o),(k_s,k_o),(v_s,v_o)))]
    keep[0].start(); keep[1].start()
    @pl.when(own)
    def _():
        swap_near[1].wait()
    @pl.when(jnp.logical_not(own))
    def _():
        swap_far[1].wait_recv()
    keep[2].start()
    half=tok_t.shape[0]//2
    tok_t[:half,:]=tok[:,:half].T
    a[2].third(); a[3].third()
    tok_t[half:,:]=tok[:,half:].T
    keep[3].start()
    for x in a: x.finish()
    f[0].second(); f[1].second()
    proj_weights(wa,wq_s,cols)
    for x in keep[4:7]: x.start()
    proj(tok,cos,sin,wq_s,q_s,k_s,v_s,0,nb//2)
    f[0].third(); f[1].third()
    f[2].second(); f[3].second()
    proj(tok,cos,sin,wq_s,q_s,k_s,v_s,nb//2,nb)
    for x in keep[7:]: x.start()
    rows=wa[:,:,:,:,3*cols:].reshape(-1,128).astype(f32).T
    ga[...]=rows[0:1,:]
    gb[...]=rows[1:2,:]
    heads=cols//HD
    for p in range(heads//2):
        q_t[p]=q_s[p].T
        v_t[p]=v_s[p].T
    plan={0:[(2,"third"),(3,"third"),(4,"second"),(5,"second")],3:[(4,"third"),(5,"third"),(6,"second")],5:[(6,"third")]}
    def body(h,_):
        for i in range(nb):
            fwd_head(h,i,q_t,k_s,v_t,start,m_t,lse)
        for at,todo in plan.items():
            @pl.when(h==at)
            def _():
                for k,what in todo: getattr(f[k],what)()
        return 0
    lax.fori_loop(0,heads,body,0)
    for p in range(heads//2):
        mixed[:,p*128:p*128+128]=m_t[p].T.astype(bf)
    for x in f: x.finish()
    for x in a+f: x.drain()
    for x in keep: x.wait()
    @pl.when(own)
    def _():
        for x in swap_far: x.wait_send()

def cuts(width):
    return [0,width//1280*384,width//2,width//2+width//1280*256,width]

def fused_fwd(lengths,tok,wq,wk,wv,w_out,wg,wu,wd,g1,g2):
    n,width=tok.shape; r,cols=wq.shape; heads=cols//HD; pr=heads//2; ff=wg.shape[1]; ac=3*cols+128
    V=pl.BlockSpec(memory_space=pltpu.VMEM); A=pl.BlockSpec(memory_space=pl.ANY); M=pl.BlockSpec(memory_space=pltpu.SMEM)
    S=jax.ShapeDtypeStruct
    vm=pltpu.VMEM
    dma=lambda *k: pltpu.SemaphoreType.DMA(k)
    wide=lambda k: S((4,2,2,r,k),bf)
    lane=np.arange(128)%64
    freq=np.where(lane<HD,np.exp((lane%(HD//2)).astype(np.float32)*np.float32(-2.0*math.log(10000.0)/HD)),0.0).astype(np.float32)[None]
    cut=cuts(ac)
    sizes=[cut[i+1]-cut[i] for i in range(4)]+[ff//2]*6+[cols]
    pair=(pr,n,128)
    return pl.pallas_call(functools.partial(fused_fwd_kernel,n,cols),
      out_shape=[S((n,width),bf),S((n,128),f32),S((n,128),f32),S(pair,bf),S(pair,bf),S(pair,bf),S((width,n),bf),S((3,pr*128,width),bf),
        S((1,n),jnp.int32),S((1,width),f32),S((1,width),f32),wide(cols),wide(ff),wide(ff),wide(ff),S((pr,128,n),f32),S((n,pr*128),bf),S((heads,n),f32)],
      in_specs=[M,V,A]+[V]*9,out_specs=[A]*8+[V]*10,
      scratch_shapes=[vm((n,width),bf),vm((n,128),f32),vm((n,128),f32),vm(pair,bf),vm(pair,bf),vm(pair,bf),vm((width,n),bf),vm((4,2,2,r,ac),bf),
        vm((5,pr*128,width),bf),vm((pr,128,n),bf),vm((pr,128,n),bf),vm((8,128),jnp.int32),vm((8,128),jnp.int32),
        vm((r,ac),bf),vm((r,cols),bf),vm((r,ff),bf),vm((r,ff),bf),vm((r,ff),bf),dma(2),dma(2),dma(10)]
        +sum([[vm((4,2,r,k),bf),dma(9),dma(2,3)] for k in sizes],[]),
      compiler_params=pltpu.CompilerParams(vmem_limit_bytes=60<<20,collective_id=0,has_side_effects=True),name="attn_fwd_gather")(
        lengths,jnp.asarray(freq),tok,wq,wk,wv,w_out,wg,wu,wd,g1[None],g2[None])

def fused_bwd_kernel(n,cols,q_s,k_s,v_s,dm,lse,start,cos,sin,d0,d1,m_i,g_i,u_i,o_i,tok_i,wt_i,d_one,grads,gtok,
        q_t,k_t,dm_t,dq_t,dk_s,dv_s,dd,dqkv,gg,gu,gow,tok_t,wt,d_buf,ga0,ga1,term,other,load_s,d_sem,core_s,core_r,far_s,far_r,fin_s,fin_r,*scr):
    z,y,m=place(); c=lax.axis_index("c")
    own=c==m
    diag={"c":1-c,"m":1-m}
    loads=[pltpu.make_async_copy(a,b,load_s.at[i]) for i,(a,b) in enumerate(((m_i,dq_t),(g_i,gg),(u_i,gu),(o_i,gow),(tok_i,tok_t),(wt_i,wt)))]
    for x in loads: x.start()
    greet(peers(z,y,m)+both(c,m))
    scr=list(scr)
    def take(k):
        got=scr[:k]
        del scr[:k]
        return got
    half=gg.shape[-1]//2
    ff=2*half
    fd,fg,fu,fo,fh0,fh1,fq=take(7)
    outs={"d0":fd.at[:,0:half],"d1":fd.at[:,half:ff],"g0":fg.at[:,0:half],"g1":fg.at[:,half:ff],"u0":fu.at[:,0:half],"u1":fu.at[:,half:ff],
        "o":fo,"h0":fh0,"h1a":fh1.at[:,0:256],"h1b":fh1.at[:,256:ga1.shape[-1]]}
    firsts,seconds,thirds={},{},{}
    ones={"d0":d0,"d1":d1}
    for name,src,first in (("g0",gg.at[:,:,:,:,0:half],"y"),("g1",gg.at[:,:,:,:,half:ff],"x"),("u0",gu.at[:,:,:,:,0:half],"y"),("u1",gu.at[:,:,:,:,half:ff],"x"),
            ("o",gow,"y"),("h0",ga0,"y"),("h1a",ga1.at[:,:,:,:,0:256],"y"),("h1b",ga1.at[:,:,:,:,256:ga1.shape[-1]],"y")):
        ones[name],sem=take(2)
        firsts[name]=First(src,ones[name],sem,first)
    for name in ("h1a","h1b"):
        two,three,ss,rs,came,sem=take(6)
        seconds[name]=SecondZ(ones[name],two,three,ss,rs)
        thirds[name]=ThirdX(two,came,outs[name],sem)
    for name in ("d0","d1","g0","g1","u0","u1","o","h0"):
        two,sem,three,ss,rs=take(5)
        seconds[name]=Second(ones[name],two,sem,"x" if name in ("g1","u1") else "y")
        thirds[name]=Third(two,three,outs[name],ss,rs)
    pairs={}
    at=0
    for name,ref in (("g",fg),("u",fu),("d",fd),("q",fq),("o",fo)):
        pairs[name]=(ref,grads.at[:,at:at+ref.shape[-1]])
        at+=ref.shape[-1]
    finals={k:remote(a,b,fin_s.at[i],fin_r.at[i],diag) for i,(k,(a,b)) in enumerate(pairs.items())}
    def give(*names):
        @pl.when(own)
        def _():
            for k in names: pairs[k][1][...]=pairs[k][0][...]
        @pl.when(jnp.logical_not(own))
        def _():
            for k in names: finals[k].start()
    def run(*steps):
        for group,what,names in steps:
            for k in names.split(): getattr(group[k],what)()
    run((seconds,"start","d0 d1"))
    loads[1].wait(); loads[2].wait()
    loads[3].wait()
    run((firsts,"start","g0 g1 u0 o"))
    heads=cols//HD; P_=heads//2
    for p in range(P_):
        q_t[p]=q_s[p].T
        k_t[p]=k_s[p].T
        dm_t[p]=dm[p].T
    loads[0].wait()
    for p in range(P_):
        for half_ in range(2):
            r=slice(half_*64,half_*64+64)
            dd[2*p+half_:2*p+half_+1,:]=jnp.sum(dm_t[p,r,:].astype(f32)*dq_t[p,r,:],0,keepdims=True)
    dk_s[...]=jnp.zeros_like(dk_s); dv_s[...]=jnp.zeros_like(dv_s)
    loads[4].wait(); loads[5].wait()
    sc=HD**-0.5
    width=tok_t.shape[0]; quarter=width//4; hp=P_*128; part=hp//2
    def raw_grads(half_):
        for p in range(half_*P_//2,(half_+1)*P_//2):
            dqkv[0,:,p*128:p*128+128]=rope_back(dq_t[p].T*sc,cos[...],sin[...]).astype(bf)
            dqkv[1,:,p*128:p*128+128]=rope_back(dk_s[p]*sc,cos[...],sin[...]).astype(bf)
            dqkv[2,:,p*128:p*128+128]=dv_s[p].astype(bf)
    def weight_grads(half_):
        ga=(ga0,ga1)[half_]
        w=ga.shape[-1]; hc=cols//2
        maps=[]
        for j in range(3):
            rr=lax.broadcasted_iota(jnp.int32,(part,w),0); cc=lax.broadcasted_iota(jnp.int32,(part,w),1)
            hh=rr//64; dd_=rr-hh*64
            maps.append(jnp.where((dd_<HD)&(cc==j*hc+hh*HD+dd_),1.0,0.0).astype(bf))
        def body(i,_):
            r=pl.ds(pl.multiple_of(i*quarter,quarter),quarter)
            t=0.0
            for j in range(3):
                t=t+dot(dot(tok_t[r,:],dqkv[j,:,half_*part:(half_+1)*part]).astype(bf),maps[j])
            ga[i]=t.astype(bf).reshape(2,2,quarter//4,w)
            return 0
        lax.fori_loop(0,4,body,0)
    def middle():
        raw_grads(0)
        weight_grads(0)
    events={0:[lambda: run((seconds,"finish","d0 d1"),(thirds,"start","d0 d1"),(firsts,"finish","g0"),(seconds,"start","g0"),(firsts,"start","u1"))],
        2:[lambda: run((firsts,"finish","u0 g1"),(seconds,"start","u0 g1"))],
        3:[lambda: run((thirds,"finish","d0 d1")),lambda: give("d"),lambda: run((seconds,"finish","g0"),(thirds,"start","g0")),middle,lambda: run((firsts,"start","h0"))],
        4:[lambda: run((seconds,"finish","g1"),(thirds,"start","g1"),(firsts,"finish","o"),(seconds,"start","o"))],
        5:[lambda: run((firsts,"finish","u1"),(seconds,"start","u1"),(thirds,"finish","g0 g1")),lambda: give("g")],
        6:[lambda: run((seconds,"finish","u0"),(thirds,"start","u0"))],
        7:[lambda: run((firsts,"finish","h0"),(seconds,"start","h0"),(seconds,"finish","o"),(thirds,"start","o"))]}
    def body(h,_):
        for i in range(n//QB):
            bwd_head(h,i,q_t,q_s,k_s,k_t,v_s,dm_t,dm,lse,dd,start,dq_t,dk_s,dv_s)
        for at,calls in events.items():
            @pl.when(h==at)
            def _():
                for call in calls: call()
        return 0
    lax.fori_loop(0,heads,body,0)
    raw_grads(1)
    nb=n//QB
    def cross(b): return remote(term.at[b],other.at[b],core_s.at[b],core_r.at[b],{"c":1-c})
    def far(b): return remote(term.at[b],gtok.at[b],far_s.at[b],far_r.at[b],diag)
    def near(b): return pltpu.make_async_copy(term.at[b],gtok.at[b],far_r.at[b])
    def fetch(b): return pltpu.make_async_copy(d_one.at[b],d_buf.at[lax.rem(b,2)],d_sem.at[lax.rem(b,2)])
    fetch(0).start(); fetch(1).start()
    def make(b,_):
        rows=pl.ds(pl.multiple_of(b*QB,QB),QB)
        t=dot(dqkv[0,rows,:],wt[0])+dot(dqkv[1,rows,:],wt[1])+dot(dqkv[2,rows,:],wt[2])
        term[b]=t.astype(bf)
        cross(b).start()
        return 0
    lax.fori_loop(0,nb,make,0)
    def total(b,_):
        cross(b).wait_recv()
        cross(b).wait_send()
        fetch(b).wait()
        term[b]=(d_buf[lax.rem(b,2)]+(term[b].astype(f32)+other[b].astype(f32))).astype(bf)
        @pl.when(b+2<nb)
        def _():
            fetch(b+2).start()
        @pl.when(own)
        def _():
            near(b).start()
        @pl.when(jnp.logical_not(own))
        def _():
            far(b).start()
        return 0
    lax.fori_loop(0,2,total,0)
    weight_grads(1)
    run((firsts,"start","h1a h1b"),(seconds,"finish","h0"),(thirds,"start","h0"),(seconds,"finish","u1"),(thirds,"start","u1"))
    lax.fori_loop(2,4,total,0)
    run((thirds,"finish","u0 o"))
    give("o")
    run((firsts,"finish","h1a"),(seconds,"start","h1a"))
    lax.fori_loop(4,nb,total,0)
    run((firsts,"finish","h1b"),(seconds,"start","h1b"),(thirds,"finish","u1 h0"))
    give("u")
    hc=cols//2; hw=fh0.shape[-1]
    rr=lax.broadcasted_iota(jnp.int32,(hw,3*cols),0); cc=lax.broadcasted_iota(jnp.int32,(hw,3*cols),1)
    jj=cc//cols
    def sort(half_): return jnp.where((rr==jj*hc+cc-jj*cols-half_*hc)&(cc-jj*cols>=half_*hc)&(cc-jj*cols<(half_+1)*hc),1.0,0.0).astype(bf)
    low=dot(fh0[...],sort(0)); last_map=sort(1)
    run((seconds,"finish","h1a"),(thirds,"start","h1a"),(seconds,"finish","h1b"),(thirds,"start","h1b"),(thirds,"finish","h1a h1b"))
    fq[...]=(low+dot(fh1[...],last_map)).astype(bf)
    give("q")
    for group in (firsts,seconds,thirds):
        for x in group.values(): x.drain()
    def drain(b,_):
        @pl.when(own)
        def _():
            near(b).wait()
        @pl.when(jnp.logical_not(own))
        def _():
            far(b).wait_recv()
            far(b).wait_send()
        return 0
    lax.fori_loop(0,nb,drain,0)
    @pl.when(jnp.logical_not(own))
    def _():
        for x in finals.values():
            x.wait_recv()
            x.wait_send()

def fused_bwd(q_s,k_s,v_s,m_t,dm,lse,start,cos,sin,gg,gu,gow,d0,d1,tok_t,wt,d_one,cols):
    pr,n,_=q_s.shape; heads=2*pr; width=tok_t.shape[0]; nb=n//QB
    V=pl.BlockSpec(memory_space=pltpu.VMEM); A=pl.BlockSpec(memory_space=pl.ANY)
    S=jax.ShapeDtypeStruct
    ff=gg.shape[-1]; r=gg.shape[-2]; w=gow.shape[-1]; h=ff//2; hw=-(-3*cols//2//128)*128
    vm=pltpu.VMEM
    dma=lambda k: pltpu.SemaphoreType.DMA((k,))
    blocks=(nb,QB,width)
    like=lambda a: vm(a.shape,a.dtype)
    one=lambda k: [vm((4,2,r,k),bf),dma(2)]
    two=lambda k: [vm((4,r,k),bf),dma(2)]
    three=lambda k: [vm((3,r,k),bf),dma(3),dma(3)]
    by_z=lambda k: [vm((2,r,k),bf),vm((3,2,r,k),bf),dma(3),dma(3),vm((r,k),bf),dma(2)]
    return pl.pallas_call(functools.partial(fused_bwd_kernel,n,cols),
      out_shape=[S((r,3*ff+3*cols+w),bf),S(blocks,bf)],
      in_specs=[V]*10+[A]*7,out_specs=[V,A],
      scratch_shapes=[vm((pr,128,n),bf)]*3+[vm((pr,128,n),f32),vm((pr,n,128),f32),vm((pr,n,128),f32),vm((heads,n),f32),vm((3,n,pr*128),bf),
        like(gg),like(gu),like(gow),like(tok_t),like(wt),vm((2,QB,width),f32),vm((4,2,2,r,hw),bf),vm((4,2,2,r,hw),bf)]+[vm(blocks,bf)]*2
        +[dma(6),dma(2)]+[dma(nb)]*4+[dma(5),dma(5)]
        +[vm((r,ff),bf)]*3+[vm((r,w),bf)]+[vm((r,hw),bf)]*2+[vm((r,3*cols),bf)]
        +one(h)*4+one(w)+one(hw)+one(256)+one(hw-256)+by_z(256)+by_z(hw-256)+(two(h)+three(h))*6+two(w)+three(w)+two(hw)+three(hw),
      compiler_params=pltpu.CompilerParams(vmem_limit_bytes=64<<20,collective_id=1,has_side_effects=True),name="attn_bwd_reduce")(
        q_s,k_s,v_s,dm,lse,start,cos,sin,d0,d1,m_t,gg,gu,gow,tok_t,wt,d_one.reshape(blocks))

def dot_nt_t(a,b,put):
    return dot(dot(a,b).astype(bf),put).astype(bf)

NORM_EPS=1e-05
DIAG=[(0,0),(3,3),(1,2),(2,1)]
CORE=[(0,1),(1,0)]

def cross_copies(n,part,other,send,recv,c):
    def one(b): return pltpu.make_async_remote_copy(src_ref=part.at[b],dst_ref=other.at[b],send_sem=send.at[b],recv_sem=recv.at[b],device_id={"c":1-c},device_id_type=MESH)
    return one

def norm_of(r):
    inv=lax.rsqrt(jnp.mean(r*r,-1,keepdims=True)+NORM_EPS)
    return r*inv,inv

def norm_back(e,nrm,inv):
    return inv*(e-nrm*jnp.mean(e*nrm,-1,keepdims=True))

def ffn_kernel(n,cols,tok,og,mixed,ofull,wg,wu,wd,ga,gb,output,gg,gu,d_one,dm,gow,one0,one1,
        out_t,t1,t2,act,normed,inv1,hb_t,dff_t,part,oa,of,oh,summed,gsum,gd,og_s,og_r,a_s,a_r,f_s,f_r,h_s,h_r,x_s,x_r,s0,s1):
    z,y,m=place(); c=lax.axis_index("c")
    own=c==m
    greet(peers(z,y,m)+both(c,m))
    nb=n//QB
    grad_far=pltpu.make_async_remote_copy(src_ref=og,dst_ref=summed,send_sem=og_s,recv_sem=og_r,device_id={"c":1-c},device_id_type=MESH)
    grad_near=pltpu.make_async_copy(og,summed,og_r)
    def rows_of(b): return pl.ds(pl.multiple_of(b*QB,QB),QB)
    ca,cf,ch=[cross_copies(n,part,o,ss,rs,c) for o,ss,rs in ((oa,a_s,a_r),(of,f_s,f_r),(oh,h_s,h_r))]
    def far(b): return pltpu.make_async_remote_copy(src_ref=summed.at[b],dst_ref=output.at[b],send_sem=x_s.at[b],recv_sem=x_r.at[b],device_id={"c":1-c,"m":1-m},device_id_type=MESH)
    def near(b): return pltpu.make_async_copy(summed.at[b],output.at[b],x_r.at[b])
    out_t[...]=dot_nt(ofull[...],spread(cols//HD*64,cols,False)).astype(bf)
    def attn_part(b,_):
        part[b]=dot_nt(mixed[rows_of(b),:],out_t[...]).astype(bf)
        ca(b).start()
        return 0
    lax.fori_loop(0,nb,attn_part,0)
    @pl.when(own)
    def _():
        grad_far.start()
        grad_near.start()
    def forward(b,_):
        rows=rows_of(b)
        ca(b).wait_recv()
        r=tok[rows,:].astype(f32)+(part[b].astype(f32)+oa[b].astype(f32))
        nrm,inv=norm_of(r)
        normed[rows,:]=nrm
        inv1[rows,:]=inv
        hb=(nrm*ga[...]).astype(bf)
        hb_t[:,rows]=hb.T
        gate=dot(hb,wg[...]); up=dot(hb,wu[...])
        sg=jax.nn.sigmoid(gate)
        gs=gate*sg
        a=(gs*up).astype(bf)
        act[rows,:]=a
        t2[rows,:]=gs.astype(bf)
        t1[rows,:]=(up*sg*(1.0+gate*(1.0-sg))).astype(bf)
        ca(b).wait_send()
        part[b]=dot_nt(a,wd[...]).astype(bf)
        cf(b).start()
        return 0
    lax.fori_loop(0,nb,forward,0)
    @pl.when(own)
    def _():
        grad_near.wait()
        grad_far.wait_send()
    @pl.when(jnp.logical_not(own))
    def _():
        grad_far.wait_recv()
    gsum[...]=jnp.zeros_like(gsum)
    def fold(v): return jnp.sum(v.reshape(QB//8,8,v.shape[-1]),0)
    def norm_two(b,_):
        rows=rows_of(b)
        cf(b).wait_recv()
        nrm,inv=norm_of(normed[rows,:]*ga[...]+(part[b].astype(f32)+of[b].astype(f32)))
        g=summed[b].astype(f32)
        summed[b]=(nrm*gb[...]).astype(bf)
        @pl.when(own)
        def _():
            near(b).start()
        @pl.when(jnp.logical_not(own))
        def _():
            far(b).start()
        gsum[8:16,:]+=fold(g*nrm)
        d2=norm_back(g*gb[...],nrm,inv)
        d_one[rows,:]=d2
        df=d2.astype(bf)
        oa[b]=df
        dff_t[:,rows]=df.T
        return 0
    lax.fori_loop(0,nb,norm_two,0)
    width=hb_t.shape[0]; quarter=width//4; ff=act.shape[1]
    def rows4(i): return pl.ds(pl.multiple_of(i*quarter,quarter),quarter)
    def down_grad(i,_):
        gd[i]=dot(dff_t[rows4(i),:],act[...]).astype(bf).reshape(2,2,quarter//4,ff)
        return 0
    lax.fori_loop(0,4,down_grad,0)
    h2=ff//2
    ch2=[First(gd.at[:,:,:,:,0:h2],one0,s0),First(gd.at[:,:,:,:,h2:ff],one1,s1)]
    for x in ch2: x.start()
    def backward(b,_):
        rows=rows_of(b)
        da=dot(oa[b],wd[...])
        dg=(da*t1[rows,:].astype(f32)).astype(bf); du=(da*t2[rows,:].astype(f32)).astype(bf)
        t1[rows,:]=dg; t2[rows,:]=du
        cf(b).wait_send()
        part[b]=(dot_nt(dg,wg[...])+dot_nt(du,wu[...])).astype(bf)
        ch(b).start()
        return 0
    lax.fori_loop(0,nb,backward,0)
    def grads(i,_):
        gg[i]=dot(hb_t[rows4(i),:],t1[...]).astype(bf).reshape(2,2,quarter//4,ff)
        gu[i]=dot(hb_t[rows4(i),:],t2[...]).astype(bf).reshape(2,2,quarter//4,ff)
        return 0
    lax.fori_loop(0,4,grads,0)
    def last(b,_):
        rows=rows_of(b)
        ch(b).wait_recv()
        dh=d_one[rows,:]+(part[b].astype(f32)+oh[b].astype(f32))
        nrm=normed[rows,:]
        gsum[0:8,:]+=fold(dh*nrm)
        d1=norm_back(dh*ga[...],nrm,inv1[rows,:])
        d_one[rows,:]=d1
        da=d1.astype(bf)
        hb_t[:,rows]=da.T
        back=dot(da,out_t[...]).astype(bf)
        for p in range(dm.shape[0]): dm[p,rows,:]=back[:,p*128:p*128+128]
        return 0
    lax.fori_loop(0,nb,last,0)
    put=spread(cols//HD*64,cols,False)
    def out_grads(i,_):
        gow[i,:,:,:,128:128+cols]=dot_nt_t(hb_t[rows4(i),:],mixed[...],put).reshape(2,2,quarter//4,cols)
        return 0
    lax.fori_loop(0,4,out_grads,0)
    line=lax.broadcasted_iota(jnp.int32,(128,width),0)
    both_gains=jnp.where(line==0,jnp.sum(gsum[0:8,:],0,keepdims=True),jnp.where(line==1,jnp.sum(gsum[8:16,:],0,keepdims=True),0.0))
    gow[:,:,:,:,0:128]=both_gains.T.astype(bf).reshape(4,2,2,quarter//4,128)
    for x in ch2: x.finish()
    for x in ch2: x.drain()
    def drain(b,_):
        ch(b).wait_send()
        @pl.when(own)
        def _():
            near(b).wait()
        @pl.when(jnp.logical_not(own))
        def _():
            far(b).wait_recv()
            far(b).wait_send()
        return 0
    lax.fori_loop(0,nb,drain,0)

def ffn_call(tok,og,mixed,ofull,wg,wu,wd,ga,gb,cols):
    n,width=tok.shape; ff=wg.shape[1]; hp=mixed.shape[1]; nb=n//QB
    V=pl.BlockSpec(memory_space=pltpu.VMEM); A=pl.BlockSpec(memory_space=pl.ANY)
    S=jax.ShapeDtypeStruct
    blocks=(nb,QB,width); r=width//16
    dma=pltpu.SemaphoreType.DMA((nb,))
    vm=pltpu.VMEM
    return pl.pallas_call(functools.partial(ffn_kernel,n,cols),
      out_shape=[S(blocks,bf)]+[S((4,2,2,r,ff),bf)]*2+[S((n,width),f32),S((hp//128,n,128),bf),S((4,2,2,r,cols+128),bf)]+[S((4,2,r,ff//2),bf)]*2,
      in_specs=[V,A]+[V]*7,out_specs=[A]+[V]*7,
      scratch_shapes=[vm((width,hp),bf),vm((n,ff),bf),vm((n,ff),bf),vm((n,ff),bf),vm((n,width),f32),vm((n,1),f32),vm((width,n),bf),vm((width,n),bf),
        vm(blocks,bf),vm(blocks,bf),vm(blocks,bf),vm(blocks,bf),vm(blocks,bf),vm((16,width),f32),vm((4,2,2,r,ff),bf),
        pltpu.SemaphoreType.DMA,pltpu.SemaphoreType.DMA]+[dma]*8+[pltpu.SemaphoreType.DMA((2,))]*2,
      compiler_params=pltpu.CompilerParams(vmem_limit_bytes=64<<20,collective_id=3,has_side_effects=True),name="ffn")(
        tok,og.reshape(blocks),mixed,ofull,wg,wu,wd,ga,gb)

def rms_forward(resid):
    inverse=lax.rsqrt(jnp.mean(resid*resid,-1,keepdims=True)+NORM_EPS)
    return (resid*inverse,inverse)

def rms_backward(grad_normed,normed,inverse):
    return inverse*(grad_normed-normed*jnp.mean(grad_normed*normed,-1,keepdims=True))

def doc_starts(lengths,n):
    at=jnp.arange(n,dtype=jnp.int32); start=jnp.zeros((n,),jnp.int32); end=jnp.int32(0)
    for i in range(lengths.shape[0]-1):
        end=end+lengths[i]
        start=jnp.where(at>=end,end,start)
    return start

def rope_tables(positions):
    lane=jnp.arange(128,dtype=jnp.int32)%64
    fr=jnp.where(lane<HD,jnp.exp((lane%(HD//2)).astype(f32)*(-2.0*math.log(10000.0)/HD)),0.0)
    a=positions.astype(f32)[:,None]*fr[None,:]
    return jnp.cos(a),jnp.sin(a)

def core_sum(part):
    return part.astype(f32)+lax.ppermute(part,"c",CORE).astype(f32)

def on_device(tokens,out_grad,doc_lengths,w_query,w_key,w_value,w_out,gain_one,w_gate,w_up,w_down,gain_two):
    cols=w_query.shape[1]; n,width=tokens.shape
    if lax.axis_size("q")==8 and lax.axis_size("m")==2 and w_query.shape[0]==48:
        tokens,cos,sin,q,k,v,tok_t,wt,start,gain_a,gain_b,ofull,gate_w,up_w,down_t,m_t,mixed,lse=fused_fwd(
            doc_lengths,tokens,w_query,w_key,w_value,w_out.T,w_gate,w_up,w_down.T,gain_one,gain_two)
        ofull,gate_w,up_w,down_t=[a.reshape(width,a.shape[-1]) for a in (ofull,gate_w,up_w,down_t)]
        output,gg,gu,d_one,dm,gow,*downs=ffn_call(tokens,out_grad,mixed,ofull,gate_w,up_w,down_t,gain_a,gain_b,cols)
        grads,gtok=fused_bwd(q,k,v,m_t,dm,lse,start,cos,sin,gg,gu,gow,*downs,tok_t,wt,d_one,cols)
        ff=w_gate.shape[1]
        got,at=[],0
        for wide in (ff,ff,ff,cols,cols,cols,128,cols):
            got.append(grads[:,at:at+wide].astype(f32))
            at+=wide
        sgate,sup,sdown,sq,sk,sv,sgain,sout=got
        return (output.reshape(n,width),gtok.astype(f32).reshape(n,width),sq,sk,sv,sout.T,sgain[:,0],sgate,sup,sdown.T,sgain[:,1])
    own=lax.axis_index("c")==lax.axis_index("m")
    pick=lambda a: jnp.where(own,a,lax.ppermute(a,"c",CORE))
    tokens,out_grad,doc_lengths=pick(tokens),pick(out_grad),pick(doc_lengths)
    start=doc_starts(doc_lengths[0],n)
    cos,sin=rope_tables(jnp.arange(n,dtype=jnp.int32)-start)
    start=start[None]
    ff=w_gate.shape[1]
    cast=lambda a: a.astype(bf)
    gains=jnp.pad(jnp.stack([cast(gain_one),cast(gain_two)],1),((0,0),(0,126)))
    apack=jnp.concatenate([cast(w_query),cast(w_key),cast(w_value),gains],1)
    def gather(a):
        return lax.all_gather(lax.ppermute(a,("c","m"),DIAG),("q","m"),axis=0,tiled=True)
    afull,ofull,gate_w,up_w,down_t=[gather(a) for a in (apack,cast(w_out).T,cast(w_gate),cast(w_up),cast(w_down).T)]
    q,k,v,m_t,mixed,lse=attn_fwd(tokens,afull[:,:3*cols],cos,sin,start)
    put=spread(cols//HD*64,cols,False)
    out_t=dot_nt(ofull,put).astype(bf)
    gain_a=afull[:,3*cols].astype(f32); gain_b=afull[:,3*cols+1].astype(f32)
    attn=core_sum(dot_nt(mixed,out_t).astype(bf))
    normed_one,inv_one=rms_forward(tokens.astype(f32)+attn)
    hidden=normed_one*gain_a
    hb=hidden.astype(bf)
    gate=dot(hb,gate_w); up=dot(hb,up_w)
    sg=jax.nn.sigmoid(gate)
    act=(gate*sg*up).astype(bf)
    ffn=core_sum(dot_nt(act,down_t).astype(bf))
    normed_two,inv_two=rms_forward(hidden+ffn)
    output=(normed_two*gain_b).astype(bf)
    g=out_grad.astype(f32)
    g_gain_two=jnp.sum(g*normed_two,0)
    d_two=rms_backward(g*gain_b,normed_two,inv_two)
    d_ffn=d_two.astype(bf)
    tn=lambda a,b: lax.dot_general(a,b,(((0,),(0,)),((),())),preferred_element_type=f32)
    d_act=dot(d_ffn,down_t)
    d_up=(d_act*gate*sg).astype(bf)
    d_gate=(d_act*up*sg*(1.0+gate*(1.0-sg))).astype(bf)
    hterm=(dot_nt(d_gate,gate_w)+dot_nt(d_up,up_w)).astype(bf)
    gff=[tn(hb,d_gate).astype(bf),tn(hb,d_up).astype(bf),tn(d_ffn,act).astype(bf)]
    d_hidden=d_two+core_sum(hterm)
    g_gain_one=jnp.sum(d_hidden*normed_one,0)
    d_one=rms_backward(d_hidden*gain_a,normed_one,inv_one)
    d_attn=d_one.astype(bf)
    dm=dot(d_attn,out_t).astype(bf)
    output=jnp.where(own,output,lax.ppermute(output,("c","m"),[(1,2),(2,1)]))

    ggain=jnp.pad(jnp.stack([g_gain_one,g_gain_two],1),((0,0),(0,126))).astype(bf)
    dqkv=attn_bwd(q,k,v,m_t,dm,lse,start,cos,sin)
    term=0.0; gqkv=[]
    for j in range(3):
        wp=dot_nt(afull[:,j*cols:(j+1)*cols],put).astype(bf)
        term=term+dot_nt(dqkv[j],wp)
        gqkv.append(dot(tn(tokens,dqkv[j]).astype(bf),put).astype(bf))
    gtok=(d_one+core_sum(term.astype(bf))).astype(bf)
    gtok=lax.ppermute(gtok,("c","m"),DIAG).astype(f32)
    g_out=dot(tn(d_attn,mixed).astype(bf),put).astype(bf)
    gatt=jnp.concatenate([ggain,g_out]+gqkv,1)
    add=lambda a: lax.psum_scatter(a,("q","m"),scatter_dimension=0,tiled=True)
    sff,sat=[add(a) for a in gff],add(gatt)
    sff,sat=lax.ppermute(jnp.concatenate(sff,1),("c","m"),DIAG).astype(f32),lax.ppermute(sat,("c","m"),DIAG).astype(f32)
    piece=lambda j: sat[:,128+j*cols:128+(j+1)*cols]
    return (output,gtok,piece(1),piece(2),piece(3),piece(0).T,sat[:,0],sff[:,:ff],sff[:,ff:2*ff],sff[:,2*ff:].T,sat[:,1])

def solution(mesh):
    dp,mp=mesh.shape["dp"],mesh.shape["mp"]
    fine=Mesh(mesh.devices.reshape(dp//2,2,mp),("q","c","m"))
    d=("q","c")
    rows,cols_=P(d,"m"),P("m",d)
    return jax.shard_map(on_device,mesh=fine,
        in_specs=(P(d,None),P(d,None),P(d,None),rows,rows,rows,cols_,P(d),rows,rows,cols_,P(d)),
        out_specs=(P(d,None),P(d,None),rows,rows,rows,cols_,P(d),rows,rows,cols_,P(d)),check_vma=False)
```

```python
import functools
import math
import jax
import jax.numpy as jnp
import numpy as np
from jax import lax
from jax.experimental import pallas as pl
from jax.experimental.pallas import tpu as pltpu
from jax.sharding import Mesh, PartitionSpec as P
MESH=pl.DeviceIdType.MESH
HD=48
C2=HD**-0.5*math.log2(math.e)
NEG=-1e30
bf=jnp.bfloat16; f32=jnp.float32
QB=256; LOOK=4
NT=(((1,),(1,)),((),()))
def dot(a,b): return jnp.dot(a,b,preferred_element_type=f32)
def dot_nt(a,b): return lax.dot_general(a,b,NT,preferred_element_type=f32)

def spread(rows, cols, rot):
    r=lax.broadcasted_iota(jnp.int32,(rows,cols),0); c=lax.broadcasted_iota(jnp.int32,(rows,cols),1)
    h=r//64; d=r-h*64
    if not rot:
        return jnp.where((d<HD)&(c==h*HD+d),1.0,0.0).astype(bf)
    lo=(d<24)&(c==h*HD+d+24); hi=(d>=24)&(d<HD)&(c==h*HD+d-24)
    return jnp.where(lo,-1.0,jnp.where(hi,1.0,0.0)).astype(bf)

def proj_weights(w,wq_s,cols):
    hp=cols//HD*64
    for m,(col,rot) in enumerate(((0,False),(0,True),(1,False),(1,True),(2,False))):
        if len(w.shape)==2:
            part=w[:,col*cols:(col+1)*cols]
        else:
            part=w[:,:,:,:,col*cols:(col+1)*cols].reshape(-1,cols)
        wq_s[m]=dot_nt(spread(hp,cols,rot),part).astype(bf)

def proj(tok,cos,sin,wq_s,q_s,k_s,v_s,lo,hi):
    def body(b,_):
        rows=pl.ds(pl.multiple_of(b*QB,QB),QB)
        x=tok[rows,:]
        cs=cos[rows,:]; sn=sin[rows,:]
        for dst,a in ((q_s,0),(k_s,2)):
            raw=dot_nt(x,wq_s[a]); rt=dot_nt(x,wq_s[a+1])
            for p in range(dst.shape[0]):
                l=slice(p*128,p*128+128)
                dst[p,rows,:]=(raw[:,l]*cs+rt[:,l]*sn).astype(bf)
        raw=dot_nt(x,wq_s[4])
        for p in range(v_s.shape[0]):
            v_s[p,rows,:]=raw[:,p*128:p*128+128].astype(bf)
        return 0
    lax.fori_loop(lo,hi,body,0)

def masks(kk0,nk,i,start):
    kidx=lax.broadcasted_iota(jnp.int32,(nk,QB),0)+kk0
    ok=kidx>=start
    qidx=lax.broadcasted_iota(jnp.int32,(nk,QB),1)+i*QB
    return ok&(kidx<=qidx)

def fwd_head(h,i,q_t,k_s,v_t,start,m_t,lse):
    p=h//2; half=h-2*p
    lo=max(0,i-LOOK)*QB; nk=(i+1)*QB-lo
    kk=slice(lo,lo+nk); qq=slice(i*QB,(i+1)*QB)
    row=lax.broadcasted_iota(jnp.int32,(128,QB),0)
    mine=(row>=half*64)&(row<half*64+64)
    qt=jnp.where(mine,q_t[p,:,qq],jnp.zeros((),bf))
    s=dot(k_s[p,kk,:],qt)
    st=start[:,qq]
    s=jnp.where(masks(lo,nk,i,st),s,NEG)
    m=jnp.max(s,0,keepdims=True)
    e=jnp.exp2((s-m)*C2)
    l=jnp.sum(e,0,keepdims=True)
    pr=(e*(1.0/l)).astype(bf)
    rows=pl.ds(pl.multiple_of(half*64,64),64)
    m_t[p,rows,qq]=dot(v_t[p,rows,kk],pr)
    lse[pl.ds(h,1),qq]=m*C2+jnp.log2(l)

def fwd_kernel(n,cols,tok,w,cos,sin,start,q_o,k_o,v_o,m_t,mixed,lse,wq_s,q_t,v_t):
    proj_weights(w,wq_s,cols)
    proj(tok,cos,sin,wq_s,q_o,k_o,v_o,0,n//QB)
    heads=cols//HD
    for p in range(heads//2):
        q_t[p]=q_o[p].T
        v_t[p]=v_o[p].T
    def body(h,_):
        for i in range(n//QB):
            fwd_head(h,i,q_t,k_o,v_t,start,m_t,lse)
        return 0
    lax.fori_loop(0,heads,body,0)
    for p in range(heads//2):
        mixed[:,p*128:p*128+128]=m_t[p].T.astype(bf)

def attn_fwd(tok,w,cos,sin,start):
    n=tok.shape[0]; cols=w.shape[1]//3; heads=cols//HD; P=heads//2
    V=pl.BlockSpec(memory_space=pltpu.VMEM)
    S=jax.ShapeDtypeStruct
    return pl.pallas_call(functools.partial(fwd_kernel,n,cols),
      out_shape=(S((P,n,128),bf),S((P,n,128),bf),S((P,n,128),bf),S((P,128,n),f32),S((n,P*128),bf),S((heads,n),f32)),
      in_specs=[V]*5,out_specs=[V]*6,
      scratch_shapes=[pltpu.VMEM((5,P*128,w.shape[0]),bf),pltpu.VMEM((P,128,n),bf),pltpu.VMEM((P,128,n),bf)],
      compiler_params=pltpu.CompilerParams(vmem_limit_bytes=60<<20),name="attn_fwd")(tok,w,cos,sin,start)

def bwd_head(h,i,q_t,q_s,k_s,k_t,v_s,dm_t,dm_s,lse,dd,start,dq_t,dk_s,dv_s):
    p=h//2; half=h-2*p
    lo=max(0,i-LOOK)*QB; nk=(i+1)*QB-lo
    kk=slice(lo,lo+nk); qq=slice(i*QB,(i+1)*QB)
    row=lax.broadcasted_iota(jnp.int32,(128,QB),0)
    mine=(row>=half*64)&(row<half*64+64)
    lane=lax.broadcasted_iota(jnp.int32,(QB,128),1)
    mlane=(lane>=half*64)&(lane<half*64+64)
    zero=jnp.zeros((),bf)
    qt=jnp.where(mine,q_t[p,:,qq],zero)
    dmt=jnp.where(mine,dm_t[p,:,qq],zero)
    qn=jnp.where(mlane,q_s[p,qq,:],zero)
    dmn=jnp.where(mlane,dm_s[p,qq,:],zero)
    s=dot(k_s[p,kk,:],qt)
    st=start[:,qq]
    pr=jnp.exp2(jnp.where(masks(lo,nk,i,st),s*C2,NEG)-lse[pl.ds(h,1),qq])
    dp=dot(v_s[p,kk,:],dmt)
    ds=(pr*(dp-dd[pl.ds(h,1),qq])).astype(bf)
    pb=pr.astype(bf)
    dv_s[p,kk,:]+=dot(pb,dmn)
    dk_s[p,kk,:]+=dot(ds,qn)
    rows=pl.ds(pl.multiple_of(half*64,64),64)
    dq_t[p,rows,qq]=dot(k_t[p,rows,kk],ds)

def rope_back(u,cs,sn):
    w=u*sn
    lane=lax.broadcasted_iota(jnp.int32,u.shape,1)&63
    up=pltpu.roll(w,128-24,axis=1); dn=pltpu.roll(w,24,axis=1)
    return u*cs+jnp.where(lane<24,up,jnp.where(lane<48,-dn,0.0))

def bwd_kernel(n,heads,q_s,k_s,v_s,m_t,dm,lse,start,cos,sin,dqkv,q_t,k_t,dm_t,dm_s,dq_t,dk_s,dv_s,dd):
    P=heads//2
    for p in range(P):
        q_t[p]=q_s[p].T
        k_t[p]=k_s[p].T
        dm_s[p]=dm[:,p*128:p*128+128]
        dm_t[p]=dm_s[p].T
        for half in range(2):
            r=slice(half*64,half*64+64)
            dd[2*p+half:2*p+half+1,:]=jnp.sum(dm_t[p,r,:].astype(f32)*m_t[p,r,:],0,keepdims=True)
    dk_s[...]=jnp.zeros_like(dk_s); dv_s[...]=jnp.zeros_like(dv_s)
    def body(h,_):
        for i in range(n//QB):
            bwd_head(h,i,q_t,q_s,k_s,k_t,v_s,dm_t,dm_s,lse,dd,start,dq_t,dk_s,dv_s)
        return 0
    lax.fori_loop(0,heads,body,0)
    sc=HD**-0.5
    for p in range(P):
        dqkv[0,:,p*128:p*128+128]=rope_back(dq_t[p].T*sc,cos[...],sin[...]).astype(bf)
        dqkv[1,:,p*128:p*128+128]=rope_back(dk_s[p]*sc,cos[...],sin[...]).astype(bf)
        dqkv[2,:,p*128:p*128+128]=dv_s[p].astype(bf)

def attn_bwd(q_s,k_s,v_s,m_t,dm,lse,start,cos,sin):
    P,n,_=q_s.shape; heads=2*P
    V=pl.BlockSpec(memory_space=pltpu.VMEM)
    S=jax.ShapeDtypeStruct
    return pl.pallas_call(functools.partial(bwd_kernel,n,heads),
      out_shape=S((3,n,P*128),bf),
      in_specs=[V]*9,out_specs=V,
      scratch_shapes=[pltpu.VMEM((P,128,n),bf),pltpu.VMEM((P,128,n),bf),pltpu.VMEM((P,128,n),bf),pltpu.VMEM((P,n,128),bf),pltpu.VMEM((P,128,n),f32),pltpu.VMEM((P,n,128),f32),pltpu.VMEM((P,n,128),f32),pltpu.VMEM((heads,n),f32)],
      compiler_params=pltpu.CompilerParams(vmem_limit_bytes=60<<20),name="attn_bwd")(q_s,k_s,v_s,m_t,dm,lse,start,cos,sin)


def place():
    q,m=lax.axis_index("q"),lax.axis_index("m")
    return q//2,lax.rem(q,2),m

def peers(z,y,m):
    return [{"q":z*2+1-y},{"m":1-m}]+[{"q":lax.rem(z+s,4)*2+y} for s in (1,2,3)]

def greet(where):
    barrier=pltpu.get_barrier_semaphore()
    for w in where:
        pl.semaphore_signal(barrier,inc=1,device_id=w,device_id_type=MESH)
    pl.semaphore_wait(barrier,len(where))

def remote(s,d,ss,rs,w):
    return pltpu.make_async_remote_copy(src_ref=s,dst_ref=d,send_sem=ss,recv_sem=rs,device_id=w,device_id_type=MESH)

class First:
    def __init__(self,source,one,sem,first="y"):
        self.source,self.one,self.first=source,one,first
        z,y,m=place()
        self.y,self.m=y,m
        ny,nx=peers(z,y,m)[:2]
        self.copy=remote(source.at[:,1-y],one,sem.at[0],sem.at[1],ny) if first=="y" else remote(source.at[:,:,1-m],one,sem.at[0],sem.at[1],nx)
    def start(self): self.copy.start()
    def finish(self):
        self.copy.wait_recv()
        def add(i,_):
            zz=i//2; o=i-zz*2
            mine=self.source[zz,self.y,o] if self.first=="y" else self.source[zz,o,self.m]
            self.one[zz,o]=(self.one[zz,o].astype(f32)+mine.astype(f32)).astype(bf)
            return 0
        lax.fori_loop(0,8,add,0)
    def drain(self): self.copy.wait_send()

class Second:
    def __init__(self,one,two,sem,first="y"):
        self.one,self.two=one,two
        z,y,m=place()
        ny,nx=peers(z,y,m)[:2]
        self.keep=m if first=="y" else y
        self.copy=remote(one.at[:,1-self.keep],two,sem.at[0],sem.at[1],nx if first=="y" else ny)
    def start(self): self.copy.start()
    def finish(self):
        self.copy.wait_recv()
        def add(zz,_):
            self.two[zz]=(self.two[zz].astype(f32)+self.one[zz,self.keep].astype(f32)).astype(bf)
            return 0
        lax.fori_loop(0,4,add,0)
    def drain(self): self.copy.wait_send()

class SecondZ:
    def __init__(self,one,two,three,send,recv):
        self.one,self.two,self.three=one,two,three
        z,y,m=place()
        self.z=z
        to=peers(z,y,m)
        self.copies=[remote(one.at[lax.rem(z+s,4)],three.at[s-1],send.at[s-1],recv.at[s-1],to[1+s]) for s in (1,2,3)]
    def start(self):
        for c in self.copies: c.start()
    def finish(self):
        for c in self.copies: c.wait_recv()
        for o in range(2):
            t=self.one[self.z,o].astype(f32)
            for s in range(3): t=t+self.three[s,o].astype(f32)
            self.two[o]=t.astype(bf)
    def drain(self):
        for c in self.copies: c.wait_send()

class ThirdX:
    def __init__(self,two,other,out,sem):
        self.two,self.other,self.out=two,other,out
        z,y,m=place()
        self.m=m
        self.copy=remote(two.at[1-m],other,sem.at[0],sem.at[1],{"m":1-m})
    def start(self): self.copy.start()
    def finish(self):
        self.copy.wait_recv()
        self.out[...]=(self.two[self.m].astype(f32)+self.other[...].astype(f32)).astype(bf)
    def drain(self): self.copy.wait_send()

class Third:
    def __init__(self,two,three,out,send,recv):
        self.two,self.three,self.out=two,three,out
        z,y,m=place()
        self.z=z
        to=peers(z,y,m)
        self.copies=[remote(two.at[lax.rem(z+s,4)],three.at[s-1],send.at[s-1],recv.at[s-1],to[1+s]) for s in (1,2,3)]
    def start(self):
        for c in self.copies: c.start()
    def finish(self):
        for c in self.copies: c.wait_recv()
        t=self.two[self.z].astype(f32)
        for s in range(3): t=t+self.three[s].astype(f32)
        self.out[...]=t.astype(bf)
    def drain(self):
        for c in self.copies: c.wait_send()

class Gather:
    def __init__(self,shard,full,cols,stage,sem,sem_z,first):
        z,y,m=place(); c=lax.axis_index("c")
        to=peers(z,y,m)
        src=shard.at[:,cols]
        self.first=first
        self.own=c==m
        self.here=pltpu.make_async_copy(src,stage.at[z,y],sem.at[0])
        self.along=[remote(src,stage.at[z,y],sem_z.at[0,s-1],sem_z.at[1,s-1],to[1+s]) for s in (1,2,3)]
        a,b=(stage.at[:,y],full.at[:,y,c,:,cols]) if first=="x" else (stage,full.at[:,:,c,:,cols])
        self.near_self=pltpu.make_async_copy(a,b,sem.at[1])
        self.near=remote(a,b,sem.at[2],sem.at[3],{"c":1-c})
        self.far_same=remote(a,b,sem.at[4],sem.at[5],{"m":1-m})
        self.far_diag=remote(a,b,sem.at[4],sem.at[6],{"c":1-c,"m":1-m})
        d=full.at[:,y,:,:,cols] if first=="x" else stage.at[:,y]
        self.across=remote(d,d,sem.at[7],sem.at[8],to[0])
    def start(self):
        self.here.start()
        for c in self.along: c.start()
    def cross(self):
        @pl.when(self.own)
        def _():
            self.near_self.start()
            self.far_same.start()
        @pl.when(jnp.logical_not(self.own))
        def _():
            self.far_diag.start()
            self.near.start()
    def crossed(self):
        @pl.when(self.own)
        def _():
            self.near_self.wait()
            self.near.wait_recv()
        @pl.when(jnp.logical_not(self.own))
        def _():
            self.far_same.wait_recv()
            self.far_diag.wait_recv()
    def second(self):
        self.here.wait()
        for c in self.along: c.wait_recv()
        if self.first=="x": self.cross()
        else: self.across.start()
    def third(self):
        if self.first=="x":
            self.crossed()
            self.across.start()
        else:
            self.across.wait_recv()
            self.cross()
    def finish(self):
        if self.first=="x": self.across.wait_recv()
        else: self.crossed()
    def drain(self):
        for c in self.along: c.wait_send()
        self.across.wait_send()
        @pl.when(self.own)
        def _():
            self.far_same.wait_send()
        @pl.when(jnp.logical_not(self.own))
        def _():
            self.far_diag.wait_send()
            self.near.wait_send()

def both(c,m):
    return [{"c":1-c},{"c":1-c,"m":1-m}]

def fused_fwd_kernel(n,cols,lengths,freq,tok_i,wq_i,wk_i,wv_i,wo_i,wg_i,wu_i,wd_i,g1_i,g2_i,
        tok_o,cos_o,sin_o,q_o,k_o,v_o,tok_t_o,wt_o,start,ga,gb,wo,wg,wu,wd,m_t,mixed,lse,
        tok,cos,sin,q_s,k_s,v_s,tok_t,wa,wq_s,q_t,v_t,docs_i,docs,a_b,o_b,g_b,u_b,d_b,swap_s,swap_r,out_s,*scr):
    z,y,m=place(); c=lax.axis_index("c")
    own=c==m
    r=a_b.shape[0]; ff=g_b.shape[1]
    eye=(lax.broadcasted_iota(jnp.int32,(r,r),0)==lax.broadcasted_iota(jnp.int32,(r,r),1)).astype(bf)
    line=lax.broadcasted_iota(jnp.int32,(128,r),0)
    gains=jnp.where(line==0,g1_i[...],jnp.where(line==1,g2_i[...],0.0)).astype(bf)
    for j,w in enumerate((wq_i,wk_i,wv_i)): a_b[:,j*cols:(j+1)*cols]=w[...].astype(bf)
    a_b[:,3*cols:]=dot_nt(eye,gains).astype(bf)
    g_b[...]=wg_i[...].astype(bf)
    u_b[...]=wu_i[...].astype(bf)
    o_b[...]=wo_i[...].astype(bf)
    d_b[...]=wd_i[...].astype(bf)
    row=lax.broadcasted_iota(jnp.int32,(8,128),0)
    table=jnp.zeros((8,128),jnp.int32)
    for i in range(lengths.shape[1]): table=jnp.where(row==i,lengths[0,i],table)
    docs_i[...]=table
    greet(peers(z,y,m)+both(c,m))
    packs=[(docs_i,docs),(tok_i,tok)]
    swap_far=[remote(a,b,swap_s.at[i],swap_r.at[i],{"c":1-c}) for i,(a,b) in enumerate(packs)]
    swap_near=[pltpu.make_async_copy(a,b,swap_r.at[i]) for i,(a,b) in enumerate(packs)]
    scr=list(scr)
    def chunk(shard,full,lo,hi,first):
        stage,sem,sem_z=scr[:3]
        del scr[:3]
        return Gather(shard,full,slice(lo,hi),stage,sem,sem_z,first)
    cut=cuts(a_b.shape[1])
    a=[chunk(a_b,wa,cut[i],cut[i+1],"xy"[i%2]) for i in range(4)]
    h2=ff//2
    f=[chunk(b,w,j*h2,j*h2+h2,"xy"[j]) for b,w in ((g_b,wg),(u_b,wu),(d_b,wd)) for j in range(2)]
    f.append(chunk(o_b,wo,0,cols,"x"))
    for x in a: x.start()
    @pl.when(own)
    def _():
        for x,w in zip(swap_near,swap_far):
            x.start(); w.start()
        swap_near[0].wait()
    @pl.when(jnp.logical_not(own))
    def _():
        swap_far[0].wait_recv()
    for x in f: x.start()
    def begin(at):
        end=jnp.zeros((1,1),jnp.int32); first=jnp.zeros(at.shape,jnp.int32)
        for i in range(lengths.shape[1]-1):
            end=end+docs[i:i+1,0:1]
            first=jnp.where(at>=end,end,first)
        return first
    start[...]=begin(lax.broadcasted_iota(jnp.int32,(1,n),1))
    def tables(b,_):
        rows=pl.ds(pl.multiple_of(b*QB,QB),QB)
        at=lax.broadcasted_iota(jnp.int32,(QB,128),0)+b*QB
        angle=(at-begin(at)).astype(f32)*freq[...]
        cos[rows,:]=jnp.cos(angle)
        sin[rows,:]=jnp.sin(angle)
        return 0
    nb=n//QB
    lax.fori_loop(0,nb//2,tables,0)
    a[0].second(); a[1].second()
    lax.fori_loop(nb//2,nb,tables,0)
    a[0].third(); a[1].third()
    a[2].second(); a[3].second()
    keep=[pltpu.make_async_copy(v,h,out_s.at[i]) for i,(v,h) in enumerate(((cos,cos_o),(sin,sin_o),(tok,tok_o),(tok_t,tok_t_o),(wq_s.at[0],wt_o.at[0]),(wq_s.at[2],wt_o.at[1]),
        (wq_s.at[4],wt_o.at[2]),(q_s,q_o),(k_s,k_o),(v_s,v_o)))]
    keep[0].start(); keep[1].start()
    @pl.when(own)
    def _():
        swap_near[1].wait()
    @pl.when(jnp.logical_not(own))
    def _():
        swap_far[1].wait_recv()
    keep[2].start()
    half=tok_t.shape[0]//2
    tok_t[:half,:]=tok[:,:half].T
    a[2].third(); a[3].third()
    tok_t[half:,:]=tok[:,half:].T
    keep[3].start()
    for x in a: x.finish()
    f[0].second(); f[1].second()
    proj_weights(wa,wq_s,cols)
    for x in keep[4:7]: x.start()
    proj(tok,cos,sin,wq_s,q_s,k_s,v_s,0,nb//2)
    f[0].third(); f[1].third()
    f[2].second(); f[3].second()
    proj(tok,cos,sin,wq_s,q_s,k_s,v_s,nb//2,nb)
    for x in keep[7:]: x.start()
    rows=wa[:,:,:,:,3*cols:].reshape(-1,128).astype(f32).T
    ga[...]=rows[0:1,:]
    gb[...]=rows[1:2,:]
    heads=cols//HD
    for p in range(heads//2):
        q_t[p]=q_s[p].T
        v_t[p]=v_s[p].T
    plan={0:[(2,"third"),(3,"third"),(4,"second"),(5,"second")],3:[(4,"third"),(5,"third"),(6,"second")],5:[(6,"third")]}
    def body(h,_):
        for i in range(nb):
            fwd_head(h,i,q_t,k_s,v_t,start,m_t,lse)
        for at,todo in plan.items():
            @pl.when(h==at)
            def _():
                for k,what in todo: getattr(f[k],what)()
        return 0
    lax.fori_loop(0,heads,body,0)
    for p in range(heads//2):
        mixed[:,p*128:p*128+128]=m_t[p].T.astype(bf)
    for x in f: x.finish()
    for x in a+f: x.drain()
    for x in keep: x.wait()
    @pl.when(own)
    def _():
        for x in swap_far: x.wait_send()

def cuts(width):
    return [0,width//1280*384,width//2,width//2+width//1280*256,width]

def fused_fwd(lengths,tok,wq,wk,wv,w_out,wg,wu,wd,g1,g2):
    n,width=tok.shape; r,cols=wq.shape; heads=cols//HD; pr=heads//2; ff=wg.shape[1]; ac=3*cols+128
    V=pl.BlockSpec(memory_space=pltpu.VMEM); A=pl.BlockSpec(memory_space=pl.ANY); M=pl.BlockSpec(memory_space=pltpu.SMEM)
    S=jax.ShapeDtypeStruct
    vm=pltpu.VMEM
    dma=lambda *k: pltpu.SemaphoreType.DMA(k)
    wide=lambda k: S((4,2,2,r,k),bf)
    lane=np.arange(128)%64
    freq=np.where(lane<HD,np.exp((lane%(HD//2)).astype(np.float32)*np.float32(-2.0*math.log(10000.0)/HD)),0.0).astype(np.float32)[None]
    cut=cuts(ac)
    sizes=[cut[i+1]-cut[i] for i in range(4)]+[ff//2]*6+[cols]
    pair=(pr,n,128)
    return pl.pallas_call(functools.partial(fused_fwd_kernel,n,cols),
      out_shape=[S((n,width),bf),S((n,128),f32),S((n,128),f32),S(pair,bf),S(pair,bf),S(pair,bf),S((width,n),bf),S((3,pr*128,width),bf),
        S((1,n),jnp.int32),S((1,width),f32),S((1,width),f32),wide(cols),wide(ff),wide(ff),wide(ff),S((pr,128,n),f32),S((n,pr*128),bf),S((heads,n),f32)],
      in_specs=[M,V,A]+[V]*9,out_specs=[A]*8+[V]*10,
      scratch_shapes=[vm((n,width),bf),vm((n,128),f32),vm((n,128),f32),vm(pair,bf),vm(pair,bf),vm(pair,bf),vm((width,n),bf),vm((4,2,2,r,ac),bf),
        vm((5,pr*128,width),bf),vm((pr,128,n),bf),vm((pr,128,n),bf),vm((8,128),jnp.int32),vm((8,128),jnp.int32),
        vm((r,ac),bf),vm((r,cols),bf),vm((r,ff),bf),vm((r,ff),bf),vm((r,ff),bf),dma(2),dma(2),dma(10)]
        +sum([[vm((4,2,r,k),bf),dma(9),dma(2,3)] for k in sizes],[]),
      compiler_params=pltpu.CompilerParams(vmem_limit_bytes=60<<20,collective_id=0,has_side_effects=True),name="attn_fwd_gather")(
        lengths,jnp.asarray(freq),tok,wq,wk,wv,w_out,wg,wu,wd,g1[None],g2[None])

def fused_bwd_kernel(n,cols,lse,start,q_i,k_i,v_i,dm_i,cos_i,sin_i,d0_i,d1_i,m_i,g_i,u_i,o_i,tok_i,wt_i,d_one,grads,gtok,
        q_t,k_t,dm_t,dq_t,dk_s,dv_s,dd,dqkv,gg,gu,gow,tok_t,wt,d_buf,ga0,ga1,term,other,q_s,k_s,v_s,dm,cos,sin,d0,d1,load_s,d_sem,core_s,core_r,far_s,far_r,fin_s,fin_r,*scr):
    z,y,m=place(); c=lax.axis_index("c")
    own=c==m
    diag={"c":1-c,"m":1-m}
    loads=[pltpu.make_async_copy(a,b,load_s.at[i]) for i,(a,b) in enumerate(((m_i,dq_t),(g_i,gg),(u_i,gu),(o_i,gow),(tok_i,tok_t),(wt_i,wt),(d0_i,d0),(d1_i,d1),(q_i,q_s),(k_i,k_s),(dm_i,dm),(v_i,v_s),(cos_i,cos),(sin_i,sin)))]
    for i in (6,7,1,8,9,10,2,3,0,11,12,13,4,5): loads[i].start()
    greet(peers(z,y,m)+both(c,m))
    scr=list(scr)
    def take(k):
        got=scr[:k]
        del scr[:k]
        return got
    half=gg.shape[-1]//2
    ff=2*half
    fd,fg,fu,fo,fh0,fh1,fq=take(7)
    outs={"d0":fd.at[:,0:half],"d1":fd.at[:,half:ff],"g0":fg.at[:,0:half],"g1":fg.at[:,half:ff],"u0":fu.at[:,0:half],"u1":fu.at[:,half:ff],
        "o":fo,"h0":fh0,"h1a":fh1.at[:,0:256],"h1b":fh1.at[:,256:ga1.shape[-1]]}
    firsts,seconds,thirds={},{},{}
    ones={"d0":d0,"d1":d1}
    for name,src,first in (("g0",gg.at[:,:,:,:,0:half],"y"),("g1",gg.at[:,:,:,:,half:ff],"x"),("u0",gu.at[:,:,:,:,0:half],"y"),("u1",gu.at[:,:,:,:,half:ff],"x"),
            ("o",gow,"y"),("h0",ga0,"y"),("h1a",ga1.at[:,:,:,:,0:256],"y"),("h1b",ga1.at[:,:,:,:,256:ga1.shape[-1]],"y")):
        ones[name],sem=take(2)
        firsts[name]=First(src,ones[name],sem,first)
    for name in ("h1a","h1b"):
        two,three,ss,rs,came,sem=take(6)
        seconds[name]=SecondZ(ones[name],two,three,ss,rs)
        thirds[name]=ThirdX(two,came,outs[name],sem)
    for name in ("d0","d1","g0","g1","u0","u1","o","h0"):
        two,sem,three,ss,rs=take(5)
        seconds[name]=Second(ones[name],two,sem,"x" if name in ("g1","u1") else "y")
        thirds[name]=Third(two,three,outs[name],ss,rs)
    pairs={}
    at=0
    for name,ref in (("g",fg),("u",fu),("d",fd),("q",fq),("o",fo)):
        pairs[name]=(ref,grads.at[:,at:at+ref.shape[-1]])
        at+=ref.shape[-1]
    finals={k:remote(a,b,fin_s.at[i],fin_r.at[i],diag) for i,(k,(a,b)) in enumerate(pairs.items())}
    def give(*names):
        @pl.when(own)
        def _():
            for k in names: pairs[k][1][...]=pairs[k][0][...]
        @pl.when(jnp.logical_not(own))
        def _():
            for k in names: finals[k].start()
    def run(*steps):
        for group,what,names in steps:
            for k in names.split(): getattr(group[k],what)()
    loads[6].wait(); loads[7].wait()
    run((seconds,"start","d0 d1"))
    loads[1].wait()
    run((firsts,"start","g0 g1"))
    for i in (8,9,10): loads[i].wait()
    heads=cols//HD; P_=heads//2
    for p in range(P_):
        q_t[p]=q_s[p].T
        k_t[p]=k_s[p].T
        dm_t[p]=dm[p].T
    loads[2].wait(); loads[3].wait()
    run((firsts,"start","u0 o"))
    loads[0].wait()
    for p in range(P_):
        for half_ in range(2):
            r=slice(half_*64,half_*64+64)
            dd[2*p+half_:2*p+half_+1,:]=jnp.sum(dm_t[p,r,:].astype(f32)*dq_t[p,r,:],0,keepdims=True)
    dk_s[...]=jnp.zeros_like(dk_s); dv_s[...]=jnp.zeros_like(dv_s)
    for i in (4,5,11,12,13): loads[i].wait()
    sc=HD**-0.5
    width=tok_t.shape[0]; quarter=width//4; hp=P_*128; part=hp//2
    def raw_grads(half_):
        for p in range(half_*P_//2,(half_+1)*P_//2):
            dqkv[0,:,p*128:p*128+128]=rope_back(dq_t[p].T*sc,cos[...],sin[...]).astype(bf)
            dqkv[1,:,p*128:p*128+128]=rope_back(dk_s[p]*sc,cos[...],sin[...]).astype(bf)
            dqkv[2,:,p*128:p*128+128]=dv_s[p].astype(bf)
    def weight_grads(half_):
        ga=(ga0,ga1)[half_]
        w=ga.shape[-1]; hc=cols//2
        maps=[]
        for j in range(3):
            rr=lax.broadcasted_iota(jnp.int32,(part,w),0); cc=lax.broadcasted_iota(jnp.int32,(part,w),1)
            hh=rr//64; dd_=rr-hh*64
            maps.append(jnp.where((dd_<HD)&(cc==j*hc+hh*HD+dd_),1.0,0.0).astype(bf))
        def body(i,_):
            r=pl.ds(pl.multiple_of(i*quarter,quarter),quarter)
            t=0.0
            for j in range(3):
                t=t+dot(dot(tok_t[r,:],dqkv[j,:,half_*part:(half_+1)*part]).astype(bf),maps[j])
            ga[i]=t.astype(bf).reshape(2,2,quarter//4,w)
            return 0
        lax.fori_loop(0,4,body,0)
    def middle():
        raw_grads(0)
        weight_grads(0)
    events={0:[lambda: run((seconds,"finish","d0 d1"),(thirds,"start","d0 d1"),(firsts,"finish","g0"),(seconds,"start","g0"),(firsts,"start","u1"))],
        2:[lambda: run((firsts,"finish","u0 g1"),(seconds,"start","u0 g1"))],
        3:[lambda: run((thirds,"finish","d0 d1")),lambda: give("d"),lambda: run((seconds,"finish","g0"),(thirds,"start","g0")),middle,lambda: run((firsts,"start","h0"))],
        4:[lambda: run((seconds,"finish","g1"),(thirds,"start","g1"),(firsts,"finish","o"),(seconds,"start","o"))],
        5:[lambda: run((firsts,"finish","u1"),(seconds,"start","u1"),(thirds,"finish","g0 g1")),lambda: give("g")],
        6:[lambda: run((seconds,"finish","u0"),(thirds,"start","u0"))],
        7:[lambda: run((firsts,"finish","h0"),(seconds,"start","h0"),(seconds,"finish","o"),(thirds,"start","o"))]}
    def body(h,_):
        for i in range(n//QB):
            bwd_head(h,i,q_t,q_s,k_s,k_t,v_s,dm_t,dm,lse,dd,start,dq_t,dk_s,dv_s)
        for at,calls in events.items():
            @pl.when(h==at)
            def _():
                for call in calls: call()
        return 0
    lax.fori_loop(0,heads,body,0)
    raw_grads(1)
    nb=n//QB
    def cross(b): return remote(term.at[b],other.at[b],core_s.at[b],core_r.at[b],{"c":1-c})
    def far(b): return remote(term.at[b],gtok.at[b],far_s.at[b],far_r.at[b],diag)
    def near(b): return pltpu.make_async_copy(term.at[b],gtok.at[b],far_r.at[b])
    def fetch(b): return pltpu.make_async_copy(d_one.at[b],d_buf.at[lax.rem(b,2)],d_sem.at[lax.rem(b,2)])
    fetch(0).start(); fetch(1).start()
    def make(b,_):
        rows=pl.ds(pl.multiple_of(b*QB,QB),QB)
        t=dot(dqkv[0,rows,:],wt[0])+dot(dqkv[1,rows,:],wt[1])+dot(dqkv[2,rows,:],wt[2])
        term[b]=t.astype(bf)
        cross(b).start()
        return 0
    lax.fori_loop(0,nb,make,0)
    def total(b,_):
        cross(b).wait_recv()
        cross(b).wait_send()
        fetch(b).wait()
        term[b]=(d_buf[lax.rem(b,2)]+(term[b].astype(f32)+other[b].astype(f32))).astype(bf)
        @pl.when(b+2<nb)
        def _():
            fetch(b+2).start()
        @pl.when(own)
        def _():
            near(b).start()
        @pl.when(jnp.logical_not(own))
        def _():
            far(b).start()
        return 0
    lax.fori_loop(0,2,total,0)
    weight_grads(1)
    run((firsts,"start","h1a h1b"),(seconds,"finish","h0"),(thirds,"start","h0"),(seconds,"finish","u1"),(thirds,"start","u1"))
    lax.fori_loop(2,4,total,0)
    run((thirds,"finish","u0 o"))
    give("o")
    run((firsts,"finish","h1a"),(seconds,"start","h1a"))
    lax.fori_loop(4,nb,total,0)
    run((firsts,"finish","h1b"),(seconds,"start","h1b"),(thirds,"finish","u1 h0"))
    give("u")
    hc=cols//2; hw=fh0.shape[-1]
    rr=lax.broadcasted_iota(jnp.int32,(hw,3*cols),0); cc=lax.broadcasted_iota(jnp.int32,(hw,3*cols),1)
    jj=cc//cols
    def sort(half_): return jnp.where((rr==jj*hc+cc-jj*cols-half_*hc)&(cc-jj*cols>=half_*hc)&(cc-jj*cols<(half_+1)*hc),1.0,0.0).astype(bf)
    low=dot(fh0[...],sort(0)); last_map=sort(1)
    run((seconds,"finish","h1a"),(thirds,"start","h1a"),(seconds,"finish","h1b"),(thirds,"start","h1b"),(thirds,"finish","h1a h1b"))
    fq[...]=(low+dot(fh1[...],last_map)).astype(bf)
    give("q")
    for group in (firsts,seconds,thirds):
        for x in group.values(): x.drain()
    def drain(b,_):
        @pl.when(own)
        def _():
            near(b).wait()
        @pl.when(jnp.logical_not(own))
        def _():
            far(b).wait_recv()
            far(b).wait_send()
        return 0
    lax.fori_loop(0,nb,drain,0)
    @pl.when(jnp.logical_not(own))
    def _():
        for x in finals.values():
            x.wait_recv()
            x.wait_send()

def fused_bwd(q_s,k_s,v_s,m_t,dm,lse,start,cos,sin,gg,gu,gow,d0,d1,tok_t,wt,d_one,cols):
    pr,n,_=q_s.shape; heads=2*pr; width=tok_t.shape[0]; nb=n//QB
    V=pl.BlockSpec(memory_space=pltpu.VMEM); A=pl.BlockSpec(memory_space=pl.ANY)
    S=jax.ShapeDtypeStruct
    ff=gg.shape[-1]; r=gg.shape[-2]; w=gow.shape[-1]; h=ff//2; hw=-(-3*cols//2//128)*128
    vm=pltpu.VMEM
    dma=lambda k: pltpu.SemaphoreType.DMA((k,))
    blocks=(nb,QB,width)
    like=lambda a: vm(a.shape,a.dtype)
    one=lambda k: [vm((4,2,r,k),bf),dma(2)]
    two=lambda k: [vm((4,r,k),bf),dma(2)]
    three=lambda k: [vm((3,r,k),bf),dma(3),dma(3)]
    by_z=lambda k: [vm((2,r,k),bf),vm((3,2,r,k),bf),dma(3),dma(3),vm((r,k),bf),dma(2)]
    return pl.pallas_call(functools.partial(fused_bwd_kernel,n,cols),
      out_shape=[S((r,3*ff+3*cols+w),bf),S(blocks,bf)],
      in_specs=[V,V]+[A]*15,out_specs=[V,A],
      scratch_shapes=[vm((pr,128,n),bf)]*3+[vm((pr,128,n),f32),vm((pr,n,128),f32),vm((pr,n,128),f32),vm((heads,n),f32),vm((3,n,pr*128),bf),
        like(gg),like(gu),like(gow),like(tok_t),like(wt),vm((2,QB,width),f32),vm((4,2,2,r,hw),bf),vm((4,2,2,r,hw),bf)]+[vm(blocks,bf)]*2
        +[like(a) for a in (q_s,k_s,v_s,dm,cos,sin,d0,d1)]+[dma(14),dma(2)]+[dma(nb)]*4+[dma(5),dma(5)]
        +[vm((r,ff),bf)]*3+[vm((r,w),bf)]+[vm((r,hw),bf)]*2+[vm((r,3*cols),bf)]
        +one(h)*4+one(w)+one(hw)+one(256)+one(hw-256)+by_z(256)+by_z(hw-256)+(two(h)+three(h))*6+two(w)+three(w)+two(hw)+three(hw),
      compiler_params=pltpu.CompilerParams(vmem_limit_bytes=64<<20,collective_id=1,has_side_effects=True),name="attn_bwd_reduce")(
        lse,start,q_s,k_s,v_s,dm,cos,sin,d0,d1,m_t,gg,gu,gow,tok_t,wt,d_one.reshape(blocks))

def dot_nt_t(a,b,put):
    return dot(dot(a,b).astype(bf),put).astype(bf)

NORM_EPS=1e-05
DIAG=[(0,0),(3,3),(1,2),(2,1)]
CORE=[(0,1),(1,0)]

def cross_copies(n,part,other,send,recv,c):
    def one(b): return pltpu.make_async_remote_copy(src_ref=part.at[b],dst_ref=other.at[b],send_sem=send.at[b],recv_sem=recv.at[b],device_id={"c":1-c},device_id_type=MESH)
    return one

def norm_of(r):
    inv=lax.rsqrt(jnp.mean(r*r,-1,keepdims=True)+NORM_EPS)
    return r*inv,inv

def norm_back(e,nrm,inv):
    return inv*(e-nrm*jnp.mean(e*nrm,-1,keepdims=True))

def ffn_kernel(n,cols,tok_i,og,mixed,ofull,wg_i,wu_i,wd_i,ga,gb,output,gg_o,gu_o,d_one_o,dm,gow,one0,one1,
        out_t,t1,t2,act,normed,inv1,hb_t,dff_t,part,oa,of,oh,summed,gsum,gd,og_s,og_r,a_s,a_r,f_s,f_r,h_s,h_r,x_s,x_r,s0,s1,tok,wg,wu,wd,gg,gu,d_one,load_s,keep_s,d_s):
    z,y,m=place(); c=lax.axis_index("c")
    own=c==m
    loads=[pltpu.make_async_copy(a,b,load_s.at[i]) for i,(a,b) in enumerate(((tok_i,tok),(wg_i,wg),(wu_i,wu),(wd_i,wd)))]
    for x in loads: x.start()
    greet(peers(z,y,m)+both(c,m))
    nb=n//QB
    grad_far=pltpu.make_async_remote_copy(src_ref=og,dst_ref=summed,send_sem=og_s,recv_sem=og_r,device_id={"c":1-c},device_id_type=MESH)
    grad_near=pltpu.make_async_copy(og,summed,og_r)
    def rows_of(b): return pl.ds(pl.multiple_of(b*QB,QB),QB)
    ca,cf,ch=[cross_copies(n,part,o,ss,rs,c) for o,ss,rs in ((oa,a_s,a_r),(of,f_s,f_r),(oh,h_s,h_r))]
    def far(b): return pltpu.make_async_remote_copy(src_ref=summed.at[b],dst_ref=output.at[b],send_sem=x_s.at[b],recv_sem=x_r.at[b],device_id={"c":1-c,"m":1-m},device_id_type=MESH)
    def near(b): return pltpu.make_async_copy(summed.at[b],output.at[b],x_r.at[b])
    out_t[...]=dot_nt(ofull[...],spread(cols//HD*64,cols,False)).astype(bf)
    def attn_part(b,_):
        part[b]=dot_nt(mixed[rows_of(b),:],out_t[...]).astype(bf)
        ca(b).start()
        return 0
    lax.fori_loop(0,nb,attn_part,0)
    @pl.when(own)
    def _():
        grad_far.start()
        grad_near.start()
    for x in loads: x.wait()
    def forward(b,_):
        rows=rows_of(b)
        ca(b).wait_recv()
        r=tok[rows,:].astype(f32)+(part[b].astype(f32)+oa[b].astype(f32))
        nrm,inv=norm_of(r)
        normed[rows,:]=nrm
        inv1[rows,:]=inv
        hb=(nrm*ga[...]).astype(bf)
        hb_t[:,rows]=hb.T
        gate=dot(hb,wg[...]); up=dot(hb,wu[...])
        sg=jax.nn.sigmoid(gate)
        gs=gate*sg
        a=(gs*up).astype(bf)
        act[rows,:]=a
        t2[rows,:]=gs.astype(bf)
        t1[rows,:]=(up*sg*(1.0+gate*(1.0-sg))).astype(bf)
        ca(b).wait_send()
        part[b]=dot_nt(a,wd[...]).astype(bf)
        cf(b).start()
        return 0
    lax.fori_loop(0,nb,forward,0)
    @pl.when(own)
    def _():
        grad_near.wait()
        grad_far.wait_send()
    @pl.when(jnp.logical_not(own))
    def _():
        grad_far.wait_recv()
    gsum[...]=jnp.zeros_like(gsum)
    def fold(v): return jnp.sum(v.reshape(QB//8,8,v.shape[-1]),0)
    def norm_two(b,_):
        rows=rows_of(b)
        cf(b).wait_recv()
        nrm,inv=norm_of(normed[rows,:]*ga[...]+(part[b].astype(f32)+of[b].astype(f32)))
        g=summed[b].astype(f32)
        summed[b]=(nrm*gb[...]).astype(bf)
        @pl.when(own)
        def _():
            near(b).start()
        @pl.when(jnp.logical_not(own))
        def _():
            far(b).start()
        gsum[8:16,:]+=fold(g*nrm)
        d2=norm_back(g*gb[...],nrm,inv)
        d_one[rows,:]=d2
        df=d2.astype(bf)
        oa[b]=df
        dff_t[:,rows]=df.T
        return 0
    lax.fori_loop(0,nb,norm_two,0)
    width=hb_t.shape[0]; quarter=width//4; ff=act.shape[1]
    def rows4(i): return pl.ds(pl.multiple_of(i*quarter,quarter),quarter)
    def down_grad(i,_):
        gd[i]=dot(dff_t[rows4(i),:],act[...]).astype(bf).reshape(2,2,quarter//4,ff)
        return 0
    lax.fori_loop(0,4,down_grad,0)
    h2=ff//2
    ch2=[First(gd.at[:,:,:,:,0:h2],one0,s0),First(gd.at[:,:,:,:,h2:ff],one1,s1)]
    for x in ch2: x.start()
    def backward(b,_):
        rows=rows_of(b)
        da=dot(oa[b],wd[...])
        dg=(da*t1[rows,:].astype(f32)).astype(bf); du=(da*t2[rows,:].astype(f32)).astype(bf)
        t1[rows,:]=dg; t2[rows,:]=du
        cf(b).wait_send()
        part[b]=(dot_nt(dg,wg[...])+dot_nt(du,wu[...])).astype(bf)
        ch(b).start()
        return 0
    lax.fori_loop(0,nb,backward,0)
    def grads(i,_):
        gg[i]=dot(hb_t[rows4(i),:],t1[...]).astype(bf).reshape(2,2,quarter//4,ff)
        gu[i]=dot(hb_t[rows4(i),:],t2[...]).astype(bf).reshape(2,2,quarter//4,ff)
        return 0
    lax.fori_loop(0,4,grads,0)
    keep=[pltpu.make_async_copy(a,b,keep_s.at[i]) for i,(a,b) in enumerate(((gg,gg_o),(gu,gu_o)))]
    for x in keep: x.start()
    def keep_d(b): return pltpu.make_async_copy(d_one.at[rows_of(b)],d_one_o.at[rows_of(b)],d_s.at[b])
    def last(b,_):
        rows=rows_of(b)
        ch(b).wait_recv()
        dh=d_one[rows,:]+(part[b].astype(f32)+oh[b].astype(f32))
        nrm=normed[rows,:]
        gsum[0:8,:]+=fold(dh*nrm)
        d1=norm_back(dh*ga[...],nrm,inv1[rows,:])
        d_one[rows,:]=d1
        keep_d(b).start()
        da=d1.astype(bf)
        hb_t[:,rows]=da.T
        back=dot(da,out_t[...]).astype(bf)
        for p in range(dm.shape[0]): dm[p,rows,:]=back[:,p*128:p*128+128]
        return 0
    lax.fori_loop(0,nb,last,0)
    put=spread(cols//HD*64,cols,False)
    def out_grads(i,_):
        gow[i,:,:,:,128:128+cols]=dot_nt_t(hb_t[rows4(i),:],mixed[...],put).reshape(2,2,quarter//4,cols)
        return 0
    lax.fori_loop(0,4,out_grads,0)
    line=lax.broadcasted_iota(jnp.int32,(128,width),0)
    both_gains=jnp.where(line==0,jnp.sum(gsum[0:8,:],0,keepdims=True),jnp.where(line==1,jnp.sum(gsum[8:16,:],0,keepdims=True),0.0))
    gow[:,:,:,:,0:128]=both_gains.T.astype(bf).reshape(4,2,2,quarter//4,128)
    for x in ch2: x.finish()
    for x in ch2: x.drain()
    for x in keep: x.wait()
    def drain(b,_):
        ch(b).wait_send()
        keep_d(b).wait()
        @pl.when(own)
        def _():
            near(b).wait()
        @pl.when(jnp.logical_not(own))
        def _():
            far(b).wait_recv()
            far(b).wait_send()
        return 0
    lax.fori_loop(0,nb,drain,0)

def ffn_call(tok,og,mixed,ofull,wg,wu,wd,ga,gb,cols):
    n,width=tok.shape; ff=wg.shape[1]; hp=mixed.shape[1]; nb=n//QB
    V=pl.BlockSpec(memory_space=pltpu.VMEM); A=pl.BlockSpec(memory_space=pl.ANY)
    S=jax.ShapeDtypeStruct
    blocks=(nb,QB,width); r=width//16
    dma=pltpu.SemaphoreType.DMA((nb,))
    vm=pltpu.VMEM
    return pl.pallas_call(functools.partial(ffn_kernel,n,cols),
      out_shape=[S(blocks,bf)]+[S((4,2,2,r,ff),bf)]*2+[S((n,width),f32),S((hp//128,n,128),bf),S((4,2,2,r,cols+128),bf)]+[S((4,2,r,ff//2),bf)]*2,
      in_specs=[A,A,V,V,A,A,A,V,V],out_specs=[A,A,A,A]+[V]*4,
      scratch_shapes=[vm((width,hp),bf),vm((n,ff),bf),vm((n,ff),bf),vm((n,ff),bf),vm((n,width),f32),vm((n,1),f32),vm((width,n),bf),vm((width,n),bf),
        vm(blocks,bf),vm(blocks,bf),vm(blocks,bf),vm(blocks,bf),vm(blocks,bf),vm((16,width),f32),vm((4,2,2,r,ff),bf),
        pltpu.SemaphoreType.DMA,pltpu.SemaphoreType.DMA]+[dma]*8+[pltpu.SemaphoreType.DMA((2,))]*2+[vm((n,width),bf),vm((width,ff),bf),vm((width,ff),bf),vm((width,ff),bf),vm((4,2,2,r,ff),bf),vm((4,2,2,r,ff),bf),vm((n,width),f32),pltpu.SemaphoreType.DMA((4,)),pltpu.SemaphoreType.DMA((2,)),dma],
      compiler_params=pltpu.CompilerParams(vmem_limit_bytes=64<<20,collective_id=3,has_side_effects=True),name="ffn")(
        tok,og.reshape(blocks),mixed,ofull,wg,wu,wd,ga,gb)

def rms_forward(resid):
    inverse=lax.rsqrt(jnp.mean(resid*resid,-1,keepdims=True)+NORM_EPS)
    return (resid*inverse,inverse)

def rms_backward(grad_normed,normed,inverse):
    return inverse*(grad_normed-normed*jnp.mean(grad_normed*normed,-1,keepdims=True))

def doc_starts(lengths,n):
    at=jnp.arange(n,dtype=jnp.int32); start=jnp.zeros((n,),jnp.int32); end=jnp.int32(0)
    for i in range(lengths.shape[0]-1):
        end=end+lengths[i]
        start=jnp.where(at>=end,end,start)
    return start

def rope_tables(positions):
    lane=jnp.arange(128,dtype=jnp.int32)%64
    fr=jnp.where(lane<HD,jnp.exp((lane%(HD//2)).astype(f32)*(-2.0*math.log(10000.0)/HD)),0.0)
    a=positions.astype(f32)[:,None]*fr[None,:]
    return jnp.cos(a),jnp.sin(a)

def core_sum(part):
    return part.astype(f32)+lax.ppermute(part,"c",CORE).astype(f32)

def on_device(tokens,out_grad,doc_lengths,w_query,w_key,w_value,w_out,gain_one,w_gate,w_up,w_down,gain_two):
    cols=w_query.shape[1]; n,width=tokens.shape
    if lax.axis_size("q")==8 and lax.axis_size("m")==2 and w_query.shape[0]==48:
        tokens,cos,sin,q,k,v,tok_t,wt,start,gain_a,gain_b,ofull,gate_w,up_w,down_t,m_t,mixed,lse=fused_fwd(
            doc_lengths,tokens,w_query,w_key,w_value,w_out.T,w_gate,w_up,w_down.T,gain_one,gain_two)
        ofull,gate_w,up_w,down_t=[a.reshape(width,a.shape[-1]) for a in (ofull,gate_w,up_w,down_t)]
        output,gg,gu,d_one,dm,gow,*downs=ffn_call(tokens,out_grad,mixed,ofull,gate_w,up_w,down_t,gain_a,gain_b,cols)
        grads,gtok=fused_bwd(q,k,v,m_t,dm,lse,start,cos,sin,gg,gu,gow,*downs,tok_t,wt,d_one,cols)
        gtok,sgate,sup,sdown,sq,sk,sv,sout,sgain=finish(gtok,grads,cols,w_gate.shape[1])
        return (output.reshape(n,width),gtok.reshape(n,width),sq,sk,sv,sout.T,sgain[0],sgate,sup,sdown.T,sgain[1])
    own=lax.axis_index("c")==lax.axis_index("m")
    pick=lambda a: jnp.where(own,a,lax.ppermute(a,"c",CORE))
    tokens,out_grad,doc_lengths=pick(tokens),pick(out_grad),pick(doc_lengths)
    start=doc_starts(doc_lengths[0],n)
    cos,sin=rope_tables(jnp.arange(n,dtype=jnp.int32)-start)
    start=start[None]
    ff=w_gate.shape[1]
    cast=lambda a: a.astype(bf)
    gains=jnp.pad(jnp.stack([cast(gain_one),cast(gain_two)],1),((0,0),(0,126)))
    apack=jnp.concatenate([cast(w_query),cast(w_key),cast(w_value),gains],1)
    def gather(a):
        return lax.all_gather(lax.ppermute(a,("c","m"),DIAG),("q","m"),axis=0,tiled=True)
    afull,ofull,gate_w,up_w,down_t=[gather(a) for a in (apack,cast(w_out).T,cast(w_gate),cast(w_up),cast(w_down).T)]
    q,k,v,m_t,mixed,lse=attn_fwd(tokens,afull[:,:3*cols],cos,sin,start)
    put=spread(cols//HD*64,cols,False)
    out_t=dot_nt(ofull,put).astype(bf)
    gain_a=afull[:,3*cols].astype(f32); gain_b=afull[:,3*cols+1].astype(f32)
    attn=core_sum(dot_nt(mixed,out_t).astype(bf))
    normed_one,inv_one=rms_forward(tokens.astype(f32)+attn)
    hidden=normed_one*gain_a
    hb=hidden.astype(bf)
    gate=dot(hb,gate_w); up=dot(hb,up_w)
    sg=jax.nn.sigmoid(gate)
    act=(gate*sg*up).astype(bf)
    ffn=core_sum(dot_nt(act,down_t).astype(bf))
    normed_two,inv_two=rms_forward(hidden+ffn)
    output=(normed_two*gain_b).astype(bf)
    g=out_grad.astype(f32)
    g_gain_two=jnp.sum(g*normed_two,0)
    d_two=rms_backward(g*gain_b,normed_two,inv_two)
    d_ffn=d_two.astype(bf)
    tn=lambda a,b: lax.dot_general(a,b,(((0,),(0,)),((),())),preferred_element_type=f32)
    d_act=dot(d_ffn,down_t)
    d_up=(d_act*gate*sg).astype(bf)
    d_gate=(d_act*up*sg*(1.0+gate*(1.0-sg))).astype(bf)
    hterm=(dot_nt(d_gate,gate_w)+dot_nt(d_up,up_w)).astype(bf)
    gff=[tn(hb,d_gate).astype(bf),tn(hb,d_up).astype(bf),tn(d_ffn,act).astype(bf)]
    d_hidden=d_two+core_sum(hterm)
    g_gain_one=jnp.sum(d_hidden*normed_one,0)
    d_one=rms_backward(d_hidden*gain_a,normed_one,inv_one)
    d_attn=d_one.astype(bf)
    dm=dot(d_attn,out_t).astype(bf)
    output=jnp.where(own,output,lax.ppermute(output,("c","m"),[(1,2),(2,1)]))

    ggain=jnp.pad(jnp.stack([g_gain_one,g_gain_two],1),((0,0),(0,126))).astype(bf)
    dqkv=attn_bwd(q,k,v,m_t,dm,lse,start,cos,sin)
    term=0.0; gqkv=[]
    for j in range(3):
        wp=dot_nt(afull[:,j*cols:(j+1)*cols],put).astype(bf)
        term=term+dot_nt(dqkv[j],wp)
        gqkv.append(dot(tn(tokens,dqkv[j]).astype(bf),put).astype(bf))
    gtok=(d_one+core_sum(term.astype(bf))).astype(bf)
    gtok=lax.ppermute(gtok,("c","m"),DIAG).astype(f32)
    g_out=dot(tn(d_attn,mixed).astype(bf),put).astype(bf)
    gatt=jnp.concatenate([ggain,g_out]+gqkv,1)
    add=lambda a: lax.psum_scatter(a,("q","m"),scatter_dimension=0,tiled=True)
    sff,sat=[add(a) for a in gff],add(gatt)
    sff,sat=lax.ppermute(jnp.concatenate(sff,1),("c","m"),DIAG).astype(f32),lax.ppermute(sat,("c","m"),DIAG).astype(f32)
    piece=lambda j: sat[:,128+j*cols:128+(j+1)*cols]
    return (output,gtok,piece(1),piece(2),piece(3),piece(0).T,sat[:,0],sff[:,:ff],sff[:,ff:2*ff],sff[:,2*ff:].T,sat[:,1])

def finish_kernel(cols,ff,gtok,grads,gtok_o,g_o,u_o,d_o,q_o,k_o,v_o,w_o,gain_o):
    gtok_o[...]=gtok[...].astype(f32)
    @pl.when(pl.program_id(0)==0)
    def _():
        at=0
        for ref,wide in ((g_o,ff),(u_o,ff),(d_o,ff),(q_o,cols),(k_o,cols),(v_o,cols)):
            ref[...]=grads[:,at:at+wide].astype(f32)
            at+=wide
        gain_o[...]=grads[:,at:at+128].astype(f32).T[0:8,:]
        w_o[...]=grads[:,at+128:].astype(f32)

def finish(gtok,grads,cols,ff):
    nb,rows,width=gtok.shape; r=grads.shape[0]
    S=jax.ShapeDtypeStruct
    block=pl.BlockSpec((1,rows,width),lambda i:(i,0,0))
    whole=lambda a,b: pl.BlockSpec((a,b),lambda i:(0,0))
    shapes=[(r,ff)]*3+[(r,cols)]*4+[(8,r)]
    return pl.pallas_call(functools.partial(finish_kernel,cols,ff),grid=(nb,),
      out_shape=[S(gtok.shape,f32)]+[S(a,f32) for a in shapes],
      in_specs=[block,whole(*grads.shape)],out_specs=[block]+[whole(*a) for a in shapes],
      compiler_params=pltpu.CompilerParams(vmem_limit_bytes=63<<20),name="finish")(gtok,grads)

def solution(mesh):
    dp,mp=mesh.shape["dp"],mesh.shape["mp"]
    fine=Mesh(mesh.devices.reshape(dp//2,2,mp),("q","c","m"))
    d=("q","c")
    rows,cols_=P(d,"m"),P("m",d)
    return jax.shard_map(on_device,mesh=fine,
        in_specs=(P(d,None),P(d,None),P(d,None),rows,rows,rows,cols_,P(d),rows,rows,cols_,P(d)),
        out_specs=(P(d,None),P(d,None),rows,rows,rows,cols_,P(d),rows,rows,cols_,P(d)),check_vma=False)
```

```python
import functools
import math
import jax
import jax.numpy as jnp
import numpy as np
from jax import lax
from jax.experimental import pallas as pl
from jax.experimental.pallas import tpu as pltpu
from jax.sharding import Mesh, PartitionSpec as P
MESH=pl.DeviceIdType.MESH
HD=48
C2=HD**-0.5*math.log2(math.e)
NEG=-1e30
bf=jnp.bfloat16; f32=jnp.float32
QB=256; LOOK=4
NT=(((1,),(1,)),((),()))
def dot(a,b): return jnp.dot(a,b,preferred_element_type=f32)
def dot_nt(a,b): return lax.dot_general(a,b,NT,preferred_element_type=f32)

def spread(rows, cols, rot):
    r=lax.broadcasted_iota(jnp.int32,(rows,cols),0); c=lax.broadcasted_iota(jnp.int32,(rows,cols),1)
    h=r//64; d=r-h*64
    if not rot:
        return jnp.where((d<HD)&(c==h*HD+d),1.0,0.0).astype(bf)
    lo=(d<24)&(c==h*HD+d+24); hi=(d>=24)&(d<HD)&(c==h*HD+d-24)
    return jnp.where(lo,-1.0,jnp.where(hi,1.0,0.0)).astype(bf)

def proj_weights(w,wq_s,cols):
    hp=cols//HD*64
    for m,(col,rot) in enumerate(((0,False),(0,True),(1,False),(1,True),(2,False))):
        if len(w.shape)==2:
            part=w[:,col*cols:(col+1)*cols]
        else:
            part=w[:,:,:,:,col*cols:(col+1)*cols].reshape(-1,cols)
        wq_s[m]=dot_nt(spread(hp,cols,rot),part).astype(bf)

def proj(tok,cos,sin,wq_s,q_s,k_s,v_s,lo,hi):
    def body(b,_):
        rows=pl.ds(pl.multiple_of(b*QB,QB),QB)
        x=tok[rows,:]
        cs=cos[rows,:]; sn=sin[rows,:]
        for dst,a in ((q_s,0),(k_s,2)):
            raw=dot_nt(x,wq_s[a]); rt=dot_nt(x,wq_s[a+1])
            for p in range(dst.shape[0]):
                l=slice(p*128,p*128+128)
                dst[p,rows,:]=(raw[:,l]*cs+rt[:,l]*sn).astype(bf)
        raw=dot_nt(x,wq_s[4])
        for p in range(v_s.shape[0]):
            v_s[p,rows,:]=raw[:,p*128:p*128+128].astype(bf)
        return 0
    lax.fori_loop(lo,hi,body,0)

def masks(kk0,nk,i,start):
    kidx=lax.broadcasted_iota(jnp.int32,(nk,QB),0)+kk0
    ok=kidx>=start
    qidx=lax.broadcasted_iota(jnp.int32,(nk,QB),1)+i*QB
    return ok&(kidx<=qidx)

def fwd_head(h,i,q_t,k_s,v_t,start,m_t,lse):
    p=h//2; half=h-2*p
    lo=max(0,i-LOOK)*QB; nk=(i+1)*QB-lo
    kk=slice(lo,lo+nk); qq=slice(i*QB,(i+1)*QB)
    row=lax.broadcasted_iota(jnp.int32,(128,QB),0)
    mine=(row>=half*64)&(row<half*64+64)
    qt=jnp.where(mine,q_t[p,:,qq],jnp.zeros((),bf))
    s=dot(k_s[p,kk,:],qt)
    st=start[:,qq]
    s=jnp.where(masks(lo,nk,i,st),s,NEG)
    m=jnp.max(s,0,keepdims=True)
    e=jnp.exp2((s-m)*C2)
    l=jnp.sum(e,0,keepdims=True)
    pr=(e*(1.0/l)).astype(bf)
    rows=pl.ds(pl.multiple_of(half*64,64),64)
    m_t[p,rows,qq]=dot(v_t[p,rows,kk],pr)
    lse[pl.ds(h,1),qq]=m*C2+jnp.log2(l)

def fwd_kernel(n,cols,tok,w,cos,sin,start,q_o,k_o,v_o,m_t,mixed,lse,wq_s,q_t,v_t):
    proj_weights(w,wq_s,cols)
    proj(tok,cos,sin,wq_s,q_o,k_o,v_o,0,n//QB)
    heads=cols//HD
    for p in range(heads//2):
        q_t[p]=q_o[p].T
        v_t[p]=v_o[p].T
    def body(h,_):
        for i in range(n//QB):
            fwd_head(h,i,q_t,k_o,v_t,start,m_t,lse)
        return 0
    lax.fori_loop(0,heads,body,0)
    for p in range(heads//2):
        mixed[:,p*128:p*128+128]=m_t[p].T.astype(bf)

def attn_fwd(tok,w,cos,sin,start):
    n=tok.shape[0]; cols=w.shape[1]//3; heads=cols//HD; P=heads//2
    V=pl.BlockSpec(memory_space=pltpu.VMEM)
    S=jax.ShapeDtypeStruct
    return pl.pallas_call(functools.partial(fwd_kernel,n,cols),
      out_shape=(S((P,n,128),bf),S((P,n,128),bf),S((P,n,128),bf),S((P,128,n),f32),S((n,P*128),bf),S((heads,n),f32)),
      in_specs=[V]*5,out_specs=[V]*6,
      scratch_shapes=[pltpu.VMEM((5,P*128,w.shape[0]),bf),pltpu.VMEM((P,128,n),bf),pltpu.VMEM((P,128,n),bf)],
      compiler_params=pltpu.CompilerParams(vmem_limit_bytes=60<<20),name="attn_fwd")(tok,w,cos,sin,start)

def bwd_head(h,i,q_t,q_s,k_s,k_t,v_s,dm_t,dm_s,lse,dd,start,dq_t,dk_s,dv_s):
    p=h//2; half=h-2*p
    lo=max(0,i-LOOK)*QB; nk=(i+1)*QB-lo
    kk=slice(lo,lo+nk); qq=slice(i*QB,(i+1)*QB)
    row=lax.broadcasted_iota(jnp.int32,(128,QB),0)
    mine=(row>=half*64)&(row<half*64+64)
    lane=lax.broadcasted_iota(jnp.int32,(QB,128),1)
    mlane=(lane>=half*64)&(lane<half*64+64)
    zero=jnp.zeros((),bf)
    qt=jnp.where(mine,q_t[p,:,qq],zero)
    dmt=jnp.where(mine,dm_t[p,:,qq],zero)
    qn=jnp.where(mlane,q_s[p,qq,:],zero)
    dmn=jnp.where(mlane,dm_s[p,qq,:],zero)
    s=dot(k_s[p,kk,:],qt)
    st=start[:,qq]
    pr=jnp.exp2(jnp.where(masks(lo,nk,i,st),s*C2,NEG)-lse[pl.ds(h,1),qq])
    dp=dot(v_s[p,kk,:],dmt)
    ds=(pr*(dp-dd[pl.ds(h,1),qq])).astype(bf)
    pb=pr.astype(bf)
    dv_s[p,kk,:]+=dot(pb,dmn)
    dk_s[p,kk,:]+=dot(ds,qn)
    rows=pl.ds(pl.multiple_of(half*64,64),64)
    dq_t[p,rows,qq]=dot(k_t[p,rows,kk],ds)

def rope_back(u,cs,sn):
    w=u*sn
    lane=lax.broadcasted_iota(jnp.int32,u.shape,1)&63
    up=pltpu.roll(w,128-24,axis=1); dn=pltpu.roll(w,24,axis=1)
    return u*cs+jnp.where(lane<24,up,jnp.where(lane<48,-dn,0.0))

def bwd_kernel(n,heads,q_s,k_s,v_s,m_t,dm,lse,start,cos,sin,dqkv,q_t,k_t,dm_t,dm_s,dq_t,dk_s,dv_s,dd):
    P=heads//2
    for p in range(P):
        q_t[p]=q_s[p].T
        k_t[p]=k_s[p].T
        dm_s[p]=dm[:,p*128:p*128+128]
        dm_t[p]=dm_s[p].T
        for half in range(2):
            r=slice(half*64,half*64+64)
            dd[2*p+half:2*p+half+1,:]=jnp.sum(dm_t[p,r,:].astype(f32)*m_t[p,r,:],0,keepdims=True)
    dk_s[...]=jnp.zeros_like(dk_s); dv_s[...]=jnp.zeros_like(dv_s)
    def body(h,_):
        for i in range(n//QB):
            bwd_head(h,i,q_t,q_s,k_s,k_t,v_s,dm_t,dm_s,lse,dd,start,dq_t,dk_s,dv_s)
        return 0
    lax.fori_loop(0,heads,body,0)
    sc=HD**-0.5
    for p in range(P):
        dqkv[0,:,p*128:p*128+128]=rope_back(dq_t[p].T*sc,cos[...],sin[...]).astype(bf)
        dqkv[1,:,p*128:p*128+128]=rope_back(dk_s[p]*sc,cos[...],sin[...]).astype(bf)
        dqkv[2,:,p*128:p*128+128]=dv_s[p].astype(bf)

def attn_bwd(q_s,k_s,v_s,m_t,dm,lse,start,cos,sin):
    P,n,_=q_s.shape; heads=2*P
    V=pl.BlockSpec(memory_space=pltpu.VMEM)
    S=jax.ShapeDtypeStruct
    return pl.pallas_call(functools.partial(bwd_kernel,n,heads),
      out_shape=S((3,n,P*128),bf),
      in_specs=[V]*9,out_specs=V,
      scratch_shapes=[pltpu.VMEM((P,128,n),bf),pltpu.VMEM((P,128,n),bf),pltpu.VMEM((P,128,n),bf),pltpu.VMEM((P,n,128),bf),pltpu.VMEM((P,128,n),f32),pltpu.VMEM((P,n,128),f32),pltpu.VMEM((P,n,128),f32),pltpu.VMEM((heads,n),f32)],
      compiler_params=pltpu.CompilerParams(vmem_limit_bytes=60<<20),name="attn_bwd")(q_s,k_s,v_s,m_t,dm,lse,start,cos,sin)


def place():
    q,m=lax.axis_index("q"),lax.axis_index("m")
    return q//2,lax.rem(q,2),m

def peers(z,y,m):
    return [{"q":z*2+1-y},{"m":1-m}]+[{"q":lax.rem(z+s,4)*2+y} for s in (1,2,3)]

def greet(where):
    barrier=pltpu.get_barrier_semaphore()
    for w in where:
        pl.semaphore_signal(barrier,inc=1,device_id=w,device_id_type=MESH)
    pl.semaphore_wait(barrier,len(where))

def remote(s,d,ss,rs,w):
    return pltpu.make_async_remote_copy(src_ref=s,dst_ref=d,send_sem=ss,recv_sem=rs,device_id=w,device_id_type=MESH)

class First:
    def __init__(self,source,one,sem,first="y"):
        self.source,self.one,self.first=source,one,first
        z,y,m=place()
        self.y,self.m=y,m
        ny,nx=peers(z,y,m)[:2]
        self.copy=remote(source.at[:,1-y],one,sem.at[0],sem.at[1],ny) if first=="y" else remote(source.at[:,:,1-m],one,sem.at[0],sem.at[1],nx)
    def start(self): self.copy.start()
    def finish(self):
        self.copy.wait_recv()
        def add(i,_):
            zz=i//2; o=i-zz*2
            mine=self.source[zz,self.y,o] if self.first=="y" else self.source[zz,o,self.m]
            self.one[zz,o]=(self.one[zz,o].astype(f32)+mine.astype(f32)).astype(bf)
            return 0
        lax.fori_loop(0,8,add,0)
    def drain(self): self.copy.wait_send()

class Second:
    def __init__(self,one,two,sem,first="y"):
        self.one,self.two=one,two
        z,y,m=place()
        ny,nx=peers(z,y,m)[:2]
        self.keep=m if first=="y" else y
        self.copy=remote(one.at[:,1-self.keep],two,sem.at[0],sem.at[1],nx if first=="y" else ny)
    def start(self): self.copy.start()
    def finish(self):
        self.copy.wait_recv()
        def add(zz,_):
            self.two[zz]=(self.two[zz].astype(f32)+self.one[zz,self.keep].astype(f32)).astype(bf)
            return 0
        lax.fori_loop(0,4,add,0)
    def drain(self): self.copy.wait_send()

class SecondZ:
    def __init__(self,one,two,three,send,recv):
        self.one,self.two,self.three=one,two,three
        z,y,m=place()
        self.z=z
        to=peers(z,y,m)
        self.copies=[remote(one.at[lax.rem(z+s,4)],three.at[s-1],send.at[s-1],recv.at[s-1],to[1+s]) for s in (1,2,3)]
    def start(self):
        for c in self.copies: c.start()
    def finish(self):
        for c in self.copies: c.wait_recv()
        for o in range(2):
            t=self.one[self.z,o].astype(f32)
            for s in range(3): t=t+self.three[s,o].astype(f32)
            self.two[o]=t.astype(bf)
    def drain(self):
        for c in self.copies: c.wait_send()

class ThirdX:
    def __init__(self,two,other,out,sem):
        self.two,self.other,self.out=two,other,out
        z,y,m=place()
        self.m=m
        self.copy=remote(two.at[1-m],other,sem.at[0],sem.at[1],{"m":1-m})
    def start(self): self.copy.start()
    def finish(self):
        self.copy.wait_recv()
        self.out[...]=(self.two[self.m].astype(f32)+self.other[...].astype(f32)).astype(bf)
    def drain(self): self.copy.wait_send()

class Third:
    def __init__(self,two,three,out,send,recv):
        self.two,self.three,self.out=two,three,out
        z,y,m=place()
        self.z=z
        to=peers(z,y,m)
        self.copies=[remote(two.at[lax.rem(z+s,4)],three.at[s-1],send.at[s-1],recv.at[s-1],to[1+s]) for s in (1,2,3)]
    def start(self):
        for c in self.copies: c.start()
    def finish(self):
        for c in self.copies: c.wait_recv()
        t=self.two[self.z].astype(f32)
        for s in range(3): t=t+self.three[s].astype(f32)
        self.out[...]=t.astype(bf)
    def drain(self):
        for c in self.copies: c.wait_send()

class Gather:
    def __init__(self,shard,full,cols,stage,sem,sem_z,first):
        z,y,m=place(); c=lax.axis_index("c")
        to=peers(z,y,m)
        src=shard.at[:,cols]
        self.first=first
        self.own=c==m
        self.here=pltpu.make_async_copy(src,stage.at[z,y],sem.at[0])
        self.along=[remote(src,stage.at[z,y],sem_z.at[0,s-1],sem_z.at[1,s-1],to[1+s]) for s in (1,2,3)]
        a,b=(stage.at[:,y],full.at[:,y,c,:,cols]) if first=="x" else (stage,full.at[:,:,c,:,cols])
        self.near_self=pltpu.make_async_copy(a,b,sem.at[1])
        self.near=remote(a,b,sem.at[2],sem.at[3],{"c":1-c})
        self.far_same=remote(a,b,sem.at[4],sem.at[5],{"m":1-m})
        self.far_diag=remote(a,b,sem.at[4],sem.at[6],{"c":1-c,"m":1-m})
        d=full.at[:,y,:,:,cols] if first=="x" else stage.at[:,y]
        self.across=remote(d,d,sem.at[7],sem.at[8],to[0])
    def start(self):
        self.here.start()
        for c in self.along: c.start()
    def cross(self):
        @pl.when(self.own)
        def _():
            self.near_self.start()
            self.far_same.start()
        @pl.when(jnp.logical_not(self.own))
        def _():
            self.far_diag.start()
            self.near.start()
    def crossed(self):
        @pl.when(self.own)
        def _():
            self.near_self.wait()
            self.near.wait_recv()
        @pl.when(jnp.logical_not(self.own))
        def _():
            self.far_same.wait_recv()
            self.far_diag.wait_recv()
    def second(self):
        self.here.wait()
        for c in self.along: c.wait_recv()
        if self.first=="x": self.cross()
        else: self.across.start()
    def third(self):
        if self.first=="x":
            self.crossed()
            self.across.start()
        else:
            self.across.wait_recv()
            self.cross()
    def finish(self):
        if self.first=="x": self.across.wait_recv()
        else: self.crossed()
    def drain(self):
        for c in self.along: c.wait_send()
        self.across.wait_send()
        @pl.when(self.own)
        def _():
            self.far_same.wait_send()
        @pl.when(jnp.logical_not(self.own))
        def _():
            self.far_diag.wait_send()
            self.near.wait_send()

def both(c,m):
    return [{"c":1-c},{"c":1-c,"m":1-m}]

def fused_fwd_kernel(n,cols,lengths,freq,tok_i,wq_i,wk_i,wv_i,wo_i,wg_i,wu_i,wd_i,g1_i,g2_i,
        tok_o,cos_o,sin_o,q_o,k_o,v_o,tok_t_o,wt_o,start,ga,gb,wo,wg,wu,wd,m_t,mixed,lse,
        tok,cos,sin,q_s,k_s,v_s,tok_t,wa,wq_s,q_t,v_t,docs_i,docs,a_b,o_b,g_b,u_b,d_b,swap_s,swap_r,out_s,*scr):
    z,y,m=place(); c=lax.axis_index("c")
    own=c==m
    r=a_b.shape[0]; ff=g_b.shape[1]
    eye=(lax.broadcasted_iota(jnp.int32,(r,r),0)==lax.broadcasted_iota(jnp.int32,(r,r),1)).astype(bf)
    line=lax.broadcasted_iota(jnp.int32,(128,r),0)
    gains=jnp.where(line==0,g1_i[...],jnp.where(line==1,g2_i[...],0.0)).astype(bf)
    for j,w in enumerate((wq_i,wk_i,wv_i)): a_b[:,j*cols:(j+1)*cols]=w[...].astype(bf)
    a_b[:,3*cols:]=dot_nt(eye,gains).astype(bf)
    g_b[...]=wg_i[...].astype(bf)
    u_b[...]=wu_i[...].astype(bf)
    o_b[...]=wo_i[...].astype(bf)
    d_b[...]=wd_i[...].astype(bf)
    row=lax.broadcasted_iota(jnp.int32,(8,128),0)
    table=jnp.zeros((8,128),jnp.int32)
    for i in range(lengths.shape[1]): table=jnp.where(row==i,lengths[0,i],table)
    docs_i[...]=table
    greet(peers(z,y,m)+both(c,m))
    packs=[(docs_i,docs),(tok_i,tok)]
    swap_far=[remote(a,b,swap_s.at[i],swap_r.at[i],{"c":1-c}) for i,(a,b) in enumerate(packs)]
    swap_near=[pltpu.make_async_copy(a,b,swap_r.at[i]) for i,(a,b) in enumerate(packs)]
    scr=list(scr)
    def chunk(shard,full,lo,hi,first):
        stage,sem,sem_z=scr[:3]
        del scr[:3]
        return Gather(shard,full,slice(lo,hi),stage,sem,sem_z,first)
    cut=cuts(a_b.shape[1])
    a=[chunk(a_b,wa,cut[i],cut[i+1],"xy"[i%2]) for i in range(4)]
    h2=ff//2
    f=[chunk(b,w,j*h2,j*h2+h2,"xy"[j]) for b,w in ((g_b,wg),(u_b,wu),(d_b,wd)) for j in range(2)]
    f.append(chunk(o_b,wo,0,cols,"x"))
    for x in a: x.start()
    @pl.when(own)
    def _():
        for x,w in zip(swap_near,swap_far):
            x.start(); w.start()
        swap_near[0].wait()
    @pl.when(jnp.logical_not(own))
    def _():
        swap_far[0].wait_recv()
    for x in f: x.start()
    def begin(at):
        end=jnp.zeros((1,1),jnp.int32); first=jnp.zeros(at.shape,jnp.int32)
        for i in range(lengths.shape[1]-1):
            end=end+docs[i:i+1,0:1]
            first=jnp.where(at>=end,end,first)
        return first
    start[...]=begin(lax.broadcasted_iota(jnp.int32,(1,n),1))
    def tables(b,_):
        rows=pl.ds(pl.multiple_of(b*QB,QB),QB)
        at=lax.broadcasted_iota(jnp.int32,(QB,128),0)+b*QB
        angle=(at-begin(at)).astype(f32)*freq[...]
        cos[rows,:]=jnp.cos(angle)
        sin[rows,:]=jnp.sin(angle)
        return 0
    nb=n//QB
    lax.fori_loop(0,nb//2,tables,0)
    a[0].second(); a[1].second()
    lax.fori_loop(nb//2,nb,tables,0)
    a[0].third(); a[1].third()
    a[2].second(); a[3].second()
    keep=[pltpu.make_async_copy(v,h,out_s.at[i]) for i,(v,h) in enumerate(((cos,cos_o),(sin,sin_o),(tok,tok_o),(tok_t,tok_t_o),(wq_s.at[0],wt_o.at[0]),(wq_s.at[2],wt_o.at[1]),
        (wq_s.at[4],wt_o.at[2]),(q_s,q_o),(k_s,k_o),(v_s,v_o)))]
    keep[0].start(); keep[1].start()
    @pl.when(own)
    def _():
        swap_near[1].wait()
    @pl.when(jnp.logical_not(own))
    def _():
        swap_far[1].wait_recv()
    keep[2].start()
    half=tok_t.shape[0]//2
    tok_t[:half,:]=tok[:,:half].T
    a[2].third(); a[3].third()
    tok_t[half:,:]=tok[:,half:].T
    keep[3].start()
    f[0].second(); f[1].second()
    for x in a: x.finish()
    proj_weights(wa,wq_s,cols)
    for x in keep[4:7]: x.start()
    proj(tok,cos,sin,wq_s,q_s,k_s,v_s,0,nb//3)
    f[0].third(); f[1].third()
    proj(tok,cos,sin,wq_s,q_s,k_s,v_s,nb//3,nb)
    f[2].second(); f[3].second()
    for x in keep[7:]: x.start()
    rows=wa[:,:,:,:,3*cols:].reshape(-1,128).astype(f32).T
    ga[...]=rows[0:1,:]
    gb[...]=rows[1:2,:]
    heads=cols//HD
    for p in range(heads//2):
        q_t[p]=q_s[p].T
        v_t[p]=v_s[p].T
    plan={0:[(4,"second"),(5,"second"),(6,"second")],1:[(2,"third"),(3,"third")],3:[(4,"third"),(5,"third"),(6,"third")]}
    def body(h,_):
        for i in range(nb):
            fwd_head(h,i,q_t,k_s,v_t,start,m_t,lse)
        for at,todo in plan.items():
            @pl.when(h==at)
            def _():
                for k,what in todo: getattr(f[k],what)()
        return 0
    lax.fori_loop(0,heads,body,0)
    for p in range(heads//2):
        mixed[:,p*128:p*128+128]=m_t[p].T.astype(bf)
    for x in f: x.finish()
    for x in a+f: x.drain()
    for x in keep: x.wait()
    @pl.when(own)
    def _():
        for x in swap_far: x.wait_send()

def cuts(width):
    return [0,width//1280*384,width//2,width//2+width//1280*256,width]

def fused_fwd(lengths,tok,wq,wk,wv,w_out,wg,wu,wd,g1,g2):
    n,width=tok.shape; r,cols=wq.shape; heads=cols//HD; pr=heads//2; ff=wg.shape[1]; ac=3*cols+128
    V=pl.BlockSpec(memory_space=pltpu.VMEM); A=pl.BlockSpec(memory_space=pl.ANY); M=pl.BlockSpec(memory_space=pltpu.SMEM)
    S=jax.ShapeDtypeStruct
    vm=pltpu.VMEM
    dma=lambda *k: pltpu.SemaphoreType.DMA(k)
    wide=lambda k: S((4,2,2,r,k),bf)
    lane=np.arange(128)%64
    freq=np.where(lane<HD,np.exp((lane%(HD//2)).astype(np.float32)*np.float32(-2.0*math.log(10000.0)/HD)),0.0).astype(np.float32)[None]
    cut=cuts(ac)
    sizes=[cut[i+1]-cut[i] for i in range(4)]+[ff//2]*6+[cols]
    pair=(pr,n,128)
    return pl.pallas_call(functools.partial(fused_fwd_kernel,n,cols),
      out_shape=[S((n,width),bf),S((n,128),f32),S((n,128),f32),S(pair,bf),S(pair,bf),S(pair,bf),S((width,n),bf),S((3,pr*128,width),bf),
        S((1,n),jnp.int32),S((1,width),f32),S((1,width),f32),wide(cols),wide(ff),wide(ff),wide(ff),S((pr,128,n),f32),S((n,pr*128),bf),S((heads,n),f32)],
      in_specs=[M,V,A]+[V]*9,out_specs=[A]*8+[V]*10,
      scratch_shapes=[vm((n,width),bf),vm((n,128),f32),vm((n,128),f32),vm(pair,bf),vm(pair,bf),vm(pair,bf),vm((width,n),bf),vm((4,2,2,r,ac),bf),
        vm((5,pr*128,width),bf),vm((pr,128,n),bf),vm((pr,128,n),bf),vm((8,128),jnp.int32),vm((8,128),jnp.int32),
        vm((r,ac),bf),vm((r,cols),bf),vm((r,ff),bf),vm((r,ff),bf),vm((r,ff),bf),dma(2),dma(2),dma(10)]
        +sum([[vm((4,2,r,k),bf),dma(9),dma(2,3)] for k in sizes],[]),
      compiler_params=pltpu.CompilerParams(vmem_limit_bytes=60<<20,collective_id=0,has_side_effects=True),name="attn_fwd_gather")(
        lengths,jnp.asarray(freq),tok,wq,wk,wv,w_out,wg,wu,wd,g1[None],g2[None])

def fused_bwd_kernel(n,cols,lse,start,q_i,k_i,v_i,dm_i,cos_i,sin_i,d0_i,d1_i,m_i,g_i,u_i,o_i,tok_i,wt_i,d_one,grads,gtok,
        q_t,k_t,dm_t,dq_t,dk_s,dv_s,dd,dqkv,gg,gu,gow,tok_t,wt,d_buf,ga0,ga1,term,other,q_s,k_s,v_s,dm,cos,sin,d0,d1,load_s,d_sem,core_s,core_r,far_s,far_r,fin_s,fin_r,*scr):
    z,y,m=place(); c=lax.axis_index("c")
    own=c==m
    diag={"c":1-c,"m":1-m}
    loads=[pltpu.make_async_copy(a,b,load_s.at[i]) for i,(a,b) in enumerate(((m_i,dq_t),(g_i,gg),(u_i,gu),(o_i,gow),(tok_i,tok_t),(wt_i,wt),(d0_i,d0),(d1_i,d1),(q_i,q_s),(k_i,k_s),(dm_i,dm),(v_i,v_s),(cos_i,cos),(sin_i,sin)))]
    for i in (6,7,1,8,9,10,2,3,0,11,12,13,4,5): loads[i].start()
    greet(peers(z,y,m)+both(c,m))
    scr=list(scr)
    def take(k):
        got=scr[:k]
        del scr[:k]
        return got
    half=gg.shape[-1]//2
    ff=2*half
    fd,fg,fu,fo,fh0,fh1,fq=take(7)
    outs={"d0":fd.at[:,0:half],"d1":fd.at[:,half:ff],"g0":fg.at[:,0:half],"g1":fg.at[:,half:ff],"u0":fu.at[:,0:half],"u1":fu.at[:,half:ff],
        "o":fo,"h0":fh0,"h1a":fh1.at[:,0:256],"h1b":fh1.at[:,256:ga1.shape[-1]]}
    firsts,seconds,thirds={},{},{}
    ones={"d0":d0,"d1":d1}
    for name,src,first in (("g0",gg.at[:,:,:,:,0:half],"y"),("g1",gg.at[:,:,:,:,half:ff],"x"),("u0",gu.at[:,:,:,:,0:half],"y"),("u1",gu.at[:,:,:,:,half:ff],"x"),
            ("o",gow,"y"),("h0",ga0,"y"),("h1a",ga1.at[:,:,:,:,0:256],"y"),("h1b",ga1.at[:,:,:,:,256:ga1.shape[-1]],"y")):
        ones[name],sem=take(2)
        firsts[name]=First(src,ones[name],sem,first)
    for name in ("h1a","h1b"):
        two,three,ss,rs,came,sem=take(6)
        seconds[name]=SecondZ(ones[name],two,three,ss,rs)
        thirds[name]=ThirdX(two,came,outs[name],sem)
    for name in ("d0","d1","g0","g1","u0","u1","o","h0"):
        two,sem,three,ss,rs=take(5)
        seconds[name]=Second(ones[name],two,sem,"x" if name in ("g1","u1") else "y")
        thirds[name]=Third(two,three,outs[name],ss,rs)
    pairs={}
    at=0
    for name,ref in (("g",fg),("u",fu),("d",fd),("q",fq),("o",fo)):
        pairs[name]=(ref,grads.at[:,at:at+ref.shape[-1]])
        at+=ref.shape[-1]
    finals={k:remote(a,b,fin_s.at[i],fin_r.at[i],diag) for i,(k,(a,b)) in enumerate(pairs.items())}
    def give(*names):
        @pl.when(own)
        def _():
            for k in names: pairs[k][1][...]=pairs[k][0][...]
        @pl.when(jnp.logical_not(own))
        def _():
            for k in names: finals[k].start()
    def run(*steps):
        for group,what,names in steps:
            for k in names.split(): getattr(group[k],what)()
    loads[6].wait(); loads[7].wait()
    run((seconds,"start","d0 d1"))
    loads[1].wait()
    run((firsts,"start","g0 g1"))
    for i in (8,9,10): loads[i].wait()
    heads=cols//HD; P_=heads//2
    for p in range(P_):
        q_t[p]=q_s[p].T
        k_t[p]=k_s[p].T
        dm_t[p]=dm[p].T
    loads[2].wait(); loads[3].wait()
    run((firsts,"start","u0 o"))
    loads[0].wait()
    for p in range(P_):
        for half_ in range(2):
            r=slice(half_*64,half_*64+64)
            dd[2*p+half_:2*p+half_+1,:]=jnp.sum(dm_t[p,r,:].astype(f32)*dq_t[p,r,:],0,keepdims=True)
    dk_s[...]=jnp.zeros_like(dk_s); dv_s[...]=jnp.zeros_like(dv_s)
    for i in (4,5,11,12,13): loads[i].wait()
    sc=HD**-0.5
    width=tok_t.shape[0]; quarter=width//4; hp=P_*128; part=hp//2
    def raw_grads(half_):
        for p in range(half_*P_//2,(half_+1)*P_//2):
            dqkv[0,:,p*128:p*128+128]=rope_back(dq_t[p].T*sc,cos[...],sin[...]).astype(bf)
            dqkv[1,:,p*128:p*128+128]=rope_back(dk_s[p]*sc,cos[...],sin[...]).astype(bf)
            dqkv[2,:,p*128:p*128+128]=dv_s[p].astype(bf)
    def weight_grads(half_):
        ga=(ga0,ga1)[half_]
        w=ga.shape[-1]; hc=cols//2
        maps=[]
        for j in range(3):
            rr=lax.broadcasted_iota(jnp.int32,(part,w),0); cc=lax.broadcasted_iota(jnp.int32,(part,w),1)
            hh=rr//64; dd_=rr-hh*64
            maps.append(jnp.where((dd_<HD)&(cc==j*hc+hh*HD+dd_),1.0,0.0).astype(bf))
        def body(i,_):
            r=pl.ds(pl.multiple_of(i*quarter,quarter),quarter)
            t=0.0
            for j in range(3):
                t=t+dot(dot(tok_t[r,:],dqkv[j,:,half_*part:(half_+1)*part]).astype(bf),maps[j])
            ga[i]=t.astype(bf).reshape(2,2,quarter//4,w)
            return 0
        lax.fori_loop(0,4,body,0)
    def middle():
        raw_grads(0)
        weight_grads(0)
    events={0:[lambda: run((seconds,"finish","d0 d1"),(thirds,"start","d0 d1"),(firsts,"finish","g0"),(seconds,"start","g0"),(firsts,"start","u1"))],
        2:[lambda: run((firsts,"finish","u0 g1"),(seconds,"start","u0 g1"))],
        3:[lambda: run((thirds,"finish","d0 d1")),lambda: give("d"),lambda: run((seconds,"finish","g0"),(thirds,"start","g0")),middle,lambda: run((firsts,"start","h0"))],
        4:[lambda: run((seconds,"finish","g1"),(thirds,"start","g1"),(firsts,"finish","o"),(seconds,"start","o"))],
        5:[lambda: run((firsts,"finish","u1"),(seconds,"start","u1"),(thirds,"finish","g0 g1")),lambda: give("g")],
        6:[lambda: run((seconds,"finish","u0"),(thirds,"start","u0"))],
        7:[lambda: run((firsts,"finish","h0"),(seconds,"start","h0"),(seconds,"finish","o"),(thirds,"start","o"))]}
    def body(h,_):
        for i in range(n//QB):
            bwd_head(h,i,q_t,q_s,k_s,k_t,v_s,dm_t,dm,lse,dd,start,dq_t,dk_s,dv_s)
        for at,calls in events.items():
            @pl.when(h==at)
            def _():
                for call in calls: call()
        return 0
    lax.fori_loop(0,heads,body,0)
    raw_grads(1)
    nb=n//QB
    def cross(b): return remote(term.at[b],other.at[b],core_s.at[b],core_r.at[b],{"c":1-c})
    def far(b): return remote(term.at[b],gtok.at[b],far_s.at[b],far_r.at[b],diag)
    def near(b): return pltpu.make_async_copy(term.at[b],gtok.at[b],far_r.at[b])
    def fetch(b): return pltpu.make_async_copy(d_one.at[b],d_buf.at[lax.rem(b,2)],d_sem.at[lax.rem(b,2)])
    fetch(0).start(); fetch(1).start()
    def make(b,_):
        rows=pl.ds(pl.multiple_of(b*QB,QB),QB)
        t=dot(dqkv[0,rows,:],wt[0])+dot(dqkv[1,rows,:],wt[1])+dot(dqkv[2,rows,:],wt[2])
        term[b]=t.astype(bf)
        cross(b).start()
        return 0
    lax.fori_loop(0,nb,make,0)
    def total(b,_):
        cross(b).wait_recv()
        cross(b).wait_send()
        fetch(b).wait()
        term[b]=(d_buf[lax.rem(b,2)]+(term[b].astype(f32)+other[b].astype(f32))).astype(bf)
        @pl.when(b+2<nb)
        def _():
            fetch(b+2).start()
        @pl.when(own)
        def _():
            near(b).start()
        @pl.when(jnp.logical_not(own))
        def _():
            far(b).start()
        return 0
    lax.fori_loop(0,2,total,0)
    weight_grads(1)
    run((firsts,"start","h1a h1b"),(seconds,"finish","h0"),(thirds,"start","h0"),(seconds,"finish","u1"),(thirds,"start","u1"))
    lax.fori_loop(2,4,total,0)
    run((thirds,"finish","u0 o"))
    give("o")
    run((firsts,"finish","h1a"),(seconds,"start","h1a"))
    lax.fori_loop(4,nb,total,0)
    run((firsts,"finish","h1b"),(seconds,"start","h1b"),(thirds,"finish","u1 h0"))
    give("u")
    hc=cols//2; hw=fh0.shape[-1]
    rr=lax.broadcasted_iota(jnp.int32,(hw,3*cols),0); cc=lax.broadcasted_iota(jnp.int32,(hw,3*cols),1)
    jj=cc//cols
    def sort(half_): return jnp.where((rr==jj*hc+cc-jj*cols-half_*hc)&(cc-jj*cols>=half_*hc)&(cc-jj*cols<(half_+1)*hc),1.0,0.0).astype(bf)
    low=dot(fh0[...],sort(0)); last_map=sort(1)
    run((seconds,"finish","h1a"),(thirds,"start","h1a"),(seconds,"finish","h1b"),(thirds,"start","h1b"),(thirds,"finish","h1a h1b"))
    fq[...]=(low+dot(fh1[...],last_map)).astype(bf)
    give("q")
    for group in (firsts,seconds,thirds):
        for x in group.values(): x.drain()
    def drain(b,_):
        @pl.when(own)
        def _():
            near(b).wait()
        @pl.when(jnp.logical_not(own))
        def _():
            far(b).wait_recv()
            far(b).wait_send()
        return 0
    lax.fori_loop(0,nb,drain,0)
    @pl.when(jnp.logical_not(own))
    def _():
        for x in finals.values():
            x.wait_recv()
            x.wait_send()

def fused_bwd(q_s,k_s,v_s,m_t,dm,lse,start,cos,sin,gg,gu,gow,d0,d1,tok_t,wt,d_one,cols):
    pr,n,_=q_s.shape; heads=2*pr; width=tok_t.shape[0]; nb=n//QB
    V=pl.BlockSpec(memory_space=pltpu.VMEM); A=pl.BlockSpec(memory_space=pl.ANY)
    S=jax.ShapeDtypeStruct
    ff=gg.shape[-1]; r=gg.shape[-2]; w=gow.shape[-1]; h=ff//2; hw=-(-3*cols//2//128)*128
    vm=pltpu.VMEM
    dma=lambda k: pltpu.SemaphoreType.DMA((k,))
    blocks=(nb,QB,width)
    like=lambda a: vm(a.shape,a.dtype)
    one=lambda k: [vm((4,2,r,k),bf),dma(2)]
    two=lambda k: [vm((4,r,k),bf),dma(2)]
    three=lambda k: [vm((3,r,k),bf),dma(3),dma(3)]
    by_z=lambda k: [vm((2,r,k),bf),vm((3,2,r,k),bf),dma(3),dma(3),vm((r,k),bf),dma(2)]
    return pl.pallas_call(functools.partial(fused_bwd_kernel,n,cols),
      out_shape=[S((r,3*ff+3*cols+w),bf),S(blocks,bf)],
      in_specs=[V,V]+[A]*15,out_specs=[V,A],
      scratch_shapes=[vm((pr,128,n),bf)]*3+[vm((pr,128,n),f32),vm((pr,n,128),f32),vm((pr,n,128),f32),vm((heads,n),f32),vm((3,n,pr*128),bf),
        like(gg),like(gu),like(gow),like(tok_t),like(wt),vm((2,QB,width),f32),vm((4,2,2,r,hw),bf),vm((4,2,2,r,hw),bf)]+[vm(blocks,bf)]*2
        +[like(a) for a in (q_s,k_s,v_s,dm,cos,sin,d0,d1)]+[dma(14),dma(2)]+[dma(nb)]*4+[dma(5),dma(5)]
        +[vm((r,ff),bf)]*3+[vm((r,w),bf)]+[vm((r,hw),bf)]*2+[vm((r,3*cols),bf)]
        +one(h)*4+one(w)+one(hw)+one(256)+one(hw-256)+by_z(256)+by_z(hw-256)+(two(h)+three(h))*6+two(w)+three(w)+two(hw)+three(hw),
      compiler_params=pltpu.CompilerParams(vmem_limit_bytes=64<<20,collective_id=1,has_side_effects=True),name="attn_bwd_reduce")(
        lse,start,q_s,k_s,v_s,dm,cos,sin,d0,d1,m_t,gg,gu,gow,tok_t,wt,d_one.reshape(blocks))

def dot_nt_t(a,b,put):
    return dot(dot(a,b).astype(bf),put).astype(bf)

NORM_EPS=1e-05
DIAG=[(0,0),(3,3),(1,2),(2,1)]
CORE=[(0,1),(1,0)]

def cross_copies(n,part,other,send,recv,c):
    def one(b): return pltpu.make_async_remote_copy(src_ref=part.at[b],dst_ref=other.at[b],send_sem=send.at[b],recv_sem=recv.at[b],device_id={"c":1-c},device_id_type=MESH)
    return one

def norm_of(r):
    inv=lax.rsqrt(jnp.mean(r*r,-1,keepdims=True)+NORM_EPS)
    return r*inv,inv

def norm_back(e,nrm,inv):
    return inv*(e-nrm*jnp.mean(e*nrm,-1,keepdims=True))

def ffn_kernel(n,cols,tok_i,og,mixed,ofull,wg_i,wu_i,wd_i,ga,gb,output,gg_o,gu_o,d_one_o,dm,gow,one0,one1,
        out_t,t1,t2,act,normed,inv1,hb_t,dff_t,part,oa,of,oh,summed,gsum,gd,og_s,og_r,a_s,a_r,f_s,f_r,h_s,h_r,x_s,x_r,s0,s1,tok,wg,wu,wd,gg,gu,d_one,load_s,keep_s,d_s):
    z,y,m=place(); c=lax.axis_index("c")
    own=c==m
    loads=[pltpu.make_async_copy(a,b,load_s.at[i]) for i,(a,b) in enumerate(((tok_i,tok),(wg_i,wg),(wu_i,wu),(wd_i,wd)))]
    for x in loads: x.start()
    greet(peers(z,y,m)+both(c,m))
    nb=n//QB
    grad_far=pltpu.make_async_remote_copy(src_ref=og,dst_ref=summed,send_sem=og_s,recv_sem=og_r,device_id={"c":1-c},device_id_type=MESH)
    grad_near=pltpu.make_async_copy(og,summed,og_r)
    def rows_of(b): return pl.ds(pl.multiple_of(b*QB,QB),QB)
    ca,cf,ch=[cross_copies(n,part,o,ss,rs,c) for o,ss,rs in ((oa,a_s,a_r),(of,f_s,f_r),(oh,h_s,h_r))]
    def far(b): return pltpu.make_async_remote_copy(src_ref=summed.at[b],dst_ref=output.at[b],send_sem=x_s.at[b],recv_sem=x_r.at[b],device_id={"c":1-c,"m":1-m},device_id_type=MESH)
    def near(b): return pltpu.make_async_copy(summed.at[b],output.at[b],x_r.at[b])
    out_t[...]=dot_nt(ofull[...],spread(cols//HD*64,cols,False)).astype(bf)
    def attn_part(b,_):
        part[b]=dot_nt(mixed[rows_of(b),:],out_t[...]).astype(bf)
        ca(b).start()
        return 0
    lax.fori_loop(0,nb,attn_part,0)
    @pl.when(own)
    def _():
        grad_far.start()
        grad_near.start()
    for x in loads: x.wait()
    def forward(b,_):
        rows=rows_of(b)
        ca(b).wait_recv()
        r=tok[rows,:].astype(f32)+(part[b].astype(f32)+oa[b].astype(f32))
        nrm,inv=norm_of(r)
        normed[rows,:]=nrm
        inv1[rows,:]=inv
        hb=(nrm*ga[...]).astype(bf)
        hb_t[:,rows]=hb.T
        gate=dot(hb,wg[...]); up=dot(hb,wu[...])
        sg=jax.nn.sigmoid(gate)
        gs=gate*sg
        a=(gs*up).astype(bf)
        act[rows,:]=a
        t2[rows,:]=gs.astype(bf)
        t1[rows,:]=(up*sg*(1.0+gate*(1.0-sg))).astype(bf)
        ca(b).wait_send()
        part[b]=dot_nt(a,wd[...]).astype(bf)
        cf(b).start()
        return 0
    lax.fori_loop(0,nb,forward,0)
    @pl.when(own)
    def _():
        grad_near.wait()
        grad_far.wait_send()
    @pl.when(jnp.logical_not(own))
    def _():
        grad_far.wait_recv()
    gsum[...]=jnp.zeros_like(gsum)
    def fold(v): return jnp.sum(v.reshape(QB//8,8,v.shape[-1]),0)
    def norm_two(b,_):
        rows=rows_of(b)
        cf(b).wait_recv()
        nrm,inv=norm_of(normed[rows,:]*ga[...]+(part[b].astype(f32)+of[b].astype(f32)))
        g=summed[b].astype(f32)
        summed[b]=(nrm*gb[...]).astype(bf)
        @pl.when(own)
        def _():
            near(b).start()
        @pl.when(jnp.logical_not(own))
        def _():
            far(b).start()
        gsum[8:16,:]+=fold(g*nrm)
        d2=norm_back(g*gb[...],nrm,inv)
        d_one[rows,:]=d2
        df=d2.astype(bf)
        oa[b]=df
        dff_t[:,rows]=df.T
        return 0
    lax.fori_loop(0,nb,norm_two,0)
    width=hb_t.shape[0]; quarter=width//4; ff=act.shape[1]
    def rows4(i): return pl.ds(pl.multiple_of(i*quarter,quarter),quarter)
    def down_grad(i,_):
        gd[i]=dot(dff_t[rows4(i),:],act[...]).astype(bf).reshape(2,2,quarter//4,ff)
        return 0
    lax.fori_loop(0,4,down_grad,0)
    h2=ff//2
    ch2=[First(gd.at[:,:,:,:,0:h2],one0,s0),First(gd.at[:,:,:,:,h2:ff],one1,s1)]
    for x in ch2: x.start()
    def backward(b,_):
        rows=rows_of(b)
        da=dot(oa[b],wd[...])
        dg=(da*t1[rows,:].astype(f32)).astype(bf); du=(da*t2[rows,:].astype(f32)).astype(bf)
        t1[rows,:]=dg; t2[rows,:]=du
        cf(b).wait_send()
        part[b]=(dot_nt(dg,wg[...])+dot_nt(du,wu[...])).astype(bf)
        ch(b).start()
        return 0
    lax.fori_loop(0,nb,backward,0)
    def grads(i,_):
        gg[i]=dot(hb_t[rows4(i),:],t1[...]).astype(bf).reshape(2,2,quarter//4,ff)
        gu[i]=dot(hb_t[rows4(i),:],t2[...]).astype(bf).reshape(2,2,quarter//4,ff)
        return 0
    lax.fori_loop(0,4,grads,0)
    keep=[pltpu.make_async_copy(a,b,keep_s.at[i]) for i,(a,b) in enumerate(((gg,gg_o),(gu,gu_o)))]
    for x in keep: x.start()
    def keep_d(b): return pltpu.make_async_copy(d_one.at[rows_of(b)],d_one_o.at[rows_of(b)],d_s.at[b])
    def last(b,_):
        rows=rows_of(b)
        ch(b).wait_recv()
        dh=d_one[rows,:]+(part[b].astype(f32)+oh[b].astype(f32))
        nrm=normed[rows,:]
        gsum[0:8,:]+=fold(dh*nrm)
        d1=norm_back(dh*ga[...],nrm,inv1[rows,:])
        d_one[rows,:]=d1
        keep_d(b).start()
        da=d1.astype(bf)
        hb_t[:,rows]=da.T
        back=dot(da,out_t[...]).astype(bf)
        for p in range(dm.shape[0]): dm[p,rows,:]=back[:,p*128:p*128+128]
        return 0
    lax.fori_loop(0,nb,last,0)
    put=spread(cols//HD*64,cols,False)
    def out_grads(i,_):
        gow[i,:,:,:,128:128+cols]=dot_nt_t(hb_t[rows4(i),:],mixed[...],put).reshape(2,2,quarter//4,cols)
        return 0
    lax.fori_loop(0,4,out_grads,0)
    line=lax.broadcasted_iota(jnp.int32,(128,width),0)
    both_gains=jnp.where(line==0,jnp.sum(gsum[0:8,:],0,keepdims=True),jnp.where(line==1,jnp.sum(gsum[8:16,:],0,keepdims=True),0.0))
    gow[:,:,:,:,0:128]=both_gains.T.astype(bf).reshape(4,2,2,quarter//4,128)
    for x in ch2: x.finish()
    for x in ch2: x.drain()
    for x in keep: x.wait()
    def drain(b,_):
        ch(b).wait_send()
        keep_d(b).wait()
        @pl.when(own)
        def _():
            near(b).wait()
        @pl.when(jnp.logical_not(own))
        def _():
            far(b).wait_recv()
            far(b).wait_send()
        return 0
    lax.fori_loop(0,nb,drain,0)

def ffn_call(tok,og,mixed,ofull,wg,wu,wd,ga,gb,cols):
    n,width=tok.shape; ff=wg.shape[1]; hp=mixed.shape[1]; nb=n//QB
    V=pl.BlockSpec(memory_space=pltpu.VMEM); A=pl.BlockSpec(memory_space=pl.ANY)
    S=jax.ShapeDtypeStruct
    blocks=(nb,QB,width); r=width//16
    dma=pltpu.SemaphoreType.DMA((nb,))
    vm=pltpu.VMEM
    return pl.pallas_call(functools.partial(ffn_kernel,n,cols),
      out_shape=[S(blocks,bf)]+[S((4,2,2,r,ff),bf)]*2+[S((n,width),f32),S((hp//128,n,128),bf),S((4,2,2,r,cols+128),bf)]+[S((4,2,r,ff//2),bf)]*2,
      in_specs=[A,A,V,V,A,A,A,V,V],out_specs=[A,A,A,A]+[V]*4,
      scratch_shapes=[vm((width,hp),bf),vm((n,ff),bf),vm((n,ff),bf),vm((n,ff),bf),vm((n,width),f32),vm((n,1),f32),vm((width,n),bf),vm((width,n),bf),
        vm(blocks,bf),vm(blocks,bf),vm(blocks,bf),vm(blocks,bf),vm(blocks,bf),vm((16,width),f32),vm((4,2,2,r,ff),bf),
        pltpu.SemaphoreType.DMA,pltpu.SemaphoreType.DMA]+[dma]*8+[pltpu.SemaphoreType.DMA((2,))]*2+[vm((n,width),bf),vm((width,ff),bf),vm((width,ff),bf),vm((width,ff),bf),vm((4,2,2,r,ff),bf),vm((4,2,2,r,ff),bf),vm((n,width),f32),pltpu.SemaphoreType.DMA((4,)),pltpu.SemaphoreType.DMA((2,)),dma],
      compiler_params=pltpu.CompilerParams(vmem_limit_bytes=64<<20,collective_id=3,has_side_effects=True),name="ffn")(
        tok,og.reshape(blocks),mixed,ofull,wg,wu,wd,ga,gb)

def rms_forward(resid):
    inverse=lax.rsqrt(jnp.mean(resid*resid,-1,keepdims=True)+NORM_EPS)
    return (resid*inverse,inverse)

def rms_backward(grad_normed,normed,inverse):
    return inverse*(grad_normed-normed*jnp.mean(grad_normed*normed,-1,keepdims=True))

def doc_starts(lengths,n):
    at=jnp.arange(n,dtype=jnp.int32); start=jnp.zeros((n,),jnp.int32); end=jnp.int32(0)
    for i in range(lengths.shape[0]-1):
        end=end+lengths[i]
        start=jnp.where(at>=end,end,start)
    return start

def rope_tables(positions):
    lane=jnp.arange(128,dtype=jnp.int32)%64
    fr=jnp.where(lane<HD,jnp.exp((lane%(HD//2)).astype(f32)*(-2.0*math.log(10000.0)/HD)),0.0)
    a=positions.astype(f32)[:,None]*fr[None,:]
    return jnp.cos(a),jnp.sin(a)

def core_sum(part):
    return part.astype(f32)+lax.ppermute(part,"c",CORE).astype(f32)

def on_device(tokens,out_grad,doc_lengths,w_query,w_key,w_value,w_out,gain_one,w_gate,w_up,w_down,gain_two):
    cols=w_query.shape[1]; n,width=tokens.shape
    if lax.axis_size("q")==8 and lax.axis_size("m")==2 and w_query.shape[0]==48:
        tokens,cos,sin,q,k,v,tok_t,wt,start,gain_a,gain_b,ofull,gate_w,up_w,down_t,m_t,mixed,lse=fused_fwd(
            doc_lengths,tokens,w_query,w_key,w_value,w_out.T,w_gate,w_up,w_down.T,gain_one,gain_two)
        ofull,gate_w,up_w,down_t=[a.reshape(width,a.shape[-1]) for a in (ofull,gate_w,up_w,down_t)]
        output,gg,gu,d_one,dm,gow,*downs=ffn_call(tokens,out_grad,mixed,ofull,gate_w,up_w,down_t,gain_a,gain_b,cols)
        grads,gtok=fused_bwd(q,k,v,m_t,dm,lse,start,cos,sin,gg,gu,gow,*downs,tok_t,wt,d_one,cols)
        gtok,sgate,sup,sdown,sq,sk,sv,sout,sgain=finish(gtok,grads,cols,w_gate.shape[1])
        return (output.reshape(n,width),gtok.reshape(n,width),sq,sk,sv,sout.T,sgain[0],sgate,sup,sdown.T,sgain[1])
    own=lax.axis_index("c")==lax.axis_index("m")
    pick=lambda a: jnp.where(own,a,lax.ppermute(a,"c",CORE))
    tokens,out_grad,doc_lengths=pick(tokens),pick(out_grad),pick(doc_lengths)
    start=doc_starts(doc_lengths[0],n)
    cos,sin=rope_tables(jnp.arange(n,dtype=jnp.int32)-start)
    start=start[None]
    ff=w_gate.shape[1]
    cast=lambda a: a.astype(bf)
    gains=jnp.pad(jnp.stack([cast(gain_one),cast(gain_two)],1),((0,0),(0,126)))
    apack=jnp.concatenate([cast(w_query),cast(w_key),cast(w_value),gains],1)
    def gather(a):
        return lax.all_gather(lax.ppermute(a,("c","m"),DIAG),("q","m"),axis=0,tiled=True)
    afull,ofull,gate_w,up_w,down_t=[gather(a) for a in (apack,cast(w_out).T,cast(w_gate),cast(w_up),cast(w_down).T)]
    q,k,v,m_t,mixed,lse=attn_fwd(tokens,afull[:,:3*cols],cos,sin,start)
    put=spread(cols//HD*64,cols,False)
    out_t=dot_nt(ofull,put).astype(bf)
    gain_a=afull[:,3*cols].astype(f32); gain_b=afull[:,3*cols+1].astype(f32)
    attn=core_sum(dot_nt(mixed,out_t).astype(bf))
    normed_one,inv_one=rms_forward(tokens.astype(f32)+attn)
    hidden=normed_one*gain_a
    hb=hidden.astype(bf)
    gate=dot(hb,gate_w); up=dot(hb,up_w)
    sg=jax.nn.sigmoid(gate)
    act=(gate*sg*up).astype(bf)
    ffn=core_sum(dot_nt(act,down_t).astype(bf))
    normed_two,inv_two=rms_forward(hidden+ffn)
    output=(normed_two*gain_b).astype(bf)
    g=out_grad.astype(f32)
    g_gain_two=jnp.sum(g*normed_two,0)
    d_two=rms_backward(g*gain_b,normed_two,inv_two)
    d_ffn=d_two.astype(bf)
    tn=lambda a,b: lax.dot_general(a,b,(((0,),(0,)),((),())),preferred_element_type=f32)
    d_act=dot(d_ffn,down_t)
    d_up=(d_act*gate*sg).astype(bf)
    d_gate=(d_act*up*sg*(1.0+gate*(1.0-sg))).astype(bf)
    hterm=(dot_nt(d_gate,gate_w)+dot_nt(d_up,up_w)).astype(bf)
    gff=[tn(hb,d_gate).astype(bf),tn(hb,d_up).astype(bf),tn(d_ffn,act).astype(bf)]
    d_hidden=d_two+core_sum(hterm)
    g_gain_one=jnp.sum(d_hidden*normed_one,0)
    d_one=rms_backward(d_hidden*gain_a,normed_one,inv_one)
    d_attn=d_one.astype(bf)
    dm=dot(d_attn,out_t).astype(bf)
    output=jnp.where(own,output,lax.ppermute(output,("c","m"),[(1,2),(2,1)]))

    ggain=jnp.pad(jnp.stack([g_gain_one,g_gain_two],1),((0,0),(0,126))).astype(bf)
    dqkv=attn_bwd(q,k,v,m_t,dm,lse,start,cos,sin)
    term=0.0; gqkv=[]
    for j in range(3):
        wp=dot_nt(afull[:,j*cols:(j+1)*cols],put).astype(bf)
        term=term+dot_nt(dqkv[j],wp)
        gqkv.append(dot(tn(tokens,dqkv[j]).astype(bf),put).astype(bf))
    gtok=(d_one+core_sum(term.astype(bf))).astype(bf)
    gtok=lax.ppermute(gtok,("c","m"),DIAG).astype(f32)
    g_out=dot(tn(d_attn,mixed).astype(bf),put).astype(bf)
    gatt=jnp.concatenate([ggain,g_out]+gqkv,1)
    add=lambda a: lax.psum_scatter(a,("q","m"),scatter_dimension=0,tiled=True)
    sff,sat=[add(a) for a in gff],add(gatt)
    sff,sat=lax.ppermute(jnp.concatenate(sff,1),("c","m"),DIAG).astype(f32),lax.ppermute(sat,("c","m"),DIAG).astype(f32)
    piece=lambda j: sat[:,128+j*cols:128+(j+1)*cols]
    return (output,gtok,piece(1),piece(2),piece(3),piece(0).T,sat[:,0],sff[:,:ff],sff[:,ff:2*ff],sff[:,2*ff:].T,sat[:,1])

def finish_kernel(cols,ff,gtok,grads,gtok_o,g_o,u_o,d_o,q_o,k_o,v_o,w_o,gain_o):
    gtok_o[...]=gtok[...].astype(f32)
    @pl.when(pl.program_id(0)==0)
    def _():
        at=0
        for ref,wide in ((g_o,ff),(u_o,ff),(d_o,ff),(q_o,cols),(k_o,cols),(v_o,cols)):
            ref[...]=grads[:,at:at+wide].astype(f32)
            at+=wide
        gain_o[...]=grads[:,at:at+128].astype(f32).T[0:8,:]
        w_o[...]=grads[:,at+128:].astype(f32)

def finish(gtok,grads,cols,ff):
    nb,rows,width=gtok.shape; r=grads.shape[0]
    S=jax.ShapeDtypeStruct
    block=pl.BlockSpec((1,rows,width),lambda i:(i,0,0))
    whole=lambda a,b: pl.BlockSpec((a,b),lambda i:(0,0))
    shapes=[(r,ff)]*3+[(r,cols)]*4+[(8,r)]
    return pl.pallas_call(functools.partial(finish_kernel,cols,ff),grid=(nb,),
      out_shape=[S(gtok.shape,f32)]+[S(a,f32) for a in shapes],
      in_specs=[block,whole(*grads.shape)],out_specs=[block]+[whole(*a) for a in shapes],
      compiler_params=pltpu.CompilerParams(vmem_limit_bytes=63<<20),name="finish")(gtok,grads)

def solution(mesh):
    dp,mp=mesh.shape["dp"],mesh.shape["mp"]
    fine=Mesh(mesh.devices.reshape(dp//2,2,mp),("q","c","m"))
    d=("q","c")
    rows,cols_=P(d,"m"),P("m",d)
    return jax.shard_map(on_device,mesh=fine,
        in_specs=(P(d,None),P(d,None),P(d,None),rows,rows,rows,cols_,P(d),rows,rows,cols_,P(d)),
        out_specs=(P(d,None),P(d,None),rows,rows,rows,cols_,P(d),rows,rows,cols_,P(d)),check_vma=False)
```

```python
import functools
import math
import jax
import jax.numpy as jnp
import numpy as np
from jax import lax
from jax.experimental import pallas as pl
from jax.experimental.pallas import tpu as pltpu
from jax.sharding import Mesh, PartitionSpec as P
MESH=pl.DeviceIdType.MESH
HD=48
C2=HD**-0.5*math.log2(math.e)
NEG=-1e30
bf=jnp.bfloat16; f32=jnp.float32
QB=256; LOOK=4
NT=(((1,),(1,)),((),()))
def dot(a,b): return jnp.dot(a,b,preferred_element_type=f32)
def dot_nt(a,b): return lax.dot_general(a,b,NT,preferred_element_type=f32)

def spread(rows, cols, rot):
    r=lax.broadcasted_iota(jnp.int32,(rows,cols),0); c=lax.broadcasted_iota(jnp.int32,(rows,cols),1)
    h=r//64; d=r-h*64
    if not rot:
        return jnp.where((d<HD)&(c==h*HD+d),1.0,0.0).astype(bf)
    lo=(d<24)&(c==h*HD+d+24); hi=(d>=24)&(d<HD)&(c==h*HD+d-24)
    return jnp.where(lo,-1.0,jnp.where(hi,1.0,0.0)).astype(bf)

def proj_weights(w,wq_s,cols):
    hp=cols//HD*64
    for m,(col,rot) in enumerate(((0,False),(0,True),(1,False),(1,True),(2,False))):
        if len(w.shape)==2:
            part=w[:,col*cols:(col+1)*cols]
        else:
            part=w[:,:,:,:,col*cols:(col+1)*cols].reshape(-1,cols)
        wq_s[m]=dot_nt(spread(hp,cols,rot),part).astype(bf)

def proj(tok,cos,sin,wq_s,q_s,k_s,v_s,lo,hi):
    def body(b,_):
        rows=pl.ds(pl.multiple_of(b*QB,QB),QB)
        x=tok[rows,:]
        cs=cos[rows,:]; sn=sin[rows,:]
        for dst,a in ((q_s,0),(k_s,2)):
            raw=dot_nt(x,wq_s[a]); rt=dot_nt(x,wq_s[a+1])
            for p in range(dst.shape[0]):
                l=slice(p*128,p*128+128)
                dst[p,rows,:]=(raw[:,l]*cs+rt[:,l]*sn).astype(bf)
        raw=dot_nt(x,wq_s[4])
        for p in range(v_s.shape[0]):
            v_s[p,rows,:]=raw[:,p*128:p*128+128].astype(bf)
        return 0
    lax.fori_loop(lo,hi,body,0)

def masks(kk0,nk,i,start):
    kidx=lax.broadcasted_iota(jnp.int32,(nk,QB),0)+kk0
    ok=kidx>=start
    qidx=lax.broadcasted_iota(jnp.int32,(nk,QB),1)+i*QB
    return ok&(kidx<=qidx)

def fwd_head(h,i,q_t,k_s,v_t,start,m_t,lse):
    p=h//2; half=h-2*p
    lo=max(0,i-LOOK)*QB; nk=(i+1)*QB-lo
    kk=slice(lo,lo+nk); qq=slice(i*QB,(i+1)*QB)
    row=lax.broadcasted_iota(jnp.int32,(128,QB),0)
    mine=(row>=half*64)&(row<half*64+64)
    qt=jnp.where(mine,q_t[p,:,qq],jnp.zeros((),bf))
    s=dot(k_s[p,kk,:],qt)
    st=start[:,qq]
    s=jnp.where(masks(lo,nk,i,st),s,NEG)
    m=jnp.max(s,0,keepdims=True)
    e=jnp.exp2((s-m)*C2)
    l=jnp.sum(e,0,keepdims=True)
    pr=(e*(1.0/l)).astype(bf)
    rows=pl.ds(pl.multiple_of(half*64,64),64)
    m_t[p,rows,qq]=dot(v_t[p,rows,kk],pr)
    lse[pl.ds(h,1),qq]=m*C2+jnp.log2(l)

def fwd_kernel(n,cols,tok,w,cos,sin,start,q_o,k_o,v_o,m_t,mixed,lse,wq_s,q_t,v_t):
    proj_weights(w,wq_s,cols)
    proj(tok,cos,sin,wq_s,q_o,k_o,v_o,0,n//QB)
    heads=cols//HD
    for p in range(heads//2):
        q_t[p]=q_o[p].T
        v_t[p]=v_o[p].T
    def body(h,_):
        for i in range(n//QB):
            fwd_head(h,i,q_t,k_o,v_t,start,m_t,lse)
        return 0
    lax.fori_loop(0,heads,body,0)
    for p in range(heads//2):
        mixed[:,p*128:p*128+128]=m_t[p].T.astype(bf)

def attn_fwd(tok,w,cos,sin,start):
    n=tok.shape[0]; cols=w.shape[1]//3; heads=cols//HD; P=heads//2
    V=pl.BlockSpec(memory_space=pltpu.VMEM)
    S=jax.ShapeDtypeStruct
    return pl.pallas_call(functools.partial(fwd_kernel,n,cols),
      out_shape=(S((P,n,128),bf),S((P,n,128),bf),S((P,n,128),bf),S((P,128,n),f32),S((n,P*128),bf),S((heads,n),f32)),
      in_specs=[V]*5,out_specs=[V]*6,
      scratch_shapes=[pltpu.VMEM((5,P*128,w.shape[0]),bf),pltpu.VMEM((P,128,n),bf),pltpu.VMEM((P,128,n),bf)],
      compiler_params=pltpu.CompilerParams(vmem_limit_bytes=60<<20),name="attn_fwd")(tok,w,cos,sin,start)

def bwd_head(h,i,q_t,q_s,k_s,k_t,v_s,dm_t,dm_s,lse,dd,start,dq_t,dk_s,dv_s):
    p=h//2; half=h-2*p
    lo=max(0,i-LOOK)*QB; nk=(i+1)*QB-lo
    kk=slice(lo,lo+nk); qq=slice(i*QB,(i+1)*QB)
    row=lax.broadcasted_iota(jnp.int32,(128,QB),0)
    mine=(row>=half*64)&(row<half*64+64)
    lane=lax.broadcasted_iota(jnp.int32,(QB,128),1)
    mlane=(lane>=half*64)&(lane<half*64+64)
    zero=jnp.zeros((),bf)
    qt=jnp.where(mine,q_t[p,:,qq],zero)
    dmt=jnp.where(mine,dm_t[p,:,qq],zero)
    qn=jnp.where(mlane,q_s[p,qq,:],zero)
    dmn=jnp.where(mlane,dm_s[p,qq,:],zero)
    s=dot(k_s[p,kk,:],qt)
    st=start[:,qq]
    pr=jnp.exp2(jnp.where(masks(lo,nk,i,st),s*C2,NEG)-lse[pl.ds(h,1),qq])
    dp=dot(v_s[p,kk,:],dmt)
    ds=(pr*(dp-dd[pl.ds(h,1),qq])).astype(bf)
    pb=pr.astype(bf)
    dv_s[p,kk,:]+=dot(pb,dmn)
    dk_s[p,kk,:]+=dot(ds,qn)
    rows=pl.ds(pl.multiple_of(half*64,64),64)
    dq_t[p,rows,qq]=dot(k_t[p,rows,kk],ds)

def rope_back(u,cs,sn):
    w=u*sn
    lane=lax.broadcasted_iota(jnp.int32,u.shape,1)&63
    up=pltpu.roll(w,128-24,axis=1); dn=pltpu.roll(w,24,axis=1)
    return u*cs+jnp.where(lane<24,up,jnp.where(lane<48,-dn,0.0))

def bwd_kernel(n,heads,q_s,k_s,v_s,m_t,dm,lse,start,cos,sin,dqkv,q_t,k_t,dm_t,dm_s,dq_t,dk_s,dv_s,dd):
    P=heads//2
    for p in range(P):
        q_t[p]=q_s[p].T
        k_t[p]=k_s[p].T
        dm_s[p]=dm[:,p*128:p*128+128]
        dm_t[p]=dm_s[p].T
        for half in range(2):
            r=slice(half*64,half*64+64)
            dd[2*p+half:2*p+half+1,:]=jnp.sum(dm_t[p,r,:].astype(f32)*m_t[p,r,:],0,keepdims=True)
    dk_s[...]=jnp.zeros_like(dk_s); dv_s[...]=jnp.zeros_like(dv_s)
    def body(h,_):
        for i in range(n//QB):
            bwd_head(h,i,q_t,q_s,k_s,k_t,v_s,dm_t,dm_s,lse,dd,start,dq_t,dk_s,dv_s)
        return 0
    lax.fori_loop(0,heads,body,0)
    sc=HD**-0.5
    for p in range(P):
        dqkv[0,:,p*128:p*128+128]=rope_back(dq_t[p].T*sc,cos[...],sin[...]).astype(bf)
        dqkv[1,:,p*128:p*128+128]=rope_back(dk_s[p]*sc,cos[...],sin[...]).astype(bf)
        dqkv[2,:,p*128:p*128+128]=dv_s[p].astype(bf)

def attn_bwd(q_s,k_s,v_s,m_t,dm,lse,start,cos,sin):
    P,n,_=q_s.shape; heads=2*P
    V=pl.BlockSpec(memory_space=pltpu.VMEM)
    S=jax.ShapeDtypeStruct
    return pl.pallas_call(functools.partial(bwd_kernel,n,heads),
      out_shape=S((3,n,P*128),bf),
      in_specs=[V]*9,out_specs=V,
      scratch_shapes=[pltpu.VMEM((P,128,n),bf),pltpu.VMEM((P,128,n),bf),pltpu.VMEM((P,128,n),bf),pltpu.VMEM((P,n,128),bf),pltpu.VMEM((P,128,n),f32),pltpu.VMEM((P,n,128),f32),pltpu.VMEM((P,n,128),f32),pltpu.VMEM((heads,n),f32)],
      compiler_params=pltpu.CompilerParams(vmem_limit_bytes=60<<20),name="attn_bwd")(q_s,k_s,v_s,m_t,dm,lse,start,cos,sin)


def place():
    q,m=lax.axis_index("q"),lax.axis_index("m")
    return q//2,lax.rem(q,2),m

def peers(z,y,m):
    return [{"q":z*2+1-y},{"m":1-m}]+[{"q":lax.rem(z+s,4)*2+y} for s in (1,2,3)]

def greet(where):
    barrier=pltpu.get_barrier_semaphore()
    for w in where:
        pl.semaphore_signal(barrier,inc=1,device_id=w,device_id_type=MESH)
    pl.semaphore_wait(barrier,len(where))

def remote(s,d,ss,rs,w):
    return pltpu.make_async_remote_copy(src_ref=s,dst_ref=d,send_sem=ss,recv_sem=rs,device_id=w,device_id_type=MESH)

class First:
    def __init__(self,source,one,sem,first="y"):
        self.source,self.one,self.first=source,one,first
        z,y,m=place()
        self.y,self.m=y,m
        ny,nx=peers(z,y,m)[:2]
        self.copy=remote(source.at[:,1-y],one,sem.at[0],sem.at[1],ny) if first=="y" else remote(source.at[:,:,1-m],one,sem.at[0],sem.at[1],nx)
    def start(self): self.copy.start()
    def finish(self):
        self.copy.wait_recv()
        def add(i,_):
            zz=i//2; o=i-zz*2
            mine=self.source[zz,self.y,o] if self.first=="y" else self.source[zz,o,self.m]
            self.one[zz,o]=(self.one[zz,o].astype(f32)+mine.astype(f32)).astype(bf)
            return 0
        lax.fori_loop(0,8,add,0)
    def drain(self): self.copy.wait_send()

class Second:
    def __init__(self,one,two,sem,first="y"):
        self.one,self.two=one,two
        z,y,m=place()
        ny,nx=peers(z,y,m)[:2]
        self.keep=m if first=="y" else y
        self.copy=remote(one.at[:,1-self.keep],two,sem.at[0],sem.at[1],nx if first=="y" else ny)
    def start(self): self.copy.start()
    def finish(self):
        self.copy.wait_recv()
        def add(zz,_):
            self.two[zz]=(self.two[zz].astype(f32)+self.one[zz,self.keep].astype(f32)).astype(bf)
            return 0
        lax.fori_loop(0,4,add,0)
    def drain(self): self.copy.wait_send()

class SecondZ:
    def __init__(self,one,two,three,send,recv):
        self.one,self.two,self.three=one,two,three
        z,y,m=place()
        self.z=z
        to=peers(z,y,m)
        self.copies=[remote(one.at[lax.rem(z+s,4)],three.at[s-1],send.at[s-1],recv.at[s-1],to[1+s]) for s in (1,2,3)]
    def start(self):
        for c in self.copies: c.start()
    def finish(self):
        for c in self.copies: c.wait_recv()
        for o in range(2):
            t=self.one[self.z,o].astype(f32)
            for s in range(3): t=t+self.three[s,o].astype(f32)
            self.two[o]=t.astype(bf)
    def drain(self):
        for c in self.copies: c.wait_send()

class ThirdX:
    def __init__(self,two,other,out,sem):
        self.two,self.other,self.out=two,other,out
        z,y,m=place()
        self.m=m
        self.copy=remote(two.at[1-m],other,sem.at[0],sem.at[1],{"m":1-m})
    def start(self): self.copy.start()
    def finish(self):
        self.copy.wait_recv()
        self.out[...]=(self.two[self.m].astype(f32)+self.other[...].astype(f32)).astype(bf)
    def drain(self): self.copy.wait_send()

class Third:
    def __init__(self,two,three,out,send,recv):
        self.two,self.three,self.out=two,three,out
        z,y,m=place()
        self.z=z
        to=peers(z,y,m)
        self.copies=[remote(two.at[lax.rem(z+s,4)],three.at[s-1],send.at[s-1],recv.at[s-1],to[1+s]) for s in (1,2,3)]
    def start(self):
        for c in self.copies: c.start()
    def finish(self):
        for c in self.copies: c.wait_recv()
        t=self.two[self.z].astype(f32)
        for s in range(3): t=t+self.three[s].astype(f32)
        self.out[...]=t.astype(bf)
    def drain(self):
        for c in self.copies: c.wait_send()

class Gather:
    def __init__(self,shard,full,cols,stage,sem,sem_z,first):
        z,y,m=place(); c=lax.axis_index("c")
        to=peers(z,y,m)
        src=shard.at[:,cols]
        self.first=first
        self.own=c==m
        self.here=pltpu.make_async_copy(src,stage.at[z,y],sem.at[0])
        self.along=[remote(src,stage.at[z,y],sem_z.at[0,s-1],sem_z.at[1,s-1],to[1+s]) for s in (1,2,3)]
        a,b=(stage.at[:,y],full.at[:,y,c,:,cols]) if first=="x" else (stage,full.at[:,:,c,:,cols])
        self.near_self=pltpu.make_async_copy(a,b,sem.at[1])
        self.near=remote(a,b,sem.at[2],sem.at[3],{"c":1-c})
        self.far_same=remote(a,b,sem.at[4],sem.at[5],{"m":1-m})
        self.far_diag=remote(a,b,sem.at[4],sem.at[6],{"c":1-c,"m":1-m})
        d=full.at[:,y,:,:,cols] if first=="x" else stage.at[:,y]
        self.across=remote(d,d,sem.at[7],sem.at[8],to[0])
    def start(self):
        self.here.start()
        for c in self.along: c.start()
    def cross(self):
        @pl.when(self.own)
        def _():
            self.near_self.start()
            self.far_same.start()
        @pl.when(jnp.logical_not(self.own))
        def _():
            self.far_diag.start()
            self.near.start()
    def crossed(self):
        @pl.when(self.own)
        def _():
            self.near_self.wait()
            self.near.wait_recv()
        @pl.when(jnp.logical_not(self.own))
        def _():
            self.far_same.wait_recv()
            self.far_diag.wait_recv()
    def second(self):
        self.here.wait()
        for c in self.along: c.wait_recv()
        if self.first=="x": self.cross()
        else: self.across.start()
    def third(self):
        if self.first=="x":
            self.crossed()
            self.across.start()
        else:
            self.across.wait_recv()
            self.cross()
    def finish(self):
        if self.first=="x": self.across.wait_recv()
        else: self.crossed()
    def drain(self):
        for c in self.along: c.wait_send()
        self.across.wait_send()
        @pl.when(self.own)
        def _():
            self.far_same.wait_send()
        @pl.when(jnp.logical_not(self.own))
        def _():
            self.far_diag.wait_send()
            self.near.wait_send()

def both(c,m):
    return [{"c":1-c},{"c":1-c,"m":1-m}]

def fused_fwd_kernel(n,cols,lengths,freq,tok_i,wq_i,wk_i,wv_i,wo_i,wg_i,wu_i,wd_i,g1_i,g2_i,
        tok_o,cos_o,sin_o,q_o,k_o,v_o,tok_t_o,wt_o,start,ga,gb,wo,wg,wu,wd,m_t,mixed,lse,
        tok,cos,sin,q_s,k_s,v_s,tok_t,wa,wq_s,q_t,v_t,docs_i,docs,a_b,o_b,g_b,u_b,d_b,swap_s,swap_r,out_s,*scr):
    z,y,m=place(); c=lax.axis_index("c")
    own=c==m
    r=a_b.shape[0]; ff=g_b.shape[1]
    eye=(lax.broadcasted_iota(jnp.int32,(r,r),0)==lax.broadcasted_iota(jnp.int32,(r,r),1)).astype(bf)
    line=lax.broadcasted_iota(jnp.int32,(128,r),0)
    gains=jnp.where(line==0,g1_i[...],jnp.where(line==1,g2_i[...],0.0)).astype(bf)
    for j,w in enumerate((wq_i,wk_i,wv_i)): a_b[:,j*cols:(j+1)*cols]=w[...].astype(bf)
    a_b[:,3*cols:]=dot_nt(eye,gains).astype(bf)
    g_b[...]=wg_i[...].astype(bf)
    u_b[...]=wu_i[...].astype(bf)
    o_b[...]=wo_i[...].astype(bf)
    d_b[...]=wd_i[...].astype(bf)
    row=lax.broadcasted_iota(jnp.int32,(8,128),0)
    table=jnp.zeros((8,128),jnp.int32)
    for i in range(lengths.shape[1]): table=jnp.where(row==i,lengths[0,i],table)
    docs_i[...]=table
    greet(peers(z,y,m)+both(c,m))
    packs=[(docs_i,docs),(tok_i,tok)]
    swap_far=[remote(a,b,swap_s.at[i],swap_r.at[i],{"c":1-c}) for i,(a,b) in enumerate(packs)]
    swap_near=[pltpu.make_async_copy(a,b,swap_r.at[i]) for i,(a,b) in enumerate(packs)]
    scr=list(scr)
    def chunk(shard,full,lo,hi,first):
        stage,sem,sem_z=scr[:3]
        del scr[:3]
        return Gather(shard,full,slice(lo,hi),stage,sem,sem_z,first)
    cut=cuts(a_b.shape[1])
    a=[chunk(a_b,wa,cut[i],cut[i+1],"xy"[i%2]) for i in range(4)]
    h2=ff//2
    f=[chunk(b,w,j*h2,j*h2+h2,"xy"[j]) for b,w in ((g_b,wg),(u_b,wu),(d_b,wd)) for j in range(2)]
    f.append(chunk(o_b,wo,0,cols,"x"))
    for x in a: x.start()
    @pl.when(own)
    def _():
        for x,w in zip(swap_near,swap_far):
            x.start(); w.start()
        swap_near[0].wait()
    @pl.when(jnp.logical_not(own))
    def _():
        swap_far[0].wait_recv()
    for x in f: x.start()
    def begin(at):
        end=jnp.zeros((1,1),jnp.int32); first=jnp.zeros(at.shape,jnp.int32)
        for i in range(lengths.shape[1]-1):
            end=end+docs[i:i+1,0:1]
            first=jnp.where(at>=end,end,first)
        return first
    start[...]=begin(lax.broadcasted_iota(jnp.int32,(1,n),1))
    def tables(b,_):
        rows=pl.ds(pl.multiple_of(b*QB,QB),QB)
        at=lax.broadcasted_iota(jnp.int32,(QB,128),0)+b*QB
        angle=(at-begin(at)).astype(f32)*freq[...]
        cos[rows,:]=jnp.cos(angle)
        sin[rows,:]=jnp.sin(angle)
        return 0
    nb=n//QB
    lax.fori_loop(0,nb//2,tables,0)
    a[0].second(); a[1].second()
    lax.fori_loop(nb//2,nb,tables,0)
    a[0].third(); a[1].third()
    a[2].second(); a[3].second()
    keep=[pltpu.make_async_copy(v,h,out_s.at[i]) for i,(v,h) in enumerate(((cos,cos_o),(sin,sin_o),(tok,tok_o),(tok_t,tok_t_o),(wq_s.at[0],wt_o.at[0]),(wq_s.at[2],wt_o.at[1]),
        (wq_s.at[4],wt_o.at[2]),(q_s,q_o),(k_s,k_o),(v_s,v_o)))]
    keep[0].start(); keep[1].start()
    @pl.when(own)
    def _():
        swap_near[1].wait()
    @pl.when(jnp.logical_not(own))
    def _():
        swap_far[1].wait_recv()
    keep[2].start()
    half=tok_t.shape[0]//2
    tok_t[:half,:]=tok[:,:half].T
    a[2].third(); a[3].third()
    tok_t[half:,:]=tok[:,half:].T
    keep[3].start()
    f[0].second(); f[1].second()
    for x in a: x.finish()
    proj_weights(wa,wq_s,cols)
    for x in keep[4:7]: x.start()
    proj(tok,cos,sin,wq_s,q_s,k_s,v_s,0,nb//3)
    f[0].third(); f[1].third()
    proj(tok,cos,sin,wq_s,q_s,k_s,v_s,nb//3,nb)
    f[2].second(); f[3].second()
    for x in keep[7:]: x.start()
    rows=wa[:,:,:,:,3*cols:].reshape(-1,128).astype(f32).T
    ga[...]=rows[0:1,:]
    gb[...]=rows[1:2,:]
    heads=cols//HD
    for p in range(heads//2):
        q_t[p]=q_s[p].T
        v_t[p]=v_s[p].T
    plan={0:[(4,"second"),(5,"second"),(6,"second")],1:[(2,"third"),(3,"third")],3:[(4,"third"),(5,"third"),(6,"third")]}
    def body(h,_):
        for i in range(nb):
            fwd_head(h,i,q_t,k_s,v_t,start,m_t,lse)
        for at,todo in plan.items():
            @pl.when(h==at)
            def _():
                for k,what in todo: getattr(f[k],what)()
        return 0
    lax.fori_loop(0,heads,body,0)
    for p in range(heads//2):
        mixed[:,p*128:p*128+128]=m_t[p].T.astype(bf)
    for x in f: x.finish()
    for x in a+f: x.drain()
    for x in keep: x.wait()
    @pl.when(own)
    def _():
        for x in swap_far: x.wait_send()

def cuts(width):
    return [0,width//1280*384,width//2,width//2+width//1280*256,width]

def fused_fwd(lengths,tok,wq,wk,wv,w_out,wg,wu,wd,g1,g2):
    n,width=tok.shape; r,cols=wq.shape; heads=cols//HD; pr=heads//2; ff=wg.shape[1]; ac=3*cols+128
    V=pl.BlockSpec(memory_space=pltpu.VMEM); A=pl.BlockSpec(memory_space=pl.ANY); M=pl.BlockSpec(memory_space=pltpu.SMEM)
    S=jax.ShapeDtypeStruct
    vm=pltpu.VMEM
    dma=lambda *k: pltpu.SemaphoreType.DMA(k)
    wide=lambda k: S((4,2,2,r,k),bf)
    lane=np.arange(128)%64
    freq=np.where(lane<HD,np.exp((lane%(HD//2)).astype(np.float32)*np.float32(-2.0*math.log(10000.0)/HD)),0.0).astype(np.float32)[None]
    cut=cuts(ac)
    sizes=[cut[i+1]-cut[i] for i in range(4)]+[ff//2]*6+[cols]
    pair=(pr,n,128)
    return pl.pallas_call(functools.partial(fused_fwd_kernel,n,cols),
      out_shape=[S((n,width),bf),S((n,128),f32),S((n,128),f32),S(pair,bf),S(pair,bf),S(pair,bf),S((width,n),bf),S((3,pr*128,width),bf),
        S((1,n),jnp.int32),S((1,width),f32),S((1,width),f32),wide(cols),wide(ff),wide(ff),wide(ff),S((pr,128,n),f32),S((n,pr*128),bf),S((heads,n),f32)],
      in_specs=[M,V,A]+[V]*9,out_specs=[A]*8+[V]*10,
      scratch_shapes=[vm((n,width),bf),vm((n,128),f32),vm((n,128),f32),vm(pair,bf),vm(pair,bf),vm(pair,bf),vm((width,n),bf),vm((4,2,2,r,ac),bf),
        vm((5,pr*128,width),bf),vm((pr,128,n),bf),vm((pr,128,n),bf),vm((8,128),jnp.int32),vm((8,128),jnp.int32),
        vm((r,ac),bf),vm((r,cols),bf),vm((r,ff),bf),vm((r,ff),bf),vm((r,ff),bf),dma(2),dma(2),dma(10)]
        +sum([[vm((4,2,r,k),bf),dma(9),dma(2,3)] for k in sizes],[]),
      compiler_params=pltpu.CompilerParams(vmem_limit_bytes=60<<20,collective_id=0,has_side_effects=True),name="attn_fwd_gather")(
        lengths,jnp.asarray(freq),tok,wq,wk,wv,w_out,wg,wu,wd,g1[None],g2[None])

def fused_bwd_kernel(n,cols,lse,start,q_i,k_i,v_i,dm_i,cos_i,sin_i,d0_i,d1_i,m_i,g_i,u_i,o_i,tok_i,wt_i,d_one,grads,gtok,
        q_t,k_t,dm_t,dq_t,dk_s,dv_s,dd,dqkv,gg,gu,gow,tok_t,wt,d_buf,ga0,ga1,term,other,q_s,k_s,v_s,dm,cos,sin,d0,d1,load_s,d_sem,core_s,core_r,far_s,far_r,fin_s,fin_r,*scr):
    z,y,m=place(); c=lax.axis_index("c")
    own=c==m
    diag={"c":1-c,"m":1-m}
    loads=[pltpu.make_async_copy(a,b,load_s.at[i]) for i,(a,b) in enumerate(((m_i,dq_t),(g_i,gg),(u_i,gu),(o_i,gow),(tok_i,tok_t),(wt_i,wt),(d0_i,d0),(d1_i,d1),(q_i,q_s),(k_i,k_s),(dm_i,dm),(v_i,v_s),(cos_i,cos),(sin_i,sin)))]
    for i in (6,7,1,8,9,10,2,3,0,11,12,13,4,5): loads[i].start()
    greet(peers(z,y,m)+both(c,m))
    scr=list(scr)
    def take(k):
        got=scr[:k]
        del scr[:k]
        return got
    half=gg.shape[-1]//2
    ff=2*half
    fd,fg,fu,fo,fh0,fh1,fq=take(7)
    outs={"d0":fd.at[:,0:half],"d1":fd.at[:,half:ff],"g0":fg.at[:,0:half],"g1":fg.at[:,half:ff],"u0":fu.at[:,0:half],"u1":fu.at[:,half:ff],
        "o":fo,"h0":fh0,"h1a":fh1.at[:,0:256],"h1b":fh1.at[:,256:ga1.shape[-1]]}
    firsts,seconds,thirds={},{},{}
    ones={"d0":d0,"d1":d1}
    for name,src,first in (("g0",gg.at[:,:,:,:,0:half],"y"),("g1",gg.at[:,:,:,:,half:ff],"x"),("u0",gu.at[:,:,:,:,0:half],"y"),("u1",gu.at[:,:,:,:,half:ff],"x"),
            ("o",gow,"y"),("h0",ga0,"y"),("h1a",ga1.at[:,:,:,:,0:256],"y"),("h1b",ga1.at[:,:,:,:,256:ga1.shape[-1]],"y")):
        ones[name],sem=take(2)
        firsts[name]=First(src,ones[name],sem,first)
    for name in ("h1a","h1b"):
        two,three,ss,rs,came,sem=take(6)
        seconds[name]=SecondZ(ones[name],two,three,ss,rs)
        thirds[name]=ThirdX(two,came,outs[name],sem)
    for name in ("d0","d1","g0","g1","u0","u1","o","h0"):
        two,sem,three,ss,rs=take(5)
        seconds[name]=Second(ones[name],two,sem,"x" if name in ("g1","u1") else "y")
        thirds[name]=Third(two,three,outs[name],ss,rs)
    pairs={}
    at=0
    for name,ref in (("g",fg),("u",fu),("d",fd),("q",fq),("o",fo)):
        pairs[name]=(ref,grads.at[:,at:at+ref.shape[-1]])
        at+=ref.shape[-1]
    finals={k:remote(a,b,fin_s.at[i],fin_r.at[i],diag) for i,(k,(a,b)) in enumerate(pairs.items())}
    def give(*names):
        @pl.when(own)
        def _():
            for k in names: pairs[k][1][...]=pairs[k][0][...]
        @pl.when(jnp.logical_not(own))
        def _():
            for k in names: finals[k].start()
    def run(*steps):
        for group,what,names in steps:
            for k in names.split(): getattr(group[k],what)()
    loads[6].wait(); loads[7].wait()
    run((seconds,"start","d0 d1"))
    loads[1].wait()
    run((firsts,"start","g0 g1"))
    for i in (8,9,10): loads[i].wait()
    heads=cols//HD; P_=heads//2
    for p in range(P_):
        q_t[p]=q_s[p].T
        k_t[p]=k_s[p].T
        dm_t[p]=dm[p].T
    loads[2].wait(); loads[3].wait()
    run((firsts,"start","u0 o"))
    loads[0].wait()
    for p in range(P_):
        for half_ in range(2):
            r=slice(half_*64,half_*64+64)
            dd[2*p+half_:2*p+half_+1,:]=jnp.sum(dm_t[p,r,:].astype(f32)*dq_t[p,r,:],0,keepdims=True)
    dk_s[...]=jnp.zeros_like(dk_s); dv_s[...]=jnp.zeros_like(dv_s)
    for i in (4,5,11,12,13): loads[i].wait()
    sc=HD**-0.5
    width=tok_t.shape[0]; quarter=width//4; hp=P_*128; part=hp//2
    def raw_grads(half_):
        for p in range(half_*P_//2,(half_+1)*P_//2):
            dqkv[0,:,p*128:p*128+128]=rope_back(dq_t[p].T*sc,cos[...],sin[...]).astype(bf)
            dqkv[1,:,p*128:p*128+128]=rope_back(dk_s[p]*sc,cos[...],sin[...]).astype(bf)
            dqkv[2,:,p*128:p*128+128]=dv_s[p].astype(bf)
    def weight_grads(half_):
        ga=(ga0,ga1)[half_]
        w=ga.shape[-1]; hc=cols//2
        maps=[]
        for j in range(3):
            rr=lax.broadcasted_iota(jnp.int32,(part,w),0); cc=lax.broadcasted_iota(jnp.int32,(part,w),1)
            hh=rr//64; dd_=rr-hh*64
            maps.append(jnp.where((dd_<HD)&(cc==j*hc+hh*HD+dd_),1.0,0.0).astype(bf))
        def body(i,_):
            r=pl.ds(pl.multiple_of(i*quarter,quarter),quarter)
            t=0.0
            for j in range(3):
                t=t+dot(dot(tok_t[r,:],dqkv[j,:,half_*part:(half_+1)*part]).astype(bf),maps[j])
            ga[i]=t.astype(bf).reshape(2,2,quarter//4,w)
            return 0
        lax.fori_loop(0,4,body,0)
    def middle():
        raw_grads(0)
        weight_grads(0)
    events={0:[lambda: run((seconds,"finish","d0 d1"),(thirds,"start","d0 d1"),(firsts,"finish","g0"),(seconds,"start","g0"),(firsts,"start","u1"))],
        2:[lambda: run((firsts,"finish","u0 g1"),(seconds,"start","u0 g1"))],
        3:[lambda: run((thirds,"finish","d0 d1")),lambda: give("d"),lambda: run((seconds,"finish","g0"),(thirds,"start","g0")),middle,lambda: run((firsts,"start","h0"))],
        4:[lambda: run((seconds,"finish","g1"),(thirds,"start","g1"),(firsts,"finish","o"),(seconds,"start","o"))],
        5:[lambda: run((firsts,"finish","u1"),(seconds,"start","u1"),(thirds,"finish","g0 g1")),lambda: give("g")],
        6:[lambda: run((seconds,"finish","u0"),(thirds,"start","u0"))],
        7:[lambda: run((firsts,"finish","h0"),(seconds,"start","h0"),(seconds,"finish","o"),(thirds,"start","o"))]}
    def body(h,_):
        for i in range(n//QB):
            bwd_head(h,i,q_t,q_s,k_s,k_t,v_s,dm_t,dm,lse,dd,start,dq_t,dk_s,dv_s)
        for at,calls in events.items():
            @pl.when(h==at)
            def _():
                for call in calls: call()
        return 0
    lax.fori_loop(0,heads,body,0)
    raw_grads(1)
    nb=n//QB
    def cross(b): return remote(term.at[b],other.at[b],core_s.at[b],core_r.at[b],{"c":1-c})
    def far(b): return remote(term.at[b],gtok.at[b],far_s.at[b],far_r.at[b],diag)
    def near(b): return pltpu.make_async_copy(term.at[b],gtok.at[b],far_r.at[b])
    def fetch(b): return pltpu.make_async_copy(d_one.at[b],d_buf.at[lax.rem(b,2)],d_sem.at[lax.rem(b,2)])
    fetch(0).start(); fetch(1).start()
    def make(b,_):
        rows=pl.ds(pl.multiple_of(b*QB,QB),QB)
        t=dot(dqkv[0,rows,:],wt[0])+dot(dqkv[1,rows,:],wt[1])+dot(dqkv[2,rows,:],wt[2])
        term[b]=t.astype(bf)
        cross(b).start()
        return 0
    lax.fori_loop(0,nb,make,0)
    def total(b,_):
        cross(b).wait_recv()
        cross(b).wait_send()
        fetch(b).wait()
        term[b]=(d_buf[lax.rem(b,2)]+(term[b].astype(f32)+other[b].astype(f32))).astype(bf)
        @pl.when(b+2<nb)
        def _():
            fetch(b+2).start()
        @pl.when(own)
        def _():
            near(b).start()
        @pl.when(jnp.logical_not(own))
        def _():
            far(b).start()
        return 0
    lax.fori_loop(0,2,total,0)
    weight_grads(1)
    run((firsts,"start","h1a h1b"),(seconds,"finish","h0"),(thirds,"start","h0"),(seconds,"finish","u1"),(thirds,"start","u1"))
    lax.fori_loop(2,4,total,0)
    run((thirds,"finish","u0 o"))
    give("o")
    run((firsts,"finish","h1a"),(seconds,"start","h1a"))
    lax.fori_loop(4,nb,total,0)
    run((firsts,"finish","h1b"),(seconds,"start","h1b"),(thirds,"finish","u1 h0"))
    give("u")
    hc=cols//2; hw=fh0.shape[-1]
    rr=lax.broadcasted_iota(jnp.int32,(hw,3*cols),0); cc=lax.broadcasted_iota(jnp.int32,(hw,3*cols),1)
    jj=cc//cols
    def sort(half_): return jnp.where((rr==jj*hc+cc-jj*cols-half_*hc)&(cc-jj*cols>=half_*hc)&(cc-jj*cols<(half_+1)*hc),1.0,0.0).astype(bf)
    low=dot(fh0[...],sort(0)); last_map=sort(1)
    run((seconds,"finish","h1a"),(thirds,"start","h1a"),(seconds,"finish","h1b"),(thirds,"start","h1b"),(thirds,"finish","h1a h1b"))
    fq[...]=(low+dot(fh1[...],last_map)).astype(bf)
    give("q")
    for group in (firsts,seconds,thirds):
        for x in group.values(): x.drain()
    def drain(b,_):
        @pl.when(own)
        def _():
            near(b).wait()
        @pl.when(jnp.logical_not(own))
        def _():
            far(b).wait_recv()
            far(b).wait_send()
        return 0
    lax.fori_loop(0,nb,drain,0)
    @pl.when(jnp.logical_not(own))
    def _():
        for x in finals.values():
            x.wait_recv()
            x.wait_send()

def fused_bwd(q_s,k_s,v_s,m_t,dm,lse,start,cos,sin,gg,gu,gow,d0,d1,tok_t,wt,d_one,cols):
    pr,n,_=q_s.shape; heads=2*pr; width=tok_t.shape[0]; nb=n//QB
    V=pl.BlockSpec(memory_space=pltpu.VMEM); A=pl.BlockSpec(memory_space=pl.ANY)
    S=jax.ShapeDtypeStruct
    ff=gg.shape[-1]; r=gg.shape[-2]; w=gow.shape[-1]; h=ff//2; hw=-(-3*cols//2//128)*128
    vm=pltpu.VMEM
    dma=lambda k: pltpu.SemaphoreType.DMA((k,))
    blocks=(nb,QB,width)
    like=lambda a: vm(a.shape,a.dtype)
    one=lambda k: [vm((4,2,r,k),bf),dma(2)]
    two=lambda k: [vm((4,r,k),bf),dma(2)]
    three=lambda k: [vm((3,r,k),bf),dma(3),dma(3)]
    by_z=lambda k: [vm((2,r,k),bf),vm((3,2,r,k),bf),dma(3),dma(3),vm((r,k),bf),dma(2)]
    return pl.pallas_call(functools.partial(fused_bwd_kernel,n,cols),
      out_shape=[S((r,3*ff+3*cols+w),bf),S(blocks,bf)],
      in_specs=[V,V]+[A]*15,out_specs=[V,A],
      scratch_shapes=[vm((pr,128,n),bf)]*3+[vm((pr,128,n),f32),vm((pr,n,128),f32),vm((pr,n,128),f32),vm((heads,n),f32),vm((3,n,pr*128),bf),
        like(gg),like(gu),like(gow),like(tok_t),like(wt),vm((2,QB,width),f32),vm((4,2,2,r,hw),bf),vm((4,2,2,r,hw),bf)]+[vm(blocks,bf)]*2
        +[like(a) for a in (q_s,k_s,v_s,dm,cos,sin,d0,d1)]+[dma(14),dma(2)]+[dma(nb)]*4+[dma(5),dma(5)]
        +[vm((r,ff),bf)]*3+[vm((r,w),bf)]+[vm((r,hw),bf)]*2+[vm((r,3*cols),bf)]
        +one(h)*4+one(w)+one(hw)+one(256)+one(hw-256)+by_z(256)+by_z(hw-256)+(two(h)+three(h))*6+two(w)+three(w)+two(hw)+three(hw),
      compiler_params=pltpu.CompilerParams(vmem_limit_bytes=64<<20,collective_id=1,has_side_effects=True),name="attn_bwd_reduce")(
        lse,start,q_s,k_s,v_s,dm,cos,sin,d0,d1,m_t,gg,gu,gow,tok_t,wt,d_one.reshape(blocks))

def dot_nt_t(a,b,put):
    return dot(dot(a,b).astype(bf),put).astype(bf)

NORM_EPS=1e-05
DIAG=[(0,0),(3,3),(1,2),(2,1)]
CORE=[(0,1),(1,0)]

def cross_copies(n,part,other,send,recv,c):
    def one(b): return pltpu.make_async_remote_copy(src_ref=part.at[b],dst_ref=other.at[b],send_sem=send.at[b],recv_sem=recv.at[b],device_id={"c":1-c},device_id_type=MESH)
    return one

def norm_of(r):
    inv=lax.rsqrt(jnp.mean(r*r,-1,keepdims=True)+NORM_EPS)
    return r*inv,inv

def norm_back(e,nrm,inv):
    return inv*(e-nrm*jnp.mean(e*nrm,-1,keepdims=True))

def ffn_kernel(n,cols,tok_i,og,mixed,ofull,wg_i,wu_i,wd_i,ga,gb,output,gg_o,gu_o,d_one_o,dm,gow,one0,one1,
        out_t,t1,t2,act,normed,inv1,hb_t,dff_t,part,oa,of,oh,summed,gsum,gd,og_s,og_r,a_s,a_r,f_s,f_r,h_s,h_r,x_s,x_r,s0,s1,tok,wg,wu,wd,gg,gu,d_one,load_s,keep_s,d_s):
    z,y,m=place(); c=lax.axis_index("c")
    own=c==m
    loads=[pltpu.make_async_copy(a,b,load_s.at[i]) for i,(a,b) in enumerate(((tok_i,tok),(wg_i,wg),(wu_i,wu),(wd_i,wd)))]
    for x in loads: x.start()
    greet(peers(z,y,m)+both(c,m))
    nb=n//QB
    grad_far=pltpu.make_async_remote_copy(src_ref=og,dst_ref=summed,send_sem=og_s,recv_sem=og_r,device_id={"c":1-c},device_id_type=MESH)
    grad_near=pltpu.make_async_copy(og,summed,og_r)
    def rows_of(b): return pl.ds(pl.multiple_of(b*QB,QB),QB)
    ca,cf,ch=[cross_copies(n,part,o,ss,rs,c) for o,ss,rs in ((oa,a_s,a_r),(of,f_s,f_r),(oh,h_s,h_r))]
    def far(b): return pltpu.make_async_remote_copy(src_ref=summed.at[b],dst_ref=output.at[b],send_sem=x_s.at[b],recv_sem=x_r.at[b],device_id={"c":1-c,"m":1-m},device_id_type=MESH)
    def near(b): return pltpu.make_async_copy(summed.at[b],output.at[b],x_r.at[b])
    out_t[...]=dot_nt(ofull[...],spread(cols//HD*64,cols,False)).astype(bf)
    def attn_part(b,_):
        part[b]=dot_nt(mixed[rows_of(b),:],out_t[...]).astype(bf)
        ca(b).start()
        return 0
    lax.fori_loop(0,nb,attn_part,0)
    @pl.when(own)
    def _():
        grad_far.start()
        grad_near.start()
    for x in loads: x.wait()
    def forward(b,_):
        rows=rows_of(b)
        ca(b).wait_recv()
        r=tok[rows,:].astype(f32)+(part[b].astype(f32)+oa[b].astype(f32))
        nrm,inv=norm_of(r)
        normed[rows,:]=nrm
        inv1[rows,:]=inv
        hb=(nrm*ga[...]).astype(bf)
        hb_t[:,rows]=hb.T
        gate=dot(hb,wg[...]); up=dot(hb,wu[...])
        sg=jax.nn.sigmoid(gate)
        gs=gate*sg
        a=(gs*up).astype(bf)
        act[rows,:]=a
        t2[rows,:]=gs.astype(bf)
        t1[rows,:]=(up*sg*(1.0+gate*(1.0-sg))).astype(bf)
        ca(b).wait_send()
        part[b]=dot_nt(a,wd[...]).astype(bf)
        cf(b).start()
        return 0
    lax.fori_loop(0,nb,forward,0)
    @pl.when(own)
    def _():
        grad_near.wait()
        grad_far.wait_send()
    @pl.when(jnp.logical_not(own))
    def _():
        grad_far.wait_recv()
    gsum[...]=jnp.zeros_like(gsum)
    def fold(v): return jnp.sum(v.reshape(QB//8,8,v.shape[-1]),0)
    def norm_two(b,_):
        rows=rows_of(b)
        cf(b).wait_recv()
        nrm,inv=norm_of(normed[rows,:]*ga[...]+(part[b].astype(f32)+of[b].astype(f32)))
        g=summed[b].astype(f32)
        summed[b]=(nrm*gb[...]).astype(bf)
        @pl.when(own)
        def _():
            near(b).start()
        @pl.when(jnp.logical_not(own))
        def _():
            far(b).start()
        gsum[8:16,:]+=fold(g*nrm)
        d2=norm_back(g*gb[...],nrm,inv)
        d_one[rows,:]=d2
        df=d2.astype(bf)
        oa[b]=df
        dff_t[:,rows]=df.T
        return 0
    lax.fori_loop(0,nb,norm_two,0)
    width=hb_t.shape[0]; quarter=width//4; ff=act.shape[1]
    def rows4(i): return pl.ds(pl.multiple_of(i*quarter,quarter),quarter)
    def down_grad(i,_):
        gd[i]=dot(dff_t[rows4(i),:],act[...]).astype(bf).reshape(2,2,quarter//4,ff)
        return 0
    lax.fori_loop(0,4,down_grad,0)
    h2=ff//2
    ch2=[First(gd.at[:,:,:,:,0:h2],one0,s0),First(gd.at[:,:,:,:,h2:ff],one1,s1)]
    for x in ch2: x.start()
    def backward(b,_):
        rows=rows_of(b)
        da=dot(oa[b],wd[...])
        dg=(da*t1[rows,:].astype(f32)).astype(bf); du=(da*t2[rows,:].astype(f32)).astype(bf)
        t1[rows,:]=dg; t2[rows,:]=du
        cf(b).wait_send()
        part[b]=(dot_nt(dg,wg[...])+dot_nt(du,wu[...])).astype(bf)
        ch(b).start()
        return 0
    lax.fori_loop(0,nb,backward,0)
    def grads(i,_):
        gg[i]=dot(hb_t[rows4(i),:],t1[...]).astype(bf).reshape(2,2,quarter//4,ff)
        gu[i]=dot(hb_t[rows4(i),:],t2[...]).astype(bf).reshape(2,2,quarter//4,ff)
        return 0
    lax.fori_loop(0,4,grads,0)
    keep=[pltpu.make_async_copy(a,b,keep_s.at[i]) for i,(a,b) in enumerate(((gg,gg_o),(gu,gu_o)))]
    for x in keep: x.start()
    def keep_d(b): return pltpu.make_async_copy(d_one.at[rows_of(b)],d_one_o.at[rows_of(b)],d_s.at[b])
    def last(b,_):
        rows=rows_of(b)
        ch(b).wait_recv()
        dh=d_one[rows,:]+(part[b].astype(f32)+oh[b].astype(f32))
        nrm=normed[rows,:]
        gsum[0:8,:]+=fold(dh*nrm)
        d1=norm_back(dh*ga[...],nrm,inv1[rows,:])
        d_one[rows,:]=d1
        keep_d(b).start()
        da=d1.astype(bf)
        hb_t[:,rows]=da.T
        back=dot(da,out_t[...]).astype(bf)
        for p in range(dm.shape[0]): dm[p,rows,:]=back[:,p*128:p*128+128]
        return 0
    lax.fori_loop(0,nb,last,0)
    put=spread(cols//HD*64,cols,False)
    def out_grads(i,_):
        gow[i,:,:,:,128:128+cols]=dot_nt_t(hb_t[rows4(i),:],mixed[...],put).reshape(2,2,quarter//4,cols)
        return 0
    lax.fori_loop(0,4,out_grads,0)
    line=lax.broadcasted_iota(jnp.int32,(128,width),0)
    both_gains=jnp.where(line==0,jnp.sum(gsum[0:8,:],0,keepdims=True),jnp.where(line==1,jnp.sum(gsum[8:16,:],0,keepdims=True),0.0))
    gow[:,:,:,:,0:128]=both_gains.T.astype(bf).reshape(4,2,2,quarter//4,128)
    for x in ch2: x.finish()
    for x in ch2: x.drain()
    for x in keep: x.wait()
    def drain(b,_):
        ch(b).wait_send()
        keep_d(b).wait()
        @pl.when(own)
        def _():
            near(b).wait()
        @pl.when(jnp.logical_not(own))
        def _():
            far(b).wait_recv()
            far(b).wait_send()
        return 0
    lax.fori_loop(0,nb,drain,0)

def ffn_call(tok,og,mixed,ofull,wg,wu,wd,ga,gb,cols):
    n,width=tok.shape; ff=wg.shape[1]; hp=mixed.shape[1]; nb=n//QB
    V=pl.BlockSpec(memory_space=pltpu.VMEM); A=pl.BlockSpec(memory_space=pl.ANY)
    S=jax.ShapeDtypeStruct
    blocks=(nb,QB,width); r=width//16
    dma=pltpu.SemaphoreType.DMA((nb,))
    vm=pltpu.VMEM
    return pl.pallas_call(functools.partial(ffn_kernel,n,cols),
      out_shape=[S(blocks,bf)]+[S((4,2,2,r,ff),bf)]*2+[S((n,width),f32),S((hp//128,n,128),bf),S((4,2,2,r,cols+128),bf)]+[S((4,2,r,ff//2),bf)]*2,
      in_specs=[A,A,V,V,A,A,A,V,V],out_specs=[A,A,A,A]+[V]*4,
      scratch_shapes=[vm((width,hp),bf),vm((n,ff),bf),vm((n,ff),bf),vm((n,ff),bf),vm((n,width),f32),vm((n,1),f32),vm((width,n),bf),vm((width,n),bf),
        vm(blocks,bf),vm(blocks,bf),vm(blocks,bf),vm(blocks,bf),vm(blocks,bf),vm((16,width),f32),vm((4,2,2,r,ff),bf),
        pltpu.SemaphoreType.DMA,pltpu.SemaphoreType.DMA]+[dma]*8+[pltpu.SemaphoreType.DMA((2,))]*2+[vm((n,width),bf),vm((width,ff),bf),vm((width,ff),bf),vm((width,ff),bf),vm((4,2,2,r,ff),bf),vm((4,2,2,r,ff),bf),vm((n,width),f32),pltpu.SemaphoreType.DMA((4,)),pltpu.SemaphoreType.DMA((2,)),dma],
      compiler_params=pltpu.CompilerParams(vmem_limit_bytes=64<<20,collective_id=3,has_side_effects=True),name="ffn")(
        tok,og.reshape(blocks),mixed,ofull,wg,wu,wd,ga,gb)

def rms_forward(resid):
    inverse=lax.rsqrt(jnp.mean(resid*resid,-1,keepdims=True)+NORM_EPS)
    return (resid*inverse,inverse)

def rms_backward(grad_normed,normed,inverse):
    return inverse*(grad_normed-normed*jnp.mean(grad_normed*normed,-1,keepdims=True))

def doc_starts(lengths,n):
    at=jnp.arange(n,dtype=jnp.int32); start=jnp.zeros((n,),jnp.int32); end=jnp.int32(0)
    for i in range(lengths.shape[0]-1):
        end=end+lengths[i]
        start=jnp.where(at>=end,end,start)
    return start

def rope_tables(positions):
    lane=jnp.arange(128,dtype=jnp.int32)%64
    fr=jnp.where(lane<HD,jnp.exp((lane%(HD//2)).astype(f32)*(-2.0*math.log(10000.0)/HD)),0.0)
    a=positions.astype(f32)[:,None]*fr[None,:]
    return jnp.cos(a),jnp.sin(a)

def core_sum(part):
    return part.astype(f32)+lax.ppermute(part,"c",CORE).astype(f32)

def on_device(tokens,out_grad,doc_lengths,w_query,w_key,w_value,w_out,gain_one,w_gate,w_up,w_down,gain_two):
    cols=w_query.shape[1]; n,width=tokens.shape
    if lax.axis_size("q")==8 and lax.axis_size("m")==2 and w_query.shape[0]==48:
        tokens,cos,sin,q,k,v,tok_t,wt,start,gain_a,gain_b,ofull,gate_w,up_w,down_t,m_t,mixed,lse=fused_fwd(
            doc_lengths,tokens,w_query,w_key,w_value,w_out.T,w_gate,w_up,w_down.T,gain_one,gain_two)
        ofull,gate_w,up_w,down_t=[a.reshape(width,a.shape[-1]) for a in (ofull,gate_w,up_w,down_t)]
        output,gg,gu,d_one,dm,gow,*downs=ffn_call(tokens,out_grad,mixed,ofull,gate_w,up_w,down_t,gain_a,gain_b,cols)
        grads,gtok=fused_bwd(q,k,v,m_t,dm,lse,start,cos,sin,gg,gu,gow,*downs,tok_t,wt,d_one,cols)
        gtok,output,sgate,sup,sdown,sq,sk,sv,sout,sgain=finish(gtok,output,grads,cols,w_gate.shape[1])
        return (output.reshape(n,width),gtok.reshape(n,width),sq,sk,sv,sout.T,sgain[0],sgate,sup,sdown.T,sgain[1])
    own=lax.axis_index("c")==lax.axis_index("m")
    pick=lambda a: jnp.where(own,a,lax.ppermute(a,"c",CORE))
    tokens,out_grad,doc_lengths=pick(tokens),pick(out_grad),pick(doc_lengths)
    start=doc_starts(doc_lengths[0],n)
    cos,sin=rope_tables(jnp.arange(n,dtype=jnp.int32)-start)
    start=start[None]
    ff=w_gate.shape[1]
    cast=lambda a: a.astype(bf)
    gains=jnp.pad(jnp.stack([cast(gain_one),cast(gain_two)],1),((0,0),(0,126)))
    apack=jnp.concatenate([cast(w_query),cast(w_key),cast(w_value),gains],1)
    def gather(a):
        return lax.all_gather(lax.ppermute(a,("c","m"),DIAG),("q","m"),axis=0,tiled=True)
    afull,ofull,gate_w,up_w,down_t=[gather(a) for a in (apack,cast(w_out).T,cast(w_gate),cast(w_up),cast(w_down).T)]
    q,k,v,m_t,mixed,lse=attn_fwd(tokens,afull[:,:3*cols],cos,sin,start)
    put=spread(cols//HD*64,cols,False)
    out_t=dot_nt(ofull,put).astype(bf)
    gain_a=afull[:,3*cols].astype(f32); gain_b=afull[:,3*cols+1].astype(f32)
    attn=core_sum(dot_nt(mixed,out_t).astype(bf))
    normed_one,inv_one=rms_forward(tokens.astype(f32)+attn)
    hidden=normed_one*gain_a
    hb=hidden.astype(bf)
    gate=dot(hb,gate_w); up=dot(hb,up_w)
    sg=jax.nn.sigmoid(gate)
    act=(gate*sg*up).astype(bf)
    ffn=core_sum(dot_nt(act,down_t).astype(bf))
    normed_two,inv_two=rms_forward(hidden+ffn)
    output=(normed_two*gain_b).astype(bf)
    g=out_grad.astype(f32)
    g_gain_two=jnp.sum(g*normed_two,0)
    d_two=rms_backward(g*gain_b,normed_two,inv_two)
    d_ffn=d_two.astype(bf)
    tn=lambda a,b: lax.dot_general(a,b,(((0,),(0,)),((),())),preferred_element_type=f32)
    d_act=dot(d_ffn,down_t)
    d_up=(d_act*gate*sg).astype(bf)
    d_gate=(d_act*up*sg*(1.0+gate*(1.0-sg))).astype(bf)
    hterm=(dot_nt(d_gate,gate_w)+dot_nt(d_up,up_w)).astype(bf)
    gff=[tn(hb,d_gate).astype(bf),tn(hb,d_up).astype(bf),tn(d_ffn,act).astype(bf)]
    d_hidden=d_two+core_sum(hterm)
    g_gain_one=jnp.sum(d_hidden*normed_one,0)
    d_one=rms_backward(d_hidden*gain_a,normed_one,inv_one)
    d_attn=d_one.astype(bf)
    dm=dot(d_attn,out_t).astype(bf)
    output=jnp.where(own,output,lax.ppermute(output,("c","m"),[(1,2),(2,1)]))

    ggain=jnp.pad(jnp.stack([g_gain_one,g_gain_two],1),((0,0),(0,126))).astype(bf)
    dqkv=attn_bwd(q,k,v,m_t,dm,lse,start,cos,sin)
    term=0.0; gqkv=[]
    for j in range(3):
        wp=dot_nt(afull[:,j*cols:(j+1)*cols],put).astype(bf)
        term=term+dot_nt(dqkv[j],wp)
        gqkv.append(dot(tn(tokens,dqkv[j]).astype(bf),put).astype(bf))
    gtok=(d_one+core_sum(term.astype(bf))).astype(bf)
    gtok=lax.ppermute(gtok,("c","m"),DIAG).astype(f32)
    g_out=dot(tn(d_attn,mixed).astype(bf),put).astype(bf)
    gatt=jnp.concatenate([ggain,g_out]+gqkv,1)
    add=lambda a: lax.psum_scatter(a,("q","m"),scatter_dimension=0,tiled=True)
    sff,sat=[add(a) for a in gff],add(gatt)
    sff,sat=lax.ppermute(jnp.concatenate(sff,1),("c","m"),DIAG).astype(f32),lax.ppermute(sat,("c","m"),DIAG).astype(f32)
    piece=lambda j: sat[:,128+j*cols:128+(j+1)*cols]
    return (output,gtok,piece(1),piece(2),piece(3),piece(0).T,sat[:,0],sff[:,:ff],sff[:,ff:2*ff],sff[:,2*ff:].T,sat[:,1])

def finish_kernel(cols,ff,gtok,output,grads,gtok_o,output_o,g_o,u_o,d_o,q_o,k_o,v_o,w_o,gain_o):
    gtok_o[...]=gtok[...].astype(f32)
    output_o[...]=output[...]
    @pl.when(pl.program_id(0)==0)
    def _():
        at=0
        for ref,wide in ((g_o,ff),(u_o,ff),(d_o,ff),(q_o,cols),(k_o,cols),(v_o,cols)):
            ref[...]=grads[:,at:at+wide].astype(f32)
            at+=wide
        gain_o[...]=grads[:,at:at+128].astype(f32).T[0:8,:]
        w_o[...]=grads[:,at+128:].astype(f32)

def finish(gtok,output,grads,cols,ff):
    nb,rows,width=gtok.shape; r=grads.shape[0]
    S=jax.ShapeDtypeStruct
    block=pl.BlockSpec((1,rows,width),lambda i:(i,0,0))
    whole=lambda a,b: pl.BlockSpec((a,b),lambda i:(0,0))
    shapes=[(r,ff)]*3+[(r,cols)]*4+[(8,r)]
    return pl.pallas_call(functools.partial(finish_kernel,cols,ff),grid=(nb,),
      out_shape=[S(gtok.shape,f32),S(output.shape,bf)]+[S(a,f32) for a in shapes],
      in_specs=[block,block,whole(*grads.shape)],out_specs=[block,block]+[whole(*a) for a in shapes],
      compiler_params=pltpu.CompilerParams(vmem_limit_bytes=63<<20),name="finish")(gtok,output,grads)

def solution(mesh):
    dp,mp=mesh.shape["dp"],mesh.shape["mp"]
    fine=Mesh(mesh.devices.reshape(dp//2,2,mp),("q","c","m"))
    d=("q","c")
    rows,cols_=P(d,"m"),P("m",d)
    return jax.shard_map(on_device,mesh=fine,
        in_specs=(P(d,None),P(d,None),P(d,None),rows,rows,rows,cols_,P(d),rows,rows,cols_,P(d)),
        out_specs=(P(d,None),P(d,None),rows,rows,rows,cols_,P(d),rows,rows,cols_,P(d)),check_vma=False)
```
